32 devices in a mesh: dp: 4 (over z), fsdp: 8 (over y, x, core).
Axes of the slice: x: 2, y: 2, z: 4, core: 2. Of those that a mesh axis runs over, the one named last changes fastest.
Arguments:
- tokens: bfloat16 [32, 1024, 1024], P(('dp', 'fsdp')), may hold values from -6 to 6
- lengths: int32 [32], P(('dp', 'fsdp')), may hold values from 64 to 1024, as said below
- cotangent: bfloat16 [32, 1024, 1024], P(('dp', 'fsdp')), may hold values from -6 to 6
- gain_one: float32 [1024], replicated, may hold values from 0.5 to 1.5
- shift_one: float32 [1024], replicated, may hold values from -1 to 1
- gain_two: float32 [1024], replicated, may hold values from 0.5 to 1.5
- shift_two: float32 [1024], replicated, may hold values from -1 to 1
- w_qkv: bfloat16 [1024, 3072], P('fsdp'), may hold values from -0.25 to 0.25
- w_proj: bfloat16 [1024, 1024], P('fsdp'), may hold values from -0.75 to 0.75
- w_fc: bfloat16 [1024, 4096], P('fsdp'), may hold values from -0.1875 to 0.1875
- w_out: bfloat16 [4096, 1024], P('fsdp'), may hold values from -0.125 to 0.125
- query_down_factor: float32 [1024, 4], replicated, may hold values from -0.1875 to 0.1875
- query_up_factor: float32 [4, 1024], replicated, may hold values from -0.3 to 0.3
- value_down_factor: float32 [1024, 4], replicated, may hold values from -0.1875 to 0.1875
- value_up_factor: float32 [4, 1024], replicated, may hold values from -0.3 to 0.3
Outputs:
- block_out: bfloat16 [32, 1024, 1024], P(('dp', 'fsdp'))
- grad_tokens: bfloat16 [32, 1024, 1024], P(('dp', 'fsdp'))
- grad_a_query: float32 [1024, 4], replicated
- query_up_gradient: float32 [4, 1024], replicated
- grad_a_value: float32 [1024, 4], replicated
- value_up_gradient: float32 [4, 1024], replicated
The draws below stay inside these ranges and needn't reach their ends.
Inputs may be any that keep to these rules, and one draw needn't show every extreme that they name: `lengths`: number of real tokens of each sequence; positions from it up to 1023 are padding.
All inputs are finite; a program needn't handle non-finite values.
Results may differ from the reference program's by a relative error of at most 0.015.
The reference program's roundings to bfloat16 on the way count: a program that leaves them out, or rounds other values in their place, can miss the bound.
Values may be sent and summed in bfloat16 or wider, within the bound.
No kernel may reach another device: no remote copies, remote signals or barrier semaphores. Data moves between devices by JAX's collectives and lax.ppermute only.
A program may use at most 256 MiB of HBM per device.

```python
import math
import jax
import jax.numpy as jnp
from jax import lax

D = 1024
H = 16
HD = 64
FF = 4096
RANK = 4
LEN = 1024
MIN_LEN = 64
ROWS = 32


def draw_lengths(key, part):
    key = jax.random.fold_in(key, 11)
    key_one, key_two, key_three, key_four = jax.random.split(key, 4)
    row_count = ROWS
    first_draw = jax.random.randint(key_one, (row_count,), MIN_LEN, LEN + 1)
    second_draw = jax.random.randint(key_two, (row_count,), MIN_LEN, LEN + 1)
    drawn = jnp.maximum(first_draw, second_draw)
    longest = jax.random.randint(key_three, (), 0, row_count)
    offset = jax.random.randint(key_four, (), 1, row_count)
    shortest = (longest + offset) % row_count
    return drawn.at[longest].set(LEN).at[shortest].set(MIN_LEN).astype(jnp.int32)


def level_of(rng, dims, cuts, smallest, top_value):
    factor_of, own = 1.0, jax.random.fold_in(rng, 6)
    for axis_at, shards_of in cuts:
        heights = jnp.exp(jax.random.uniform(jax.random.fold_in(own, axis_at), (shards_of,), jnp.float32, smallest / len(cuts), top_value / len(cuts)))
        factor_of = factor_of * jnp.repeat(heights, dims[axis_at] // shards_of).reshape([-1 if axis == axis_at else 1 for axis in range(len(dims))])
    return factor_of


def normal_values(rng, shape, scale, reach, cuts=(), held_as=jnp.bfloat16):
    level = level_of(rng, shape, cuts, -0.22, 0.18) if cuts else 1.0
    array = jax.random.normal(rng, shape, jnp.float32) * scale * level
    return jnp.minimum(jnp.maximum(array, -reach), reach).astype(held_as)


def setup_inputs(seed: int = 0) -> dict:
    streams_of = jax.random.split(jax.random.key(seed), 16)
    tokens = normal_values(streams_of[0], (ROWS, LEN, D), 1.0, 6.0, ((0, 32),))
    lengths = draw_lengths(jax.random.fold_in(streams_of[15], 71), 0)
    cotangent = normal_values(streams_of[2], (ROWS, LEN, D), 1.0, 6.0, ((0, 32),))
    gain_one = jnp.clip(1.0 + 0.1 * jax.random.normal(streams_of[3], (D,), jnp.float32), 0.5, 1.5)
    shift_one = normal_values(streams_of[4], (D,), 0.2, 1.0, (), jnp.float32)
    gain_two = jnp.clip(1.0 + 0.1 * jax.random.normal(streams_of[5], (D,), jnp.float32), 0.5, 1.5)
    shift_two = normal_values(streams_of[6], (D,), 0.2, 1.0, (), jnp.float32)
    w_qkv = normal_values(streams_of[7], (D, 3 * D), (D // 2) ** -0.5, 0.25, ((0, 8),))
    w_proj = normal_values(streams_of[8], (D, D), (D // 16) ** -0.5, 0.75, ((0, 8),))
    w_fc = normal_values(streams_of[9], (D, FF), D ** -0.5, 0.1875, ((0, 8),))
    w_out = normal_values(streams_of[10], (FF, D), (FF // 2) ** -0.5, 0.125, ((0, 8),))
    query_down_factor = normal_values(streams_of[11], (D, RANK), D ** -0.5, 0.1875, (), jnp.float32)
    query_up_factor = normal_values(streams_of[12], (RANK, D), 0.05, 0.3, (), jnp.float32)
    value_down_factor = normal_values(streams_of[13], (D, RANK), D ** -0.5, 0.1875, (), jnp.float32)
    value_up_factor = normal_values(streams_of[14], (RANK, D), 0.05, 0.3, (), jnp.float32)
    return dict(tokens=tokens, lengths=lengths, cotangent=cotangent, gain_one=gain_one, shift_one=shift_one, gain_two=gain_two, shift_two=shift_two, w_qkv=w_qkv, w_proj=w_proj, w_fc=w_fc, w_out=w_out, query_down_factor=query_down_factor, query_up_factor=query_up_factor, value_down_factor=value_down_factor, value_up_factor=value_up_factor)


@jax.custom_vjp
def narrow_product(v):
    return lax.optimization_barrier(v.astype(jnp.bfloat16)).astype(jnp.float32)

@jax.custom_vjp
def narrow_product_backward(v):
    return v

def low_keep(v):
    return (narrow_product(v), None)

def low_pass(kept, grad):
    return (grad,)

def back_keep(v):
    return (v, None)

def back_low(kept, grad):
    return (narrow_product(grad),)
narrow_product.defvjp(low_keep, low_pass)
narrow_product_backward.defvjp(back_keep, back_low)
adapter_scale_factor = 8.0
norm_eps = 1e-05
neg_big = -1e+30
finest_precision = lax.Precision.HIGHEST

def layer_norm(values, gain, shift):
    center = values - lax.optimization_barrier(jnp.mean(values, axis=-1, keepdims=True))
    spread = lax.optimization_barrier(jnp.mean(center * center, axis=-1, keepdims=True))
    return center * lax.rsqrt(spread + norm_eps) * gain + shift

def matrix_product(left, right):
    return jnp.dot(left, right, precision=finest_precision)

def sequence_forward(frozen, length, row_in, query_down_factor, query_up_factor, value_down_factor, value_up_factor):
    gain_one, shift_one, gain_two, shift_two, w_qkv, w_proj, w_fc, w_out = frozen
    seq_len = row_in.shape[0]
    embedding_width = row_in.shape[1]
    score_scale = 1.0 / math.sqrt(HD)
    query_down_low = narrow_product(query_down_factor)
    query_up_low = narrow_product(query_up_factor)
    value_down_low = narrow_product(value_down_factor)
    value_up_low = narrow_product(value_up_factor)
    normed_one = narrow_product(layer_norm(row_in, gain_one, shift_one))
    combined_weight = matrix_product(normed_one, w_qkv)
    query_narrow_product = narrow_product(narrow_product_backward(matrix_product(normed_one, query_down_low)))
    value_narrow_product = narrow_product(narrow_product_backward(matrix_product(normed_one, value_down_low)))
    query_rows = narrow_product(narrow_product_backward(combined_weight[:, :embedding_width] + adapter_scale_factor * matrix_product(query_narrow_product, query_up_low)))
    keys_all = narrow_product(narrow_product_backward(combined_weight[:, embedding_width:2 * embedding_width]))
    value_rows_complete = narrow_product(narrow_product_backward(combined_weight[:, 2 * embedding_width:] + adapter_scale_factor * matrix_product(value_narrow_product, value_up_low)))
    q_heads = query_rows.reshape(seq_len, H, HD)
    k_heads = keys_all.reshape(seq_len, H, HD)
    v_heads = value_rows_complete.reshape(seq_len, H, HD)
    raw_scores = jnp.einsum('qhd,khd->hqk', q_heads, k_heads, precision=finest_precision)
    scores = narrow_product_backward(raw_scores * score_scale)
    positions = jnp.arange(seq_len, dtype=jnp.int32)
    allowed = (positions[None, :] <= positions[:, None]) & (positions[None, :] < length)
    scores = jnp.where(allowed[None], scores, neg_big)
    row_top = lax.optimization_barrier(jnp.max(scores, axis=-1, keepdims=True))
    exp_scores = jnp.exp(scores - row_top)
    attn_probs = exp_scores / lax.optimization_barrier(jnp.sum(exp_scores, axis=-1, keepdims=True))
    attended = jnp.einsum('hqk,khd->qhd', narrow_product(attn_probs), v_heads, precision=finest_precision)
    attended = narrow_product(narrow_product_backward(attended.reshape(seq_len, embedding_width)))
    hidden = row_in + narrow_product_backward(matrix_product(attended, w_proj))
    normed_two = narrow_product(layer_norm(hidden, gain_two, shift_two))
    pre_act = narrow_product_backward(matrix_product(normed_two, w_fc))
    activated = narrow_product(jax.nn.gelu(pre_act, approximate=True))
    mlp_out = narrow_product_backward(matrix_product(activated, w_out))
    row_mask = (positions < length).astype(jnp.float32)[:, None]
    return row_mask * (hidden + mlp_out)

def reference(tokens, lengths, cotangent, gain_one, shift_one, gain_two, shift_two, w_qkv, w_proj, w_fc, w_out, query_down_factor, query_up_factor, value_down_factor, value_up_factor):
    frozen = (gain_one.astype(jnp.float32), shift_one.astype(jnp.float32), gain_two.astype(jnp.float32), shift_two.astype(jnp.float32), w_qkv.astype(jnp.float32), w_proj.astype(jnp.float32), w_fc.astype(jnp.float32), w_out.astype(jnp.float32))
    adapters = (query_down_factor.astype(jnp.float32), query_up_factor.astype(jnp.float32), value_down_factor.astype(jnp.float32), value_up_factor.astype(jnp.float32))

    def one_row(sums_sofar, row_items):
        row_in, row_cot, length = row_items

        def forward(x_in, down_q, up_q, down_v, up_v):
            return sequence_forward(frozen, length, x_in, down_q, up_q, down_v, up_v)
        row_out, pull_back = jax.vjp(forward, row_in, adapters[0], adapters[1], adapters[2], adapters[3])
        grads = pull_back(row_cot)
        new_sums = tuple((old + new for old, new in zip(sums_sofar, grads[1:])))
        return (new_sums, (row_out.astype(jnp.bfloat16), grads[0].astype(jnp.bfloat16)))
    zero_sums = tuple((jnp.zeros_like(item) for item in adapters))
    totals, (block_out, grad_tokens) = lax.scan(one_row, zero_sums, (tokens.astype(jnp.float32), cotangent.astype(jnp.float32), lengths))
    return (block_out, grad_tokens, totals[0], totals[1], totals[2], totals[3])
```

```python
import functools

import jax
import jax.numpy as jnp
from jax import lax
from jax.experimental import pallas as pl
from jax.experimental.pallas import tpu as pltpu
from jax.sharding import PartitionSpec as P

BF = jnp.bfloat16
F32 = jnp.float32
HD = 64
PAIR = 2 * HD
PAD = 128
SCALE = 8.0
EPS = 1e-05
NEG = -1e30
BLOCK = 256
FF_STEP = 512
VMEM_LIMIT = 58 * 2**20
GELU_C = 0.7978845608028654
GELU_A = 0.044715
ANY = pl.BlockSpec(memory_space=pl.ANY)
SMEM = pl.BlockSpec(memory_space=pltpu.SMEM)


def dot(a, b):
    return lax.dot_general(a, b, (((1,), (0,)), ((), ())), preferred_element_type=F32)


def dot_nt(a, b):
    return lax.dot_general(a, b, (((1,), (1,)), ((), ())), preferred_element_type=F32)


def dot_tn(a, b):
    return lax.dot_general(a, b, (((0,), (0,)), ((), ())), preferred_element_type=F32)


def lane(shape):
    return lax.broadcasted_iota(jnp.int32, shape, 1)


def row(shape):
    return lax.broadcasted_iota(jnp.int32, shape, 0)


def split3(x):
    a = x.astype(BF)
    r = x - a.astype(F32)
    b = r.astype(BF)
    c = (r - b.astype(F32)).astype(BF)
    return a, b, c


def whole(shape):
    return pl.BlockSpec(shape, lambda *_: (0,) * len(shape))


def params(**kw):
    return pltpu.CompilerParams(vmem_limit_bytes=VMEM_LIMIT, **kw)


def norm_stats(x):
    mean = jnp.mean(x, axis=-1, keepdims=True)
    center = x - mean
    inv = lax.rsqrt(jnp.mean(center * center, axis=-1, keepdims=True) + EPS)
    return center * inv, inv


def norm_back(xhat, inv, g):
    return inv * (
        g
        - jnp.mean(g, axis=-1, keepdims=True)
        - xhat * jnp.mean(g * xhat, axis=-1, keepdims=True)
    )


def pad_rows(parts, width):
    have = sum(p.shape[0] for p in parts)
    return jnp.concatenate(parts + [jnp.zeros((PAD - have, width), F32)], axis=0).astype(BF)


def norm_one_kernel(
    x_ref, gain_ref, shift_ref, dq_ref, dv_ref, uq_ref, uv_ref,
    n_ref, narrow_ref, down_ref, upq_ref, upv_ref,
):
    width = x_ref.shape[1]
    rank = dq_ref.shape[0]

    @pl.when(pl.program_id(0) == 0)
    def _():
        blank = jnp.zeros((rank, width), F32)
        down_ref[...] = pad_rows([dq_ref[...], dv_ref[...]], width)
        upq_ref[...] = pad_rows([uq_ref[...]], width)
        upv_ref[...] = pad_rows([blank, uv_ref[...]], width)

    xhat, _ = norm_stats(x_ref[...].astype(F32))
    low = (xhat * gain_ref[...] + shift_ref[...]).astype(BF)
    n_ref[...] = low
    narrow_ref[...] = dot_nt(low, down_ref[...]).astype(BF)


def norm_one(x, gain, shift, dq, dv, uq, uv):
    length, width = x.shape
    small = whole((1, width))
    adapter = whole(dq.shape)
    padded = whole((PAD, width))
    return pl.pallas_call(
        norm_one_kernel,
        grid=(length // BLOCK,),
        in_specs=[pl.BlockSpec((BLOCK, width), lambda i: (i, 0)), small, small] + [adapter] * 4,
        out_specs=[
            pl.BlockSpec((BLOCK, width), lambda i: (i, 0)),
            pl.BlockSpec((BLOCK, PAD), lambda i: (i, 0)),
            padded, padded, padded,
        ],
        out_shape=[
            jax.ShapeDtypeStruct((length, width), BF),
            jax.ShapeDtypeStruct((length, PAD), BF),
        ]
        + [jax.ShapeDtypeStruct((PAD, width), BF)] * 3,
        compiler_params=params(),
        name="norm_one",
    )(x, gain, shift, dq, dv, uq, uv)


def attend_pair(length, q, kp, vp, o_ref, qx_ref, col, kx, vx):
    size = kp.shape[0]
    ln = lane((size, PAIR))
    first = ln < HD
    bias = jnp.where(row((size, PAIR)) < length, 0.0, NEG).astype(BF)
    zero = jnp.zeros((size, PAIR), BF)
    kx[0] = jnp.where(first, kp, jnp.where(ln == HD, bias, zero))
    kx[1] = jnp.where(first, jnp.where(ln == 0, bias, zero), kp)
    vx[:, :PAIR] = vp
    vx[:, PAIR:] = jnp.ones((size, PAIR), BF)
    for i in range(size // BLOCK):
        begin, end = i * BLOCK, (i + 1) * BLOCK
        lq = lane((BLOCK, PAIR))
        fq = lq < HD
        qs = q[begin:end].astype(F32) * (1.0 / HD**0.5)
        outs = []
        for h in range(2):
            other = HD * (1 - h)
            base = jnp.where(fq if h == 0 else ~fq, qs, jnp.where(lq == other, 1.0, 0.0))
            qh = base.astype(BF)
            near = dot_nt(qh, kx[h, begin:end, :])
            near = jnp.where(lane((BLOCK, BLOCK)) <= row((BLOCK, BLOCK)), near, NEG)
            top = jnp.max(near, axis=-1, keepdims=True)
            if i:
                far = dot_nt(qh, kx[h, :begin, :])
                top = jnp.maximum(top, jnp.max(far, axis=-1, keepdims=True))
            acc = dot(jnp.exp(near - top).astype(BF), vx[begin:end, :])
            if i:
                acc = acc + dot(jnp.exp(far - top).astype(BF), vx[:begin, :])
            total = acc[:, PAIR:]
            outs.append(acc[:, :PAIR] / total)
            a, b, c = split3(-(top + jnp.log(total)))
            kept = jnp.where(
                lq == other + 1,
                a.astype(F32),
                jnp.where(
                    lq == other + 2,
                    b.astype(F32),
                    jnp.where(lq == other + 3, c.astype(F32), base),
                ),
            )
            at = 2 * col + h * PAIR
            qx_ref[begin:end, at : at + PAIR] = kept.astype(BF)
        o_ref[begin:end, col : col + PAIR] = jnp.where(fq, outs[0], outs[1]).astype(BF)


QUAD = 2 * PAIR


def qkv_copies(parts, index_ref, shards, wbuf, sem, step, slot, group):
    rows = shards[0].shape[0]
    copies = []
    for i, ref in enumerate(shards):
        at = pl.multiple_of(index_ref[i] * rows, rows)
        for p in range(parts):
            src = ref.at[:, pl.ds(pl.multiple_of(p * group + step * QUAD, QUAD), QUAD)]
            dst = wbuf.at[slot, pl.ds(at, rows), pl.ds(p * QUAD, QUAD)]
            copies.append(pltpu.make_async_copy(src, dst, sem.at[slot]))
    return copies


def forward_kernel(count, len_ref, index_ref, *refs):
    shards = refs[:count]
    n_ref, narrow_ref, upq_ref, upv_ref, o_ref, qx_ref, k_ref, v_ref, wbuf, kx, vx, sem = refs[count:]
    step = pl.program_id(0)
    steps = pl.num_programs(0)
    group = shards[0].shape[1] // 3
    slot = lax.rem(step, 2)

    @pl.when(step == 0)
    def _():
        for c in qkv_copies(3, index_ref, shards, wbuf, sem, 0, 0, group):
            c.start()

    @pl.when(step + 1 < steps)
    def _():
        for c in qkv_copies(3, index_ref, shards, wbuf, sem, step + 1, 1 - slot, group):
            c.start()

    for c in qkv_copies(3, index_ref, shards, wbuf, sem, step, slot, group):
        c.wait()
    n = n_ref[...]
    narrow = narrow_ref[...]
    q = dot(n, wbuf[slot, :, :QUAD]) + SCALE * dot(narrow, upq_ref[...])
    k = dot(n, wbuf[slot, :, QUAD : 2 * QUAD])
    v = dot(n, wbuf[slot, :, 2 * QUAD :]) + SCALE * dot(narrow, upv_ref[...])
    q = q.astype(BF)
    k_ref[...] = k.astype(BF)
    v_ref[...] = v.astype(BF)
    length = len_ref[0]
    for p in range(2):
        col = p * PAIR
        attend_pair(
            length,
            q[:, col : col + PAIR],
            k_ref[:, col : col + PAIR],
            v_ref[:, col : col + PAIR],
            o_ref, qx_ref, col, kx, vx,
        )


def attention_forward(lengths, index, shards, n, narrow, upq, upv):
    length, width = n.shape
    group = shards[0].shape[1] // 3
    steps = group // QUAD
    quad = pl.BlockSpec((length, QUAD), lambda s: (0, s))
    up = pl.BlockSpec((PAD, QUAD), lambda s: (0, s))
    return pl.pallas_call(
        functools.partial(forward_kernel, len(shards)),
        grid=(steps,),
        in_specs=[SMEM, SMEM]
        + [ANY] * len(shards)
        + [whole((length, width)), whole((length, PAD)), up, up],
        out_specs=[quad, pl.BlockSpec((length, 2 * QUAD), lambda s: (0, s)), quad, quad],
        out_shape=[
            jax.ShapeDtypeStruct((length, group), BF),
            jax.ShapeDtypeStruct((length, 2 * group), BF),
            jax.ShapeDtypeStruct((length, group), BF),
            jax.ShapeDtypeStruct((length, group), BF),
        ],
        scratch_shapes=[
            pltpu.VMEM((2, width, 3 * QUAD), BF),
            pltpu.VMEM((2, length, PAIR), BF),
            pltpu.VMEM((length, QUAD), BF),
            pltpu.SemaphoreType.DMA((2,)),
        ],
        compiler_params=params(),
        name="attention_forward",
    )(lengths, index, *shards, n, narrow, upq, upv)


def ff_copies(index_ref, fcs, outs, fbuf, obuf, sem, step, slot):
    rows = fcs[0].shape[0]
    copies = []
    for i, ref in enumerate(fcs):
        at = pl.multiple_of(index_ref[i] * rows, rows)
        src = ref.at[:, pl.ds(pl.multiple_of(step * FF_STEP, FF_STEP), FF_STEP)]
        copies.append(pltpu.make_async_copy(src, fbuf.at[slot, pl.ds(at, rows), :], sem.at[slot]))
    src = outs.at[pl.ds(pl.multiple_of(step * FF_STEP, FF_STEP), FF_STEP), :]
    copies.append(pltpu.make_async_copy(src, obuf.at[slot], sem.at[slot]))
    return copies


def proj_copies(index_ref, projs, wbuf, sem):
    rows = projs[0].shape[0]
    copies = []
    for i, ref in enumerate(projs):
        at = pl.multiple_of(index_ref[i] * rows, rows)
        copies.append(pltpu.make_async_copy(ref, wbuf.at[pl.ds(at, rows), :], sem.at[0]))
    return copies


def gelu_both(v):
    square = v * v
    t = jnp.tanh(v * (GELU_C + (GELU_C * GELU_A) * square))
    half = 0.5 * t + 0.5
    act = v * half
    slope = half + act * (1.0 - half) * (2.0 * GELU_C + (6.0 * GELU_C * GELU_A) * square)
    return act, slope


def middle_kernel(count, heads, len_ref, index_ref, *refs):
    projs, refs = refs[:count], refs[count:]
    fcs, refs = refs[:count], refs[count:]
    outs, refs = refs[0], refs[1:]
    atts, refs = refs[:heads], refs[heads:]
    (x_ref, cot_ref, gain_ref, shift_ref, block_ref, gh_ref, ga_ref,
     wproj, fbuf, obuf, hidden, n2, low, acc, back, psem, sem) = refs
    step = pl.program_id(0)
    steps = pl.num_programs(0)
    size = x_ref.shape[0]
    slot = lax.rem(step, 2)

    @pl.when(step == 0)
    def _():
        first = proj_copies(index_ref, projs, wproj, psem)
        for c in first:
            c.start()
        for c in ff_copies(index_ref, fcs, outs, fbuf, obuf, sem, 0, 0):
            c.start()
        for c in first:
            c.wait()
        for i in range(size // BLOCK):
            at = pl.ds(i * BLOCK, BLOCK)
            total = x_ref[at, :].astype(F32)
            for j, ref in enumerate(atts):
                wide = ref.shape[1]
                total = total + dot(ref[at, :], wproj[j * wide : (j + 1) * wide, :])
            hidden[at, :] = total
            xhat, _ = norm_stats(total)
            n2[at, :] = (xhat * gain_ref[...] + shift_ref[...]).astype(BF)
            keep = row((BLOCK, 1)) + i * BLOCK < len_ref[0]
            low[at, :] = jnp.where(keep, cot_ref[at, :].astype(F32), 0.0).astype(BF)

    @pl.when(step + 1 < steps)
    def _():
        for c in ff_copies(index_ref, fcs, outs, fbuf, obuf, sem, step + 1, 1 - slot):
            c.start()

    for c in ff_copies(index_ref, fcs, outs, fbuf, obuf, sem, step, slot):
        c.wait()
    fc = fbuf[slot]
    out = obuf[slot]
    for i in range(size // BLOCK):
        at = pl.ds(i * BLOCK, BLOCK)
        act, slope = gelu_both(dot(n2[at, :], fc))
        mlp = dot(act.astype(BF), out)
        grad = (dot_nt(low[at, :], out) * slope).astype(BF)
        u = dot_nt(grad, fc)

        @pl.when(step == 0)
        def _():
            acc[at, :] = mlp
            back[at, :] = u

        @pl.when(step > 0)
        def _():
            acc[at, :] += mlp
            back[at, :] += u

    @pl.when(step == steps - 1)
    def _():
        for i in range(size // BLOCK):
            at = pl.ds(i * BLOCK, BLOCK)
            h = hidden[at, :]
            keep = row((BLOCK, 1)) + i * BLOCK < len_ref[0]
            block_ref[at, :] = jnp.where(keep, h + acc[at, :], 0.0).astype(BF)
            xhat, inv = norm_stats(h)
            gh = low[at, :].astype(F32) + norm_back(xhat, inv, gain_ref[...] * back[at, :])
            gh_ref[at, :] = gh
            ga_ref[at, :] = dot_nt(gh.astype(BF), wproj[...]).astype(BF)


def middle(lengths, index, projs, fcs, outs, atts, x, cot, gain, shift):
    size, width = x.shape
    hidden_units = outs.shape[0]
    full = whole((size, width))
    once = pl.BlockSpec((size, width), lambda s: (0, 0), pipeline_mode=pl.Buffered(1))
    return pl.pallas_call(
        functools.partial(middle_kernel, len(projs), len(atts)),
        grid=(hidden_units // FF_STEP,),
        in_specs=[SMEM, SMEM]
        + [ANY] * (2 * len(projs) + 1)
        + [whole(a.shape) for a in atts]
        + [once, once, whole((1, width)), whole((1, width))],
        out_specs=[full, full, full],
        out_shape=[
            jax.ShapeDtypeStruct((size, width), BF),
            jax.ShapeDtypeStruct((size, width), F32),
            jax.ShapeDtypeStruct((size, width), BF),
        ],
        scratch_shapes=[
            pltpu.VMEM((width, width), BF),
            pltpu.VMEM((2, width, FF_STEP), BF),
            pltpu.VMEM((2, FF_STEP, width), BF),
            pltpu.VMEM((size, width), F32),
            pltpu.VMEM((size, width), BF),
            pltpu.VMEM((size, width), BF),
            pltpu.VMEM((size, width), F32),
            pltpu.VMEM((size, width), F32),
            pltpu.SemaphoreType.DMA((1,)),
            pltpu.SemaphoreType.DMA((2,)),
        ],
        compiler_params=params(),
        name="middle",
    )(lengths, index, *projs, *fcs, outs, *atts, x, cot, gain, shift)


def backward_kernel(
    len_ref, qx_ref, k_ref, v_ref, o_ref, g_ref, dq_ref, dk_ref, dv_ref, kx, vx, gx, dqa
):
    size = k_ref.shape[0]
    ln = lane((size, PAIR))
    first = ln < HD
    bias = jnp.where(row((size, PAIR)) < len_ref[0], 0.0, NEG).astype(BF)
    kp = k_ref[...]
    vp = v_ref[...]
    g = g_ref[...]
    zero = jnp.zeros((size, PAIR), BF)
    one = jnp.ones((size, PAIR), BF)
    prod = g.astype(F32) * o_ref[...].astype(F32)
    for h in range(2):
        other = HD * (1 - h)
        mine = first if h == 0 else ~first
        extra = (ln > other) & (ln <= other + 3)
        kx[h] = jnp.where(mine, kp, jnp.where(ln == other, bias, jnp.where(extra, one, zero)))
        vx[h] = jnp.where(mine, vp, jnp.where(extra, one, zero))
        dots = jnp.sum(jnp.where(mine, prod, 0.0), axis=-1, keepdims=True)
        a, b, c = split3(jnp.broadcast_to(-dots, (size, PAIR)))
        gx[h] = jnp.where(
            mine,
            g,
            jnp.where(
                ln == other + 1,
                a,
                jnp.where(ln == other + 2, b, jnp.where(ln == other + 3, c, zero)),
            ),
        )
    qp = jnp.where(first, qx_ref[:, :PAIR], qx_ref[:, PAIR:])
    blocks = size // BLOCK
    for kb in range(blocks):
        keys = slice(kb * BLOCK, (kb + 1) * BLOCK)
        dvs = []
        dks = []
        for h in range(2):
            dv = dk = None
            for qb in range(kb, blocks):
                queries = slice(qb * BLOCK, (qb + 1) * BLOCK)
                st = dot_nt(kx[h, keys, :], qx_ref[queries, h * PAIR : (h + 1) * PAIR])
                if qb == kb:
                    st = jnp.where(row((BLOCK, BLOCK)) <= lane((BLOCK, BLOCK)), st, NEG)
                p = jnp.exp(st)
                dp = dot_nt(vx[h, keys, :], gx[h, queries, :])
                ds = (p * dp).astype(BF)
                a = dot(p.astype(BF), g[queries])
                b = dot(ds, qp[queries])
                c = dot_tn(ds, kp[keys])
                dv = a if dv is None else dv + a
                dk = b if dk is None else dk + b
                if kb == 0:
                    dqa[h, queries, :] = c
                else:
                    dqa[h, queries, :] += c
            dvs.append(dv)
            dks.append(dk)
        f = lane((BLOCK, PAIR)) < HD
        dv_ref[keys, :] = jnp.where(f, dvs[0], dvs[1]).astype(BF)
        dk_ref[keys, :] = jnp.where(f, dks[0], dks[1]).astype(BF)
    dq_ref[...] = (jnp.where(first, dqa[0], dqa[1]) * (1.0 / HD**0.5)).astype(BF)


def attention_backward(lengths, qx, k, v, o, ga, at):
    size, group = k.shape
    pair = pl.BlockSpec((size, PAIR), lambda p: (0, p))
    start = at // PAIR
    return pl.pallas_call(
        backward_kernel,
        grid=(group // PAIR,),
        in_specs=[
            SMEM,
            pl.BlockSpec((size, 2 * PAIR), lambda p: (0, p)),
            pair, pair, pair,
            pl.BlockSpec((size, PAIR), lambda p: (0, p + start)),
        ],
        out_specs=[pair] * 3,
        out_shape=[jax.ShapeDtypeStruct((size, group), BF)] * 3,
        scratch_shapes=[pltpu.VMEM((2, size, PAIR), BF)] * 3 + [pltpu.VMEM((2, size, PAIR), F32)],
        compiler_params=params(),
        name="attention_backward",
    )(lengths, qx, k, v, o, ga)


def adapter_kernel(groups, *refs):
    dqs, refs = refs[:groups], refs[groups:]
    dvs, refs = refs[:groups], refs[groups:]
    n_ref, narrow_ref, upq_ref, upv_ref, joint_ref, sums_ref = refs
    narrow = narrow_ref[...]
    total = None
    for j in range(groups):
        wide = dqs[j].shape[1]
        cols = slice(j * wide, (j + 1) * wide)
        dq = dqs[j][...]
        dv = dvs[j][...]
        part = dot_nt(dq, upq_ref[:, cols]) + dot_nt(dv, upv_ref[:, cols])
        total = part if total is None else total + part
        gq = SCALE * dot_tn(narrow, dq)
        gv = SCALE * dot_tn(narrow, dv)
        sums_ref[8:16, cols] = jnp.where(row((8, wide)) < 4, gq[:8], gv[:8])
    joint = (SCALE * total).astype(BF)
    joint_ref[...] = joint
    sums_ref[0:8, :] = dot_tn(joint, n_ref[...])[:8]


def adapter_sums(dqs, dvs, n, narrow, upq, upv):
    size, width = n.shape
    return pl.pallas_call(
        functools.partial(adapter_kernel, len(dqs)),
        out_shape=[
            jax.ShapeDtypeStruct((size, PAD), BF),
            jax.ShapeDtypeStruct((16, width), F32),
        ],
        compiler_params=params(),
        name="adapter_sums",
    )(*dqs, *dvs, n, narrow, upq, upv)


def token_copies(index_ref, shards, wbuf, sem, step, slot, group):
    rows = shards[0].shape[0]
    copies = []
    for i, ref in enumerate(shards):
        at = pl.multiple_of(index_ref[i] * rows, rows)
        copies.append(
            pltpu.make_async_copy(
                ref.at[:, step * group : (step + 1) * group],
                wbuf.at[slot, pl.ds(at, rows), :],
                sem.at[slot],
            )
        )
    return copies


def token_kernel(count, groups, index_ref, *refs):
    shards, refs = refs[: count * groups], refs[count * groups :]
    grads, refs = refs[: 3 * groups], refs[3 * groups :]
    joint_ref, down_ref, gh_ref, x_ref, gain_ref, o_ref, wbuf, acc, sem = refs
    size = x_ref.shape[0]
    group = shards[0].shape[1] // 3
    steps = [(j, p) for j in range(groups) for p in range(3)]

    def copies(s):
        j, p = steps[s]
        return token_copies(
            index_ref, shards[j * count : (j + 1) * count], wbuf, sem, p, s % 2, group
        )

    for c in copies(0):
        c.start()
    for s, (j, p) in enumerate(steps):
        if s + 1 < len(steps):
            for c in copies(s + 1):
                c.start()
        for c in copies(s):
            c.wait()
        g = grads[p * groups + j]
        for i in range(size // BLOCK):
            at = pl.ds(i * BLOCK, BLOCK)
            part = dot_nt(g[at, :], wbuf[s % 2])
            if s == 0:
                part = part + dot(joint_ref[at, :], down_ref[...])
            else:
                part = part + acc[at, :]
            if s + 1 < len(steps):
                acc[at, :] = part
            else:
                xhat, inv = norm_stats(x_ref[at, :].astype(F32))
                o_ref[at, :] = (
                    gh_ref[at, :] + norm_back(xhat, inv, gain_ref[...] * part)
                ).astype(BF)


def token_gradient(index, shards, dqs, dks, dvs, joint, down, gh, x, gain):
    size, width = x.shape
    groups = len(dqs)
    count = len(shards[0])
    group = shards[0][0].shape[1] // 3
    flat = [s for part in shards for s in part]
    vm = pl.BlockSpec(memory_space=pltpu.VMEM)
    return pl.pallas_call(
        functools.partial(token_kernel, count, groups),
        in_specs=[SMEM] + [ANY] * len(flat) + [vm] * (3 * groups + 5),
        out_specs=vm,
        out_shape=jax.ShapeDtypeStruct((size, width), BF),
        scratch_shapes=[
            pltpu.VMEM((2, width, group), BF),
            pltpu.VMEM((size, width), F32),
            pltpu.SemaphoreType.DMA((2,)),
        ],
        compiler_params=params(),
        name="token_gradient",
    )(index, *flat, *dqs, *dks, *dvs, joint, down, gh, x, gain)


def local(
    tokens, lengths, cotangent, gain_one, shift_one, gain_two, shift_two,
    w_qkv, w_proj, w_fc, w_out,
    query_down_factor, query_up_factor, value_down_factor, value_up_factor,
):
    _, size, width = tokens.shape
    x = tokens.reshape(size, width)
    cot = cotangent.reshape(size, width)

    def gather(w):
        return lax.all_gather(w, "fsdp", axis=0, tiled=True)

    qkv, proj, fc, out = gather(w_qkv), gather(w_proj), gather(w_fc), gather(w_out)
    index = jnp.zeros((1,), jnp.int32)

    n, narrow, down, upq, upv = norm_one(
        x, gain_one[None], shift_one[None],
        query_down_factor.T, value_down_factor.T, query_up_factor, value_up_factor,
    )
    o, qx, k, v = attention_forward(lengths, index, [qkv], n, narrow, upq, upv)
    block_out, gh, ga = middle(
        lengths, index, [proj], [fc], out, [o], x, cot, gain_two[None], shift_two[None]
    )
    dq, dk, dv = attention_backward(lengths, qx, k, v, o, ga, 0)
    joint, sums = adapter_sums([dq], [dv], n, narrow, upq, upv)
    sums = lax.psum(sums, ("dp", "fsdp"))
    grad = token_gradient(index, [[qkv]], [dq], [dk], [dv], joint, down, gh, x, gain_one[None])
    return (
        block_out.reshape(tokens.shape),
        grad.reshape(tokens.shape),
        sums[0:4].T,
        sums[8:12],
        sums[4:8].T,
        sums[12:16],
    )


def solution(mesh):
    rows = P(("dp", "fsdp"), None, None)
    frozen = P("fsdp", None)
    return jax.shard_map(
        local,
        mesh=mesh,
        in_specs=(rows, P(("dp", "fsdp")), rows, P(), P(), P(), P())
        + (frozen,) * 4
        + (P(),) * 4,
        out_specs=(rows, rows, P(), P(), P(), P()),
        check_vma=False,
    )
```

```python
import functools

import jax
import jax.numpy as jnp
from jax import lax
from jax.experimental import pallas as pl
from jax.experimental.pallas import tpu as pltpu
from jax.sharding import PartitionSpec as P

BF = jnp.bfloat16
F32 = jnp.float32
HD = 64
PAIR = 2 * HD
PAD = 128
SCALE = 8.0
EPS = 1e-05
NEG = -1e30
BLOCK = 256
FF_STEP = 512
VMEM_LIMIT = 58 * 2**20
GELU_C = 0.7978845608028654
GELU_A = 0.044715
ANY = pl.BlockSpec(memory_space=pl.ANY)
SMEM = pl.BlockSpec(memory_space=pltpu.SMEM)


def dot(a, b):
    return lax.dot_general(a, b, (((1,), (0,)), ((), ())), preferred_element_type=F32)


def dot_nt(a, b):
    return lax.dot_general(a, b, (((1,), (1,)), ((), ())), preferred_element_type=F32)


def dot_tn(a, b):
    return lax.dot_general(a, b, (((0,), (0,)), ((), ())), preferred_element_type=F32)


def lane(shape):
    return lax.broadcasted_iota(jnp.int32, shape, 1)


def row(shape):
    return lax.broadcasted_iota(jnp.int32, shape, 0)


def split3(x):
    a = x.astype(BF)
    r = x - a.astype(F32)
    b = r.astype(BF)
    c = (r - b.astype(F32)).astype(BF)
    return a, b, c


def whole(shape):
    return pl.BlockSpec(shape, lambda *_: (0,) * len(shape))


def params(**kw):
    return pltpu.CompilerParams(vmem_limit_bytes=VMEM_LIMIT, **kw)


def norm_stats(x):
    mean = jnp.mean(x, axis=-1, keepdims=True)
    center = x - mean
    inv = lax.rsqrt(jnp.mean(center * center, axis=-1, keepdims=True) + EPS)
    return center * inv, inv


def norm_back(xhat, inv, g):
    return inv * (
        g
        - jnp.mean(g, axis=-1, keepdims=True)
        - xhat * jnp.mean(g * xhat, axis=-1, keepdims=True)
    )


def pad_rows(parts, width):
    have = sum(p.shape[0] for p in parts)
    return jnp.concatenate(parts + [jnp.zeros((PAD - have, width), F32)], axis=0).astype(BF)


def norm_one_kernel(
    x_ref, gain_ref, shift_ref, dq_ref, dv_ref, uq_ref, uv_ref,
    n_ref, narrow_ref, down_ref, upq_ref, upv_ref,
):
    width = x_ref.shape[1]
    rank = dq_ref.shape[0]

    @pl.when(pl.program_id(0) == 0)
    def _():
        blank = jnp.zeros((rank, width), F32)
        down_ref[...] = pad_rows([dq_ref[...], dv_ref[...]], width)
        upq_ref[...] = pad_rows([uq_ref[...]], width)
        upv_ref[...] = pad_rows([blank, uv_ref[...]], width)

    xhat, _ = norm_stats(x_ref[...].astype(F32))
    low = (xhat * gain_ref[...] + shift_ref[...]).astype(BF)
    n_ref[...] = low
    narrow_ref[...] = dot_nt(low, down_ref[...]).astype(BF)


def norm_one(x, gain, shift, dq, dv, uq, uv):
    length, width = x.shape
    small = whole((1, width))
    adapter = whole(dq.shape)
    padded = whole((PAD, width))
    return pl.pallas_call(
        norm_one_kernel,
        grid=(length // BLOCK,),
        in_specs=[pl.BlockSpec((BLOCK, width), lambda i: (i, 0)), small, small] + [adapter] * 4,
        out_specs=[
            pl.BlockSpec((BLOCK, width), lambda i: (i, 0)),
            pl.BlockSpec((BLOCK, PAD), lambda i: (i, 0)),
            padded, padded, padded,
        ],
        out_shape=[
            jax.ShapeDtypeStruct((length, width), BF),
            jax.ShapeDtypeStruct((length, PAD), BF),
        ]
        + [jax.ShapeDtypeStruct((PAD, width), BF)] * 3,
        compiler_params=params(),
        name="norm_one",
    )(x, gain, shift, dq, dv, uq, uv)


def attend_pair(length, q, kp, vp, o_ref, qx_ref, col, kx, vx):
    size = kp.shape[0]
    ln = lane((size, PAIR))
    first = ln < HD
    bias = jnp.where(row((size, PAIR)) < length, 0.0, NEG).astype(BF)
    zero = jnp.zeros((size, PAIR), BF)
    kx[0] = jnp.where(first, kp, jnp.where(ln == HD, bias, zero))
    kx[1] = jnp.where(first, jnp.where(ln == 0, bias, zero), kp)
    vx[:, :PAIR] = vp
    vx[:, PAIR:] = jnp.ones((size, PAIR), BF)
    for i in range(size // BLOCK):
        begin, end = i * BLOCK, (i + 1) * BLOCK
        lq = lane((BLOCK, PAIR))
        fq = lq < HD
        qs = q[begin:end].astype(F32) * (1.0 / HD**0.5)
        outs = []
        for h in range(2):
            other = HD * (1 - h)
            base = jnp.where(fq if h == 0 else ~fq, qs, jnp.where(lq == other, 1.0, 0.0))
            qh = base.astype(BF)
            near = dot_nt(qh, kx[h, begin:end, :])
            near = jnp.where(lane((BLOCK, BLOCK)) <= row((BLOCK, BLOCK)), near, NEG)
            top = jnp.max(near, axis=-1, keepdims=True)
            if i:
                far = dot_nt(qh, kx[h, :begin, :])
                top = jnp.maximum(top, jnp.max(far, axis=-1, keepdims=True))
            acc = dot(jnp.exp(near - top).astype(BF), vx[begin:end, :])
            if i:
                acc = acc + dot(jnp.exp(far - top).astype(BF), vx[:begin, :])
            total = acc[:, PAIR:]
            outs.append(acc[:, :PAIR] / total)
            a, b, c = split3(-(top + jnp.log(total)))
            kept = jnp.where(
                lq == other + 1,
                a.astype(F32),
                jnp.where(
                    lq == other + 2,
                    b.astype(F32),
                    jnp.where(lq == other + 3, c.astype(F32), base),
                ),
            )
            at = 2 * col + h * PAIR
            qx_ref[begin:end, at : at + PAIR] = kept.astype(BF)
        o_ref[begin:end, col : col + PAIR] = jnp.where(fq, outs[0], outs[1]).astype(BF)


QUAD = 2 * PAIR


def qkv_copies(index_ref, shards, wbuf, sem, quad, group):
    rows = shards[0].shape[0]
    copies = []
    for i, ref in enumerate(shards):
        at = pl.multiple_of(index_ref[i] * rows, rows)
        for p in range(3):
            col = p * group + quad * QUAD
            src = ref.at[:, col : col + QUAD]
            dst = wbuf.at[pl.ds(at, rows), p * QUAD : (p + 1) * QUAD]
            copies.append(pltpu.make_async_copy(src, dst, sem.at[p]))
    return copies


def forward_kernel(count, kept, quad, group, len_ref, index_ref, *refs):
    shards, refs = refs[:count], refs[count + kept :]
    n_ref, narrow_ref, upq_ref, upv_ref, o_ref, qx_ref, k_ref, v_ref, wbuf, kx, vx, sem = refs
    copies = qkv_copies(index_ref, shards, wbuf, sem, quad, group)
    for c in copies:
        c.start()
    for c in copies:
        c.wait()
    n = n_ref[...]
    narrow = narrow_ref[...]
    q = dot(n, wbuf[:, :QUAD]) + SCALE * dot(narrow, upq_ref[...])
    k = dot(n, wbuf[:, QUAD : 2 * QUAD])
    v = dot(n, wbuf[:, 2 * QUAD :]) + SCALE * dot(narrow, upv_ref[...])
    q = q.astype(BF)
    k_ref[...] = k.astype(BF)
    v_ref[...] = v.astype(BF)
    length = len_ref[0]
    for p in range(2):
        col = p * PAIR
        attend_pair(
            length,
            q[:, col : col + PAIR],
            k_ref[:, col : col + PAIR],
            v_ref[:, col : col + PAIR],
            o_ref, qx_ref, col, kx, vx,
        )


def attention_forward(lengths, index, shards, n, narrow, upq, upv, quad, group, at, kept):
    length, width = n.shape
    here = at // QUAD + quad
    block = pl.BlockSpec((length, QUAD), lambda s: (0, here))
    up = pl.BlockSpec((PAD, QUAD), lambda s: (0, here))
    first = 2 + len(shards)
    return pl.pallas_call(
        functools.partial(forward_kernel, len(shards), len(kept), quad, group),
        grid=(1,),
        in_specs=[SMEM, SMEM]
        + [ANY] * (len(shards) + len(kept))
        + [whole((length, width)), whole((length, PAD)), up, up],
        out_specs=[block, pl.BlockSpec((length, 2 * QUAD), lambda s: (0, here)), block, block],
        out_shape=[
            jax.ShapeDtypeStruct((length, width), BF),
            jax.ShapeDtypeStruct((length, 2 * width), BF),
            jax.ShapeDtypeStruct((length, width), BF),
            jax.ShapeDtypeStruct((length, width), BF),
        ],
        input_output_aliases={first + i: i for i in range(len(kept))},
        scratch_shapes=[
            pltpu.VMEM((width, 3 * QUAD), BF),
            pltpu.VMEM((2, length, PAIR), BF),
            pltpu.VMEM((length, QUAD), BF),
            pltpu.SemaphoreType.DMA((3,)),
        ],
        compiler_params=params(),
        cost_estimate=pl.CostEstimate(
            flops=2 * length * width * 3 * QUAD + 16 * length * length * QUAD,
            bytes_accessed=8 * 2**20,
            transcendentals=4 * length * length,
        ),
        name="attention_forward",
    )(lengths, index, *shards, *kept, n, narrow, upq, upv)


def ff_copies(index_ref, fcs, outs, fbuf, obuf, sem, step):
    rows = fcs[0].shape[0]
    per = outs[0].shape[0] // FF_STEP
    slot = step % 2
    shard, part = divmod(step, per)
    col = pl.multiple_of((index_ref[shard] * per + part) * FF_STEP, FF_STEP)
    copies = []
    for i, ref in enumerate(fcs):
        at = pl.multiple_of(index_ref[i] * rows, rows)
        src = ref.at[:, pl.ds(col, FF_STEP)]
        copies.append(pltpu.make_async_copy(src, fbuf.at[slot, pl.ds(at, rows), :], sem.at[slot]))
    src = outs[shard].at[part * FF_STEP : (part + 1) * FF_STEP, :]
    copies.append(pltpu.make_async_copy(src, obuf.at[slot], sem.at[slot]))
    return copies


def proj_copies(index_ref, projs, col, wbuf, sem):
    rows = projs[0].shape[0]
    width = wbuf.shape[1]
    copies = []
    for i, ref in enumerate(projs):
        at = pl.multiple_of(index_ref[i] * rows, rows)
        src = ref.at[:, col : col + width]
        copies.append(pltpu.make_async_copy(src, wbuf.at[pl.ds(at, rows), :], sem.at[0]))
    return copies


def gelu_both(v):
    square = v * v
    t = jnp.tanh(v * (GELU_C + (GELU_C * GELU_A) * square))
    half = 0.5 * t + 0.5
    act = v * half
    slope = half + act * (1.0 - half) * (2.0 * GELU_C + (6.0 * GELU_C * GELU_A) * square)
    return act, slope


def middle_kernel(count, col, len_ref, index_ref, *refs):
    projs, refs = refs[:count], refs[count:]
    fcs, refs = refs[:count], refs[count:]
    outs, refs = refs[:count], refs[count:]
    (att_ref, x_ref, cot_ref, gain_ref, shift_ref, block_ref, gh_ref, ga_ref,
     wproj, fbuf, obuf, hidden, n2, low, acc, back, psem, sem) = refs
    size = x_ref.shape[0]
    steps = count * outs[0].shape[0] // FF_STEP
    step = pl.program_id(0)
    slot = lax.rem(step, 2)
    copies = functools.partial(ff_copies, index_ref, fcs, outs, fbuf, obuf, sem)

    @pl.when(step == 0)
    def _():
        first = proj_copies(index_ref, projs, col, wproj, psem)
        for c in first:
            c.start()
        for c in copies(0):
            c.start()
        for c in first:
            c.wait()
        for i in range(size // BLOCK):
            at = pl.ds(i * BLOCK, BLOCK)
            total = x_ref[at, :].astype(F32) + dot(att_ref[at, :], wproj[...])
            hidden[at, :] = total
            xhat, _ = norm_stats(total)
            n2[at, :] = (xhat * gain_ref[...] + shift_ref[...]).astype(BF)
            keep = row((BLOCK, 1)) + i * BLOCK < len_ref[0]
            low[at, :] = jnp.where(keep, cot_ref[at, :].astype(F32), 0.0).astype(BF)
            acc[at, :] = jnp.zeros((BLOCK, x_ref.shape[1]), F32)
            back[at, :] = jnp.zeros((BLOCK, x_ref.shape[1]), F32)

    for s in range(1, steps):

        @pl.when(step + 1 == s)
        def _(s=s):
            for c in copies(s):
                c.start()

    for even in range(2):

        @pl.when(slot == even)
        def _(even=even):
            for c in copies(even):
                c.wait()

    for i in range(size // BLOCK):
        at = pl.ds(i * BLOCK, BLOCK)
        act, slope = gelu_both(dot(n2[at, :], fbuf[slot]))
        acc[at, :] += dot(act.astype(BF), obuf[slot])
        grad = (dot_nt(low[at, :], obuf[slot]) * slope).astype(BF)
        back[at, :] += dot_nt(grad, fbuf[slot])

    @pl.when(step == steps - 1)
    def _():
        for i in range(size // BLOCK):
            at = pl.ds(i * BLOCK, BLOCK)
            h = hidden[at, :]
            keep = row((BLOCK, 1)) + i * BLOCK < len_ref[0]
            block_ref[at, :] = jnp.where(keep, h + acc[at, :], 0.0).astype(BF)
            xhat, inv = norm_stats(h)
            gh = low[at, :].astype(F32) + norm_back(xhat, inv, gain_ref[...] * back[at, :])
            gh_ref[at, :] = gh
            ga_ref[at, :] = dot_nt(gh.astype(BF), wproj[...]).astype(BF)


def middle(lengths, index, projs, col, fcs, outs, att, x, cot, gain, shift):
    size, width = x.shape
    vm = pl.BlockSpec(memory_space=pltpu.VMEM)
    units = len(outs) * outs[0].shape[0]
    return pl.pallas_call(
        functools.partial(middle_kernel, len(projs), col),
        grid=(units // FF_STEP,),
        in_specs=[SMEM, SMEM] + [ANY] * (3 * len(projs)) + [vm] * 5,
        out_specs=[vm] * 3,
        out_shape=[
            jax.ShapeDtypeStruct((size, width), BF),
            jax.ShapeDtypeStruct((size, width), F32),
            jax.ShapeDtypeStruct((size, width), BF),
        ],
        scratch_shapes=[
            pltpu.VMEM((width, width), BF),
            pltpu.VMEM((2, width, FF_STEP), BF),
            pltpu.VMEM((2, FF_STEP, width), BF),
            pltpu.VMEM((size, width), F32),
            pltpu.VMEM((size, width), BF),
            pltpu.VMEM((size, width), BF),
            pltpu.VMEM((size, width), F32),
            pltpu.VMEM((size, width), F32),
            pltpu.SemaphoreType.DMA((1,)),
            pltpu.SemaphoreType.DMA((2,)),
        ],
        compiler_params=params(),
        cost_estimate=pl.CostEstimate(
            flops=8 * size * width * units + 4 * size * width * width,
            bytes_accessed=32 * 2**20,
            transcendentals=size * units,
        ),
        name="middle",
    )(lengths, index, *projs, *fcs, *outs, att, x, cot, gain, shift)


def backward_kernel(
    len_ref, qx_ref, k_ref, v_ref, o_ref, g_ref, dq_ref, dk_ref, dv_ref, kx, vx, gx, dqa
):
    size = k_ref.shape[0]
    ln = lane((size, PAIR))
    first = ln < HD
    bias = jnp.where(row((size, PAIR)) < len_ref[0], 0.0, NEG).astype(BF)
    kp = k_ref[...]
    vp = v_ref[...]
    g = g_ref[...]
    zero = jnp.zeros((size, PAIR), BF)
    one = jnp.ones((size, PAIR), BF)
    prod = g.astype(F32) * o_ref[...].astype(F32)
    for h in range(2):
        other = HD * (1 - h)
        mine = first if h == 0 else ~first
        extra = (ln > other) & (ln <= other + 3)
        kx[h] = jnp.where(mine, kp, jnp.where(ln == other, bias, jnp.where(extra, one, zero)))
        vx[h] = jnp.where(mine, vp, jnp.where(extra, one, zero))
        dots = jnp.sum(jnp.where(mine, prod, 0.0), axis=-1, keepdims=True)
        a, b, c = split3(jnp.broadcast_to(-dots, (size, PAIR)))
        gx[h] = jnp.where(
            mine,
            g,
            jnp.where(
                ln == other + 1,
                a,
                jnp.where(ln == other + 2, b, jnp.where(ln == other + 3, c, zero)),
            ),
        )
    qp = jnp.where(first, qx_ref[:, :PAIR], qx_ref[:, PAIR:])
    blocks = size // BLOCK
    for kb in range(blocks):
        keys = slice(kb * BLOCK, (kb + 1) * BLOCK)
        dvs = []
        dks = []
        for h in range(2):
            dv = dk = None
            for qb in range(kb, blocks):
                queries = slice(qb * BLOCK, (qb + 1) * BLOCK)
                st = dot_nt(kx[h, keys, :], qx_ref[queries, h * PAIR : (h + 1) * PAIR])
                if qb == kb:
                    st = jnp.where(row((BLOCK, BLOCK)) <= lane((BLOCK, BLOCK)), st, NEG)
                p = jnp.exp(st)
                dp = dot_nt(vx[h, keys, :], gx[h, queries, :])
                ds = (p * dp).astype(BF)
                a = dot(p.astype(BF), g[queries])
                b = dot(ds, qp[queries])
                c = dot_tn(ds, kp[keys])
                dv = a if dv is None else dv + a
                dk = b if dk is None else dk + b
                if kb == 0:
                    dqa[h, queries, :] = c
                else:
                    dqa[h, queries, :] += c
            dvs.append(dv)
            dks.append(dk)
        f = lane((BLOCK, PAIR)) < HD
        dv_ref[keys, :] = jnp.where(f, dvs[0], dvs[1]).astype(BF)
        dk_ref[keys, :] = jnp.where(f, dks[0], dks[1]).astype(BF)
    dq_ref[...] = (jnp.where(first, dqa[0], dqa[1]) * (1.0 / HD**0.5)).astype(BF)


def attention_backward(lengths, qx, k, v, o, ga):
    size, group = k.shape
    pair = pl.BlockSpec((size, PAIR), lambda p: (0, p))
    return pl.pallas_call(
        backward_kernel,
        grid=(group // PAIR,),
        in_specs=[
            SMEM,
            pl.BlockSpec((size, 2 * PAIR), lambda p: (0, p)),
            pair, pair, pair, pair,
        ],
        out_specs=[pair] * 3,
        out_shape=[jax.ShapeDtypeStruct((size, group), BF)] * 3,
        scratch_shapes=[pltpu.VMEM((2, size, PAIR), BF)] * 3 + [pltpu.VMEM((2, size, PAIR), F32)],
        compiler_params=params(),
        name="attention_backward",
    )(lengths, qx, k, v, o, ga)


def adapter_kernel(dq_ref, dv_ref, n_ref, narrow_ref, upq_ref, upv_ref, joint_ref, sums_ref):
    narrow = narrow_ref[...]
    dq = dq_ref[...]
    dv = dv_ref[...]
    joint = (SCALE * (dot_nt(dq, upq_ref[...]) + dot_nt(dv, upv_ref[...]))).astype(BF)
    joint_ref[...] = joint
    gq = SCALE * dot_tn(narrow, dq)[:8]
    gv = SCALE * dot_tn(narrow, dv)[:8]
    sums_ref[0:8, :] = dot_tn(joint, n_ref[...])[:8]
    sums_ref[8:16, :] = jnp.where(row(gq.shape) < 4, gq, gv)


def adapter_sums(dq, dv, n, narrow, upq, upv):
    size, width = n.shape
    return pl.pallas_call(
        adapter_kernel,
        out_shape=[
            jax.ShapeDtypeStruct((size, PAD), BF),
            jax.ShapeDtypeStruct((16, width), F32),
        ],
        compiler_params=params(),
        name="adapter_sums",
    )(dq, dv, n, narrow, upq, upv)


def token_copies(index_ref, shards, wbuf, sem, part, slot, group):
    rows = shards[0].shape[0]
    copies = []
    for i, ref in enumerate(shards):
        at = pl.multiple_of(index_ref[i] * rows, rows)
        copies.append(
            pltpu.make_async_copy(
                ref.at[:, part * group : (part + 1) * group],
                wbuf.at[slot, pl.ds(at, rows), :],
                sem.at[slot],
            )
        )
    return copies


def token_kernel(counts, group, index_ref, *refs):
    shards = []
    for count in counts:
        shards.append(refs[:count])
        refs = refs[count:]
    grads, refs = refs[:3], refs[3:]
    joint_ref, down_ref, gh_ref, x_ref, gain_ref, o_ref, wbuf, acc, sem = refs
    size = x_ref.shape[0]
    steps = [(j, p) for j in range(len(counts)) for p in range(3)]

    def copies(s):
        j, p = steps[s]
        return token_copies(index_ref, shards[j], wbuf, sem, p, s % 2, group)

    for c in copies(0):
        c.start()
    for s, (j, p) in enumerate(steps):
        if s + 1 < len(steps):
            for c in copies(s + 1):
                c.start()
        for c in copies(s):
            c.wait()
        for i in range(size // BLOCK):
            at = pl.ds(i * BLOCK, BLOCK)
            part = dot_nt(grads[p][at, j * group : (j + 1) * group], wbuf[s % 2])
            if s == 0:
                part = part + dot(joint_ref[at, :], down_ref[...])
            else:
                part = part + acc[at, :]
            if s + 1 < len(steps):
                acc[at, :] = part
            else:
                xhat, inv = norm_stats(x_ref[at, :].astype(F32))
                o_ref[at, :] = (
                    gh_ref[at, :] + norm_back(xhat, inv, gain_ref[...] * part)
                ).astype(BF)


def token_gradient(index, shards, group, dq, dk, dv, joint, down, gh, x, gain):
    size, width = x.shape
    flat = [s for part in shards for s in part]
    vm = pl.BlockSpec(memory_space=pltpu.VMEM)
    return pl.pallas_call(
        functools.partial(token_kernel, [len(p) for p in shards], group),
        in_specs=[SMEM] + [ANY] * len(flat) + [vm] * 8,
        out_specs=vm,
        out_shape=jax.ShapeDtypeStruct((size, width), BF),
        scratch_shapes=[
            pltpu.VMEM((2, width, group), BF),
            pltpu.VMEM((size, width), F32),
            pltpu.SemaphoreType.DMA((2,)),
        ],
        compiler_params=params(),
        cost_estimate=pl.CostEstimate(
            flops=6 * size * width * width, bytes_accessed=20 * 2**20, transcendentals=0
        ),
        name="token_gradient",
    )(index, *flat, dq, dk, dv, joint, down, gh, x, gain)


BOTH = ("dp", "fsdp")


def swap(value, fn, total):
    return lax.ppermute(value, BOTH, [(i, fn(i)) for i in range(total)])


def cube_gather(w, after, total, fsdp):
    if after is not None:
        w, _ = lax.optimization_barrier((w, after))

    def even(i):
        return (i // fsdp) % 2 == 0

    a = swap(w, lambda i: i ^ (2 if even(i) else 4), total)
    b = swap(a, lambda i: i ^ (4 if even(i) else 2), total)
    c = swap(a, lambda i: i ^ fsdp, total)
    pairs = []
    for part in (w, a, b, c):
        pairs += [part, swap(part, lambda i: i ^ 1, total)]
    return pairs, a


def all_sum(value, total):
    if total & (total - 1):
        return lax.psum(value, BOTH)
    half = value.shape[0] // 2
    odd = lax.axis_index("fsdp") % 2
    mine = lax.dynamic_slice_in_dim(value, odd * half, half)
    other = lax.dynamic_slice_in_dim(value, (1 - odd) * half, half)
    mine = mine + swap(other, lambda i: i ^ 1, total)
    bit = 2
    while bit < total:
        mine = mine + swap(mine, lambda i, bit=bit: i ^ bit, total)
        bit *= 2
    other = swap(mine, lambda i: i ^ 1, total)
    top = jnp.where(odd == 0, mine, other)
    low = jnp.where(odd == 0, other, mine)
    return jnp.concatenate([top, low], axis=0)


def local(
    sizes, tokens, lengths, cotangent, gain_one, shift_one, gain_two, shift_two,
    w_qkv, w_proj, w_fc, w_out,
    query_down_factor, query_up_factor, value_down_factor, value_up_factor,
):
    _, size, width = tokens.shape
    dp, fsdp = sizes
    total = dp * fsdp
    x = tokens.reshape(size, width)
    cot = cotangent.reshape(size, width)
    group = width // 2
    cols = [jnp.concatenate([w_qkv[:, p * width + j * group : p * width + (j + 1) * group]
                             for p in range(3)] + ([w_proj] if j else []), axis=1)
            for j in range(2)]
    if fsdp == 8 and dp % 2 == 0:
        here = lax.axis_index("fsdp").astype(jnp.int32)
        odd = lax.axis_index("dp").astype(jnp.int32) % 2
        a, c = 2 + 2 * odd, 4 - 2 * odd
        index = jnp.stack([here ^ (m ^ s) for m in (0, a, 6, c) for s in (0, 1)])
        first, sent = cube_gather(cols[0], None, total, fsdp)
        second, sent = cube_gather(cols[1], sent, total, fsdp)
        fcs, sent = cube_gather(w_fc, sent, total, fsdp)
        outs, sent = cube_gather(w_out, sent, total, fsdp)
    else:
        index = jnp.zeros((1,), jnp.int32)
        first, second, fcs, outs = [
            [lax.all_gather(w, "fsdp", axis=0, tiled=True)] for w in cols + [w_fc, w_out]
        ]

    n, narrow, down, upq, upv = norm_one(
        x, gain_one[None], shift_one[None],
        query_down_factor.T, value_down_factor.T, query_up_factor, value_up_factor,
    )
    kept = []
    for j, shards in enumerate((first, second)):
        for quad in range(group // QUAD):
            kept = attention_forward(
                lengths, index, shards, n, narrow, upq, upv, quad, group, j * group, kept
            )
    o, qx, k, v = kept
    block_out, gh, ga = middle(
        lengths, index, second, 3 * group, fcs, outs, o, x, cot, gain_two[None], shift_two[None]
    )
    dq, dk, dv = attention_backward(lengths, qx, k, v, o, ga)
    joint, sums = adapter_sums(dq, dv, n, narrow, upq, upv)
    sums = all_sum(sums, total)
    grad = token_gradient(
        index, [first, second], group, dq, dk, dv, joint, down, gh, x, gain_one[None]
    )
    return (
        block_out.reshape(tokens.shape),
        grad.reshape(tokens.shape),
        sums[0:4].T,
        sums[8:12],
        sums[4:8].T,
        sums[12:16],
    )


def solution(mesh):
    rows = P(BOTH, None, None)
    frozen = P("fsdp", None)
    return jax.shard_map(
        functools.partial(local, (mesh.shape["dp"], mesh.shape["fsdp"])),
        mesh=mesh,
        in_specs=(rows, P(BOTH), rows, P(), P(), P(), P()) + (frozen,) * 4 + (P(),) * 4,
        out_specs=(rows, rows, P(), P(), P(), P()),
        check_vma=False,
    )
```

```python
import functools

import jax
import jax.numpy as jnp
from jax import lax
from jax.experimental import pallas as pl
from jax.experimental.pallas import tpu as pltpu
from jax.sharding import PartitionSpec as P

BF = jnp.bfloat16
F32 = jnp.float32
HD = 64
PAIR = 2 * HD
PAD = 16
SCALE = 8.0
EPS = 1e-05
NEG = -1e30
BLOCK = 256
FF_STEP = 1024
ROWS = 512
VMEM_LIMIT = 58 * 2**20
GELU_C = 0.7978845608028654
GELU_A = 0.044715
ANY = pl.BlockSpec(memory_space=pl.ANY)
SMEM = pl.BlockSpec(memory_space=pltpu.SMEM)
CHEAP = pl.CostEstimate(flops=1000, bytes_accessed=1000, transcendentals=0)


def dot(a, b):
    return lax.dot_general(a, b, (((1,), (0,)), ((), ())), preferred_element_type=F32)


def dot_nt(a, b):
    return lax.dot_general(a, b, (((1,), (1,)), ((), ())), preferred_element_type=F32)


def dot_tn(a, b):
    return lax.dot_general(a, b, (((0,), (0,)), ((), ())), preferred_element_type=F32)


def lane(shape):
    return lax.broadcasted_iota(jnp.int32, shape, 1)


def row(shape):
    return lax.broadcasted_iota(jnp.int32, shape, 0)


def split3(x):
    a = x.astype(BF)
    r = x - a.astype(F32)
    b = r.astype(BF)
    c = (r - b.astype(F32)).astype(BF)
    return a, b, c


def whole(shape):
    return pl.BlockSpec(shape, lambda *_: (0,) * len(shape))


def params(**kw):
    return pltpu.CompilerParams(vmem_limit_bytes=VMEM_LIMIT, **kw)


def norm_stats(x):
    mean = jnp.mean(x, axis=-1, keepdims=True)
    center = x - mean
    inv = lax.rsqrt(jnp.mean(center * center, axis=-1, keepdims=True) + EPS)
    return center * inv, inv


def norm_back(xhat, inv, g):
    return inv * (
        g
        - jnp.mean(g, axis=-1, keepdims=True)
        - xhat * jnp.mean(g * xhat, axis=-1, keepdims=True)
    )


def pad_rows(parts, width):
    have = sum(p.shape[0] for p in parts)
    return jnp.concatenate(parts + [jnp.zeros((PAD - have, width), F32)], axis=0).astype(BF)


def norm_one_kernel(
    x_ref, gain_ref, shift_ref, dq_ref, dv_ref, uq_ref, uv_ref,
    n_ref, narrow_ref, down_ref, upq_ref, upv_ref,
):
    width = x_ref.shape[1]
    rank = dq_ref.shape[0]

    @pl.when(pl.program_id(0) == 0)
    def _():
        blank = jnp.zeros((rank, width), F32)
        down_ref[...] = pad_rows([dq_ref[...], dv_ref[...]], width)
        upq_ref[...] = pad_rows([uq_ref[...]], width)
        upv_ref[...] = pad_rows([blank, uv_ref[...]], width)

    xhat, _ = norm_stats(x_ref[...].astype(F32))
    low = (xhat * gain_ref[...] + shift_ref[...]).astype(BF)
    n_ref[...] = low
    narrow_ref[...] = dot_nt(down_ref[...], low).astype(BF)


def norm_one(x, gain, shift, dq, dv, uq, uv):
    length, width = x.shape
    small = whole((1, width))
    adapter = whole(dq.shape)
    padded = whole((PAD, width))
    return pl.pallas_call(
        norm_one_kernel,
        grid=(length // BLOCK,),
        in_specs=[pl.BlockSpec((BLOCK, width), lambda i: (i, 0)), small, small] + [adapter] * 4,
        out_specs=[
            pl.BlockSpec((BLOCK, width), lambda i: (i, 0)),
            pl.BlockSpec((PAD, BLOCK), lambda i: (0, i)),
            padded, padded, padded,
        ],
        out_shape=[
            jax.ShapeDtypeStruct((length, width), BF),
            jax.ShapeDtypeStruct((PAD, length), BF),
        ]
        + [jax.ShapeDtypeStruct((PAD, width), BF)] * 3,
        compiler_params=params(),
        name="norm_one",
    )(x, gain, shift, dq, dv, uq, uv)


def repack_kernel(quads, half, qkv_ref, proj_ref, a_ref, b_ref):
    width = proj_ref.shape[1]
    for q in range(quads):
        ref, place = (a_ref, q) if q < half else (b_ref, q - half)
        for p in range(3):
            at = (3 * place + p) * QUAD
            ref[:, at : at + QUAD] = qkv_ref[:, p * width + q * QUAD : p * width + (q + 1) * QUAD]
    at = 3 * (quads - half) * QUAD
    b_ref[:, at : at + width] = proj_ref[...]


def repack(w_qkv, w_proj, half):
    rows, width = w_proj.shape
    quads = width // QUAD
    return pl.pallas_call(
        functools.partial(repack_kernel, quads, half),
        out_shape=[
            jax.ShapeDtypeStruct((rows, 3 * half * QUAD), BF),
            jax.ShapeDtypeStruct((rows, 3 * (quads - half) * QUAD + width), BF),
        ],
        compiler_params=params(),
        name="repack",
    )(w_qkv, w_proj)


QUAD = 2 * PAIR


def causal_below(x):
    size, wide = x.shape
    near = jnp.where(row((size, size)) <= lane((size, size)), x[:, :size], NEG)
    return near if wide == size else jnp.concatenate([near, x[:, size:]], axis=1)


def attend(length, pairs, o_ref, qx_ref, kx, vt, qt, ot):
    size = pairs[0][0].shape[0]
    ln = lane((size, PAIR))
    first = ln < HD
    bias = jnp.where(row((size, PAIR)) < length, 0.0, NEG).astype(BF)
    zero = jnp.zeros((size, PAIR), BF)
    ones = jnp.ones((16, size), BF)
    extra = jnp.where(row((HD, size)) == 0, 1.0, 0.0).astype(BF)

    def prepare(p):
        q, k, v = pairs[p]
        kx[2 * p] = jnp.where(first, k, jnp.where(ln == HD, bias, zero))
        kx[2 * p + 1] = jnp.where(first, jnp.where(ln == 0, bias, zero), k)
        v_t = v.T
        q_t = q.T
        for h in range(2):
            mine = slice(h * HD, (h + 1) * HD)
            vt[2 * p + h, :HD, :] = v_t[mine]
            vt[2 * p + h, HD:, :] = ones
            parts = [q_t[mine], extra] if h == 0 else [extra, q_t[mine]]
            qt[2 * p + h] = jnp.concatenate(parts, axis=0)

    def scores(t):
        return [
            (b, causal_below(dot(kx[t, b : b + BLOCK, :], qt[t, :, b:])))
            for b in range(0, size, BLOCK)
        ]

    def finish(t, parts):
        top = None
        for b, s in parts:
            high = jnp.max(s, axis=0, keepdims=True)
            if b == 0:
                top = high
            else:
                top = jnp.concatenate([top[:, :b], jnp.maximum(top[:, b:], high)], axis=1)
        acc = None
        for b, s in parts:
            p = jnp.exp(s - top[:, b:]).astype(BF)
            a = dot(vt[t, :, b : b + BLOCK], p)
            acc = a if b == 0 else jnp.concatenate([acc[:, :b], acc[:, b:] + a], axis=1)
        total = acc[HD : HD + 1]
        ot[t * HD : (t + 1) * HD, :] = acc[:HD] * (1.0 / total)
        a, b, c = split3(-(top + jnp.log(total)))
        r = row((HD, size))
        more = jnp.where(
            r == 0,
            1.0,
            jnp.where(
                r == 1,
                a.astype(F32),
                jnp.where(r == 2, b.astype(F32), jnp.where(r == 3, c.astype(F32), 0.0)),
            ),
        ).astype(BF)
        at = t * PAIR
        h = t % 2
        qx_ref[at + h * HD : at + (h + 1) * HD, :] = qt[t, h * HD : (h + 1) * HD, :]
        qx_ref[at + (1 - h) * HD : at + (2 - h) * HD, :] = more

    count = 2 * len(pairs)
    prepare(0)
    later = scores(0)
    for t in range(count):
        now = later
        if t + 1 < count:
            if t % 2:
                prepare((t + 1) // 2)
            later = scores(t + 1)
        finish(t, now)
    o_ref[...] = ot[...].T.astype(BF)


def qkv_copies(index_ref, shards, wbuf, sem, quad):
    rows = shards[0].shape[0]
    wide = wbuf.shape[1]
    copies = []
    for i, ref in enumerate(shards):
        at = pl.multiple_of(index_ref[i] * rows, rows)
        src = ref.at[:, quad * wide : (quad + 1) * wide]
        copies.append(pltpu.make_async_copy(src, wbuf.at[pl.ds(at, rows), :], sem))
    return copies


def forward_kernel(count, kept, quads, len_ref, index_ref, *refs):
    shards, refs = refs[:count], refs[count + kept :]
    (n_ref, narrow_ref, upq_ref, upv_ref, o_ref, qx_ref, q_ref, k_ref, v_ref,
     wbuf, kx, vt, qt, ot, sem) = refs
    step = pl.program_id(0)

    def copies(i):
        return qkv_copies(index_ref, shards, wbuf.at[i], sem.at[i], quads[i])

    @pl.when(step == 0)
    def _():
        for i in range(len(quads)):
            for c in copies(i):
                c.start()

    for i in range(len(quads)):

        @pl.when(step == i)
        def _(i=i):
            for c in copies(i):
                c.wait()

    n = n_ref[...]
    narrow = narrow_ref[...]
    w = wbuf.at[step]
    q = dot(n, w[:, :QUAD]) + SCALE * dot_tn(narrow, upq_ref[...])
    k = dot(n, w[:, QUAD : 2 * QUAD])
    v = dot(n, w[:, 2 * QUAD :]) + SCALE * dot_tn(narrow, upv_ref[...])
    q_ref[...] = (q.astype(BF).astype(F32) * (1.0 / HD**0.5)).astype(BF)
    k_ref[...] = k.astype(BF)
    v_ref[...] = v.astype(BF)
    cols = [slice(p * PAIR, (p + 1) * PAIR) for p in range(QUAD // PAIR)]
    pairs = [(q_ref[:, c], k_ref[:, c], v_ref[:, c]) for c in cols]
    attend(len_ref[0], pairs, o_ref, qx_ref, kx, vt, qt, ot)


def attention_forward(lengths, index, shards, n, narrow, upq, upv, quads, here, kept):
    length, width = n.shape
    block = pl.BlockSpec((length, QUAD), lambda s: (0, here + s))
    up = pl.BlockSpec((PAD, QUAD), lambda s: (0, here + s))
    first = 2 + len(shards)
    heads = QUAD // HD
    return pl.pallas_call(
        functools.partial(forward_kernel, len(shards), len(kept), quads),
        grid=(len(quads),),
        in_specs=[SMEM, SMEM]
        + [ANY] * (len(shards) + len(kept))
        + [whole((length, width)), whole((PAD, length)), up, up],
        out_specs=[block, pl.BlockSpec((2 * QUAD, length), lambda s: (here + s, 0))] + [block] * 3,
        out_shape=[
            jax.ShapeDtypeStruct((length, width), BF),
            jax.ShapeDtypeStruct((2 * width, length), BF),
        ]
        + [jax.ShapeDtypeStruct((length, width), BF)] * 3,
        input_output_aliases={first + i: i for i in range(len(kept))},
        scratch_shapes=[
            pltpu.VMEM((len(quads), width, 3 * QUAD), BF),
            pltpu.VMEM((heads, length, PAIR), BF),
            pltpu.VMEM((heads, HD + 16, length), BF),
            pltpu.VMEM((heads, PAIR, length), BF),
            pltpu.VMEM((QUAD, length), F32),
            pltpu.SemaphoreType.DMA((len(quads),)),
        ],
        compiler_params=params(),
        cost_estimate=CHEAP,
        name="attention_forward",
    )(lengths, index, *shards, *kept, n, narrow, upq, upv)


def rows_copies(index_ref, shards, col, wide, wbuf, sem):
    rows = shards[0].shape[0]
    copies = []
    for i, ref in enumerate(shards):
        at = pl.multiple_of(index_ref[i] * rows, rows)
        src = ref.at[:, pl.ds(col, wide)]
        copies.append(pltpu.make_async_copy(src, wbuf.at[pl.ds(at, rows), :], sem))
    return copies


def out_slice(index_ref, outs, step):
    rows = outs[0].shape[0]
    if rows >= FF_STEP:
        shard, part = divmod(step, rows // FF_STEP)
        begin = index_ref[shard] * rows + part * FF_STEP
        return pl.multiple_of(begin, FF_STEP), [(outs[shard], part * FF_STEP, 0, FF_STEP)]
    each = FF_STEP // rows
    begin = index_ref[step * each] * rows // FF_STEP * FF_STEP
    begin = pl.multiple_of(begin, FF_STEP)
    pieces = [
        (outs[i], 0, pl.multiple_of(index_ref[i] * rows - begin, rows), rows)
        for i in range(step * each, (step + 1) * each)
    ]
    return begin, pieces


def gelu_both(v):
    square = v * v
    t = jnp.tanh(v * (GELU_C + (GELU_C * GELU_A) * square))
    half = 0.5 * t + 0.5
    act = v * half
    slope = half + act * (1.0 - half) * (2.0 * GELU_C + (6.0 * GELU_C * GELU_A) * square)
    return act, slope


def blocks_of(size, rows):
    return [pl.ds(i * rows, rows) for i in range(size // rows)]


def rise_kernel(count, col, index_ref, *refs):
    projs, refs = refs[:count], refs[count:]
    fcs, refs = refs[:count], refs[count:]
    (o_ref, x_ref, gain_ref, shift_ref, pre_ref, hidden_ref,
     wproj, fbuf, obuf, xbuf, hidden, n2, psem, fsem, osem, hsem) = refs
    step = pl.program_id(0)
    steps = pl.num_programs(0)
    size, width = xbuf.shape
    slot = lax.rem(step, 2)
    places = blocks_of(size, BLOCK)

    def fc_copies(s, slot):
        col = pl.multiple_of(s * FF_STEP, FF_STEP)
        return rows_copies(index_ref, fcs, col, FF_STEP, fbuf.at[slot], fsem.at[slot])

    def row_copies(i):
        at = places[i]
        return [
            pltpu.make_async_copy(o_ref.at[at, :], obuf.at[at, :], osem.at[i]),
            pltpu.make_async_copy(x_ref.at[at, :], xbuf.at[at, :], osem.at[i]),
        ]

    def hidden_copy(i):
        at = places[i]
        return pltpu.make_async_copy(hidden.at[at, :], hidden_ref.at[at, :], hsem)

    @pl.when(step == 0)
    def _():
        first = rows_copies(index_ref, projs, col, width, wproj, psem)
        for c in first:
            c.start()
        for i in range(len(places)):
            for c in row_copies(i):
                c.start()
        for c in fc_copies(0, 0):
            c.start()
        for c in first:
            c.wait()
        for i, at in enumerate(places):
            for c in row_copies(i):
                c.wait()
            hidden[at, :] = xbuf[at, :].astype(F32) + dot(obuf[at, :], wproj[...])
            hidden_copy(i).start()
        for at in places:
            xhat, _ = norm_stats(hidden[at, :])
            n2[at, :] = (xhat * gain_ref[...] + shift_ref[...]).astype(BF)

    @pl.when(step + 1 < steps)
    def _():
        for c in fc_copies(step + 1, 1 - slot):
            c.start()

    for c in fc_copies(step, slot):
        c.wait()
    for at in blocks_of(size, ROWS):
        pre_ref[at, :] = dot(n2[at, :], fbuf[slot])

    @pl.when(step == steps - 1)
    def _():
        for i in range(len(places)):
            hidden_copy(i).wait()


def rise(index, projs, col, fcs, o, x, gain, shift):
    size, width = x.shape
    units = fcs[0].shape[1]
    small = whole((1, width))
    return pl.pallas_call(
        functools.partial(rise_kernel, len(projs), col),
        grid=(units // FF_STEP,),
        in_specs=[SMEM] + [ANY] * (2 * len(projs) + 2) + [small, small],
        out_specs=[pl.BlockSpec((size, FF_STEP), lambda s: (0, s)), ANY],
        out_shape=[
            jax.ShapeDtypeStruct((size, units), F32),
            jax.ShapeDtypeStruct((size, width), F32),
        ],
        scratch_shapes=[
            pltpu.VMEM((width, width), BF),
            pltpu.VMEM((2, width, FF_STEP), BF),
            pltpu.VMEM((size, width), BF),
            pltpu.VMEM((size, width), BF),
            pltpu.VMEM((size, width), F32),
            pltpu.VMEM((size, width), BF),
            pltpu.SemaphoreType.DMA,
            pltpu.SemaphoreType.DMA((2,)),
            pltpu.SemaphoreType.DMA((size // BLOCK,)),
            pltpu.SemaphoreType.DMA,
        ],
        compiler_params=params(),
        cost_estimate=CHEAP,
        name="rise",
    )(index, *projs, *fcs, o, x, gain, shift)


def fall_kernel(count, col, steps, len_ref, index_ref, *refs):
    projs, refs = refs[:count], refs[count:]
    fcs, refs = refs[:count], refs[count:]
    outs, refs = refs[:count], refs[count:]
    (pre_ref, hidden_ref, cot_ref, gain_ref, block_ref, gh_ref, ga_ref,
     wproj, fbuf, obuf, pbuf, hidden, cbuf, low, acc, back, block, gatt, sem, lsem, wsem) = refs
    step = pl.program_id(0)
    size, width = low.shape
    slot = lax.rem(step, 2)

    def copies(s):
        begin, pieces = out_slice(index_ref, outs, s)
        slot = s % 2
        found = []
        for ref, at, to, rows in pieces:
            found.append(
                pltpu.make_async_copy(
                    ref.at[at : at + rows, :], obuf.at[slot, pl.ds(to, rows), :], sem.at[slot]
                )
            )
        src = pre_ref.at[:, pl.ds(begin, FF_STEP)]
        found.append(pltpu.make_async_copy(src, pbuf.at[slot], sem.at[slot]))
        return found + rows_copies(index_ref, fcs, begin, FF_STEP, fbuf.at[slot], sem.at[slot])

    late = [pltpu.make_async_copy(hidden_ref, hidden, lsem.at[1])]
    late += rows_copies(index_ref, projs, col, width, wproj, lsem.at[1])
    first = pltpu.make_async_copy(cot_ref, cbuf, lsem.at[0])

    @pl.when(step == 0)
    def _():
        first.start()
        for c in copies(0):
            c.start()
        for c in copies(1):
            c.start()
        for c in late:
            c.start()
        first.wait()
        for i, at in enumerate(blocks_of(size, BLOCK)):
            keep = row((BLOCK, 1)) + i * BLOCK < len_ref[0]
            low[at, :] = jnp.where(keep, cbuf[at, :].astype(F32), 0.0).astype(BF)

    for s in range(2, steps):

        @pl.when(step + 1 == s)
        def _(s=s):
            for c in copies(s):
                c.start()

    for even in range(2):

        @pl.when(slot == even)
        def _(even=even):
            for c in copies(even):
                c.wait()

    def body(begin):
        for at in blocks_of(size, ROWS):
            act, slope = gelu_both(pbuf[slot, at, :])
            mlp = dot(act.astype(BF), obuf[slot])
            grad = (dot_nt(low[at, :], obuf[slot]) * slope).astype(BF)
            u = dot_nt(grad, fbuf[slot])
            if begin:
                acc[at, :] = mlp
                back[at, :] = u
            else:
                acc[at, :] += mlp
                back[at, :] += u

    @pl.when(step == 0)
    def _():
        body(True)

    @pl.when(step > 0)
    def _():
        body(False)

    @pl.when(step == steps - 1)
    def _():
        for c in late:
            c.wait()
        sent = []
        for i, at in enumerate(blocks_of(size, BLOCK)):
            h = hidden[at, :]
            keep = row((BLOCK, 1)) + i * BLOCK < len_ref[0]
            block[at, :] = jnp.where(keep, h + acc[at, :], 0.0).astype(BF)
            xhat, inv = norm_stats(h)
            gh = low[at, :].astype(F32) + norm_back(xhat, inv, gain_ref[...] * back[at, :])
            hidden[at, :] = gh
            gatt[at, :] = dot_nt(gh.astype(BF), wproj[...]).astype(BF)
            here = [
                pltpu.make_async_copy(block.at[at, :], block_ref.at[at, :], wsem),
                pltpu.make_async_copy(hidden.at[at, :], gh_ref.at[at, :], wsem),
                pltpu.make_async_copy(gatt.at[at, :], ga_ref.at[at, :], wsem),
            ]
            for c in here:
                c.start()
            sent += here
        for c in sent:
            c.wait()


def fall(lengths, index, projs, col, fcs, outs, pre, hidden, cot, gain):
    size, width = cot.shape
    units = pre.shape[1]
    steps = units // FF_STEP
    return pl.pallas_call(
        functools.partial(fall_kernel, len(projs), col, steps),
        grid=(steps,),
        in_specs=[SMEM, SMEM] + [ANY] * (3 * len(projs) + 3) + [whole((1, width))],
        out_specs=[ANY] * 3,
        out_shape=[
            jax.ShapeDtypeStruct((size, width), BF),
            jax.ShapeDtypeStruct((size, width), F32),
            jax.ShapeDtypeStruct((size, width), BF),
        ],
        scratch_shapes=[
            pltpu.VMEM((width, width), BF),
            pltpu.VMEM((2, width, FF_STEP), BF),
            pltpu.VMEM((2, FF_STEP, width), BF),
            pltpu.VMEM((2, size, FF_STEP), F32),
            pltpu.VMEM((size, width), F32),
            pltpu.VMEM((size, width), BF),
            pltpu.VMEM((size, width), BF),
            pltpu.VMEM((size, width), F32),
            pltpu.VMEM((size, width), F32),
            pltpu.VMEM((size, width), BF),
            pltpu.VMEM((size, width), BF),
            pltpu.SemaphoreType.DMA((2,)),
            pltpu.SemaphoreType.DMA((2,)),
            pltpu.SemaphoreType.DMA,
        ],
        compiler_params=params(),
        cost_estimate=CHEAP,
        name="fall",
    )(lengths, index, *projs, *fcs, *outs, pre, hidden, cot, gain)


def backward_kernel(
    len_ref, qx_ref, q_ref, k_ref, v_ref, o_ref, g_ref, upq_ref, upv_ref, narrow_ref, n_ref,
    dq_ref, dk_ref, dv_ref, joint_ref, sums_ref, kx, vx, gx, kt, dqt, total,
):
    size = k_ref.shape[0]
    step = pl.program_id(0)
    ln = lane((size, PAIR))
    first = ln < HD
    bias = jnp.where(row((size, PAIR)) < len_ref[0], 0.0, NEG).astype(BF)
    kp = k_ref[...]
    vp = v_ref[...]
    g = g_ref[...]
    qp = q_ref[...]
    zero = jnp.zeros((size, PAIR), BF)
    one = jnp.ones((size, PAIR), BF)
    prod = g.astype(F32) * o_ref[...].astype(F32)
    for h in range(2):
        other = HD * (1 - h)
        mine = first if h == 0 else ~first
        extra = (ln > other) & (ln <= other + 3)
        kx[h] = jnp.where(mine, kp, jnp.where(ln == other, bias, jnp.where(extra, one, zero)))
        vx[h] = jnp.where(mine, vp, jnp.where(extra, one, zero))
        dots = jnp.sum(jnp.where(mine, prod, 0.0), axis=-1, keepdims=True)
        a, b, c = split3(jnp.broadcast_to(-dots, (size, PAIR)))
        gx[h] = jnp.where(
            mine,
            g,
            jnp.where(
                ln == other + 1,
                a,
                jnp.where(ln == other + 2, b, jnp.where(ln == other + 3, c, zero)),
            ),
        )
    kt[...] = kp.T

    def products(b, h):
        st = dot(kx[h, b : b + BLOCK, :], qx_ref[h * PAIR : (h + 1) * PAIR, b:])
        return st, dot_nt(vx[h, b : b + BLOCK, :], gx[h, b:, :])

    held = {}

    def finish(b, h, st, dp):
        p = jnp.exp(causal_below(st))
        ds = (p * dp).astype(BF)
        mine = slice(h * HD, (h + 1) * HD)
        c = dot(kt[mine, b : b + BLOCK], ds)
        if b == 0:
            dqt[mine, :] = c
        else:
            dqt[mine, b:] += c
        held[h] = (dot(p.astype(BF), g[b:]), dot(ds, qp[b:]))
        if h == 1:
            f = lane((BLOCK, PAIR)) < HD
            dv_ref[b : b + BLOCK, :] = jnp.where(f, held[0][0], held[1][0]).astype(BF)
            dk_ref[b : b + BLOCK, :] = jnp.where(f, held[0][1], held[1][1]).astype(BF)

    tasks = [(b, h) for b in range(0, size, BLOCK) for h in range(2)]
    later = products(*tasks[0])
    for j, t in enumerate(tasks):
        now = later
        if j + 1 < len(tasks):
            later = products(*tasks[j + 1])
        finish(*t, *now)
    dq = (dqt[...] * (1.0 / HD**0.5)).T.astype(BF)
    dq_ref[...] = dq
    dv = dv_ref[...]
    narrow = narrow_ref[...]
    part = dot_nt(upq_ref[...], dq) + dot_nt(upv_ref[...], dv)
    gq = SCALE * dot(narrow, dq)[:8]
    gv = SCALE * dot(narrow, dv)[:8]
    cols = pl.ds(pl.multiple_of(step * PAIR, PAIR), PAIR)
    sums_ref[8:16, cols] = jnp.where(row((8, PAIR)) < 4, gq, gv)

    @pl.when(step == 0)
    def _():
        total[...] = part

    @pl.when(step > 0)
    def _():
        total[...] += part

    @pl.when(step == pl.num_programs(0) - 1)
    def _():
        joint = (SCALE * total[...]).astype(BF)
        joint_ref[...] = joint
        sums_ref[0:8, :] = dot(joint, n_ref[...])[:8]


def attention_backward(lengths, qx, q, k, v, o, ga, upq, upv, narrow, n):
    size, width = k.shape
    pair = pl.BlockSpec((size, PAIR), lambda p: (0, p))
    up = pl.BlockSpec((PAD, PAIR), lambda p: (0, p))
    return pl.pallas_call(
        backward_kernel,
        grid=(width // PAIR,),
        in_specs=[SMEM, pl.BlockSpec((2 * PAIR, size), lambda p: (p, 0))]
        + [pair] * 5
        + [up, up, whole((PAD, size)), whole((size, width))],
        out_specs=[pair] * 3 + [whole((PAD, size)), whole((16, width))],
        out_shape=[jax.ShapeDtypeStruct((size, width), BF)] * 3
        + [jax.ShapeDtypeStruct((PAD, size), BF), jax.ShapeDtypeStruct((16, width), F32)],
        scratch_shapes=[pltpu.VMEM((2, size, PAIR), BF)] * 3
        + [
            pltpu.VMEM((PAIR, size), BF),
            pltpu.VMEM((PAIR, size), F32),
            pltpu.VMEM((PAD, size), F32),
        ],
        compiler_params=params(),
        cost_estimate=CHEAP,
        name="attention_backward",
    )(lengths, qx, q, k, v, o, ga, upq, upv, narrow, n)


def token_kernel(counts, quads, index_ref, *refs):
    shards = []
    for count in counts:
        shards.append(refs[:count])
        refs = refs[count:]
    (dq_ref, dk_ref, dv_ref, joint_ref, down_ref, gh_ref, x_ref, gain_ref, o_ref, wbuf, sem) = refs
    step = pl.program_id(0)
    pieces = [(j, q) for j in range(len(counts)) for q in range(quads[j])]

    def copies(s):
        j, q = pieces[s]
        return qkv_copies(index_ref, shards[j], wbuf.at[s], sem.at[s], q)

    @pl.when(step == 0)
    def _():
        for s in range(len(pieces)):
            for c in copies(s):
                c.start()

    total = dot_tn(joint_ref[...], down_ref[...])
    for s in range(len(pieces)):

        @pl.when(step == 0)
        def _(s=s):
            for c in copies(s):
                c.wait()

        cols = slice(s * QUAD, (s + 1) * QUAD)
        g = jnp.concatenate([ref[:, cols] for ref in (dq_ref, dk_ref, dv_ref)], axis=1)
        total = total + dot_nt(g, wbuf[s])
    xhat, inv = norm_stats(x_ref[...].astype(F32))
    o_ref[...] = (gh_ref[...] + norm_back(xhat, inv, gain_ref[...] * total)).astype(BF)


def token_gradient(index, shards, quads, dq, dk, dv, joint, down, gh, x, gain):
    size, width = x.shape
    flat = [s for part in shards for s in part]
    block = pl.BlockSpec((BLOCK, width), lambda i: (i, 0))
    return pl.pallas_call(
        functools.partial(token_kernel, [len(p) for p in shards], quads),
        grid=(size // BLOCK,),
        in_specs=[SMEM]
        + [ANY] * len(flat)
        + [block] * 3
        + [pl.BlockSpec((PAD, BLOCK), lambda i: (0, i)), whole((PAD, width))]
        + [block, block, whole((1, width))],
        out_specs=block,
        out_shape=jax.ShapeDtypeStruct((size, width), BF),
        scratch_shapes=[
            pltpu.VMEM((sum(quads), width, 3 * QUAD), BF),
            pltpu.SemaphoreType.DMA((sum(quads),)),
        ],
        compiler_params=params(),
        cost_estimate=CHEAP,
        name="token_gradient",
    )(index, *flat, dq, dk, dv, joint, down, gh, x, gain)


BOTH = ("dp", "fsdp")


def swap(value, fn, total):
    return lax.ppermute(value, BOTH, [(i, fn(i)) for i in range(total)])


def after(value, *others):
    return lax.optimization_barrier((value,) + others)[0]


class Cube:
    def __init__(self, total, fsdp):
        self.total, self.fsdp = total, fsdp

    def even(self, i):
        return (i // self.fsdp) % 2 == 0

    def sibling(self, value):
        return swap(value, lambda i: i ^ 1, self.total)

    def first(self, value):
        return swap(value, lambda i: i ^ (2 if self.even(i) else 4), self.total)

    def second(self, value):
        b = swap(value, lambda i: i ^ (4 if self.even(i) else 2), self.total)
        c = swap(value, lambda i: i ^ self.fsdp, self.total)
        return b, c

    def index(self):
        here = lax.axis_index("fsdp").astype(jnp.int32)
        odd = lax.axis_index("dp").astype(jnp.int32) % 2
        a, c = 2 + 2 * odd, 4 - 2 * odd
        return jnp.stack([here ^ (m ^ s) for m in (0, a, 6, c) for s in (0, 1)])


def all_sum(value, total):
    if total & (total - 1):
        return lax.psum(value, BOTH)
    half = value.shape[0] // 2
    odd = lax.axis_index("fsdp") % 2
    mine = lax.dynamic_slice_in_dim(value, odd * half, half)
    other = lax.dynamic_slice_in_dim(value, (1 - odd) * half, half)
    mine = mine + swap(other, lambda i: i ^ 1, total)
    bit = 2
    while bit < total:
        mine = mine + swap(mine, lambda i, bit=bit: i ^ bit, total)
        bit *= 2
    other = swap(mine, lambda i: i ^ 1, total)
    top = jnp.where(odd == 0, mine, other)
    low = jnp.where(odd == 0, other, mine)
    return jnp.concatenate([top, low], axis=0)


def local(
    sizes, tokens, lengths, cotangent, gain_one, shift_one, gain_two, shift_two,
    w_qkv, w_proj, w_fc, w_out,
    query_down_factor, query_up_factor, value_down_factor, value_up_factor,
):
    _, size, width = tokens.shape
    dp, fsdp = sizes
    total = dp * fsdp
    x = tokens.reshape(size, width)
    cot = cotangent.reshape(size, width)
    quads = width // QUAD
    half = quads // 2
    w0, w1 = repack(w_qkv, w_proj, half)
    small = (
        x, gain_one[None], shift_one[None],
        query_down_factor.T, value_down_factor.T, query_up_factor, value_up_factor,
    )
    low = tuple(range(half))
    col = 3 * (quads - half) * QUAD
    if fsdp == 8 and dp % 2 == 0:
        cube = Cube(total, fsdp)
        index = cube.index()
        a0, a1, af, ao = [cube.first(w) for w in (w0, w1, w_fc, w_out)]
        s0, s1, sf, so = [cube.sibling(w) for w in (w0, w1, w_fc, w_out)]
        n, narrow, down, upq, upv = norm_one(*small)
        attend = functools.partial(
            attention_forward, lengths, index, n=n, narrow=narrow, upq=upq, upv=upv
        )
        a0 = after(a0, n)
        b0, c0 = cube.second(a0)
        first = [w0, s0] + [p for t in (a0, b0, c0) for p in (t, cube.sibling(t))]
        kept = attend(first, quads=low[:1], here=0, kept=[])
        a1 = after(a1, kept[0])
        b1, c1 = cube.second(a1)
        kept = attend(first, quads=low[1:], here=1, kept=kept)
        b1, c1 = after(b1, kept[0]), after(c1, kept[0])
        second = [w1, s1] + [p for t in (a1, b1, c1) for p in (t, cube.sibling(t))]
        af = after(af, kept[0])
        bf, cf = cube.second(af)
        kept = attend(second, quads=low, here=half, kept=kept)
        bf, cf = after(bf, kept[0]), after(cf, kept[0])
        fcs = [w_fc, sf] + [p for t in (af, bf, cf) for p in (t, cube.sibling(t))]
        ao = after(ao, kept[0])
        bo, co = cube.second(ao)
        o, qx, q, k, v = kept
        pre, hidden = rise(index, second, col, fcs, o, x, gain_two[None], shift_two[None])
        bo, co = after(bo, hidden), after(co, hidden)
        outs = [w_out, so] + [p for t in (ao, bo, co) for p in (t, cube.sibling(t))]
    else:
        index = jnp.zeros((1,), jnp.int32)
        first, second, fcs, outs = [
            [lax.all_gather(w, "fsdp", axis=0, tiled=True)] for w in (w0, w1, w_fc, w_out)
        ]
        n, narrow, down, upq, upv = norm_one(*small)
        kept = attention_forward(lengths, index, first, n, narrow, upq, upv, low, 0, [])
        kept = attention_forward(lengths, index, second, n, narrow, upq, upv, low, half, kept)
        o, qx, q, k, v = kept
        pre, hidden = rise(index, second, col, fcs, o, x, gain_two[None], shift_two[None])
    block_out, gh, ga = fall(
        lengths, index, second, col, fcs, outs, pre, hidden, cot, gain_two[None]
    )
    dq, dk, dv, joint, sums = attention_backward(
        lengths, qx, q, k, v, o, ga, upq, upv, narrow, n
    )
    sums = all_sum(sums, total)
    grad = token_gradient(
        index, [first, second], (half, quads - half), dq, dk, dv, joint, down, gh, x,
        gain_one[None],
    )
    return (
        block_out.reshape(tokens.shape),
        grad.reshape(tokens.shape),
        sums[0:4].T,
        sums[8:12],
        sums[4:8].T,
        sums[12:16],
    )


def solution(mesh):
    rows = P(BOTH, None, None)
    frozen = P("fsdp", None)
    return jax.shard_map(
        functools.partial(local, (mesh.shape["dp"], mesh.shape["fsdp"])),
        mesh=mesh,
        in_specs=(rows, P(BOTH), rows, P(), P(), P(), P()) + (frozen,) * 4 + (P(),) * 4,
        out_specs=(rows, rows, P(), P(), P(), P()),
        check_vma=False,
    )
```

```python
import functools

import jax
import jax.numpy as jnp
from jax import lax
from jax.experimental import pallas as pl
from jax.experimental.pallas import tpu as pltpu
from jax.sharding import PartitionSpec as P

BF = jnp.bfloat16
F32 = jnp.float32
HD = 64
PAIR = 2 * HD
PAD = 16
SCALE = 8.0
EPS = 1e-05
NEG = -1e30
BLOCK = 256
FF_STEP = 1024
ROWS = 512
VMEM_LIMIT = 58 * 2**20
GELU_C = 0.7978845608028654
GELU_A = 0.044715
ANY = pl.BlockSpec(memory_space=pl.ANY)
SMEM = pl.BlockSpec(memory_space=pltpu.SMEM)
CHEAP = pl.CostEstimate(flops=1000, bytes_accessed=1000, transcendentals=0)


def dot(a, b):
    return lax.dot_general(a, b, (((1,), (0,)), ((), ())), preferred_element_type=F32)


def dot_nt(a, b):
    return lax.dot_general(a, b, (((1,), (1,)), ((), ())), preferred_element_type=F32)


def dot_tn(a, b):
    return lax.dot_general(a, b, (((0,), (0,)), ((), ())), preferred_element_type=F32)


def lane(shape):
    return lax.broadcasted_iota(jnp.int32, shape, 1)


def row(shape):
    return lax.broadcasted_iota(jnp.int32, shape, 0)


def split3(x):
    a = x.astype(BF)
    r = x - a.astype(F32)
    b = r.astype(BF)
    c = (r - b.astype(F32)).astype(BF)
    return a, b, c


def whole(shape):
    return pl.BlockSpec(shape, lambda *_: (0,) * len(shape))


def params(**kw):
    return pltpu.CompilerParams(vmem_limit_bytes=VMEM_LIMIT, **kw)


def norm_stats(x):
    mean = jnp.mean(x, axis=-1, keepdims=True)
    center = x - mean
    inv = lax.rsqrt(jnp.mean(center * center, axis=-1, keepdims=True) + EPS)
    return center * inv, inv


def norm_back(xhat, inv, g):
    return inv * (
        g
        - jnp.mean(g, axis=-1, keepdims=True)
        - xhat * jnp.mean(g * xhat, axis=-1, keepdims=True)
    )


def pad_rows(parts, width):
    have = sum(p.shape[0] for p in parts)
    return jnp.concatenate(parts + [jnp.zeros((PAD - have, width), F32)], axis=0).astype(BF)


def norm_one_kernel(
    x_ref, gain_ref, shift_ref, dq_ref, dv_ref, uq_ref, uv_ref,
    n_ref, narrow_ref, down_ref, upq_ref, upv_ref,
):
    width = x_ref.shape[1]
    rank = dq_ref.shape[0]

    @pl.when(pl.program_id(0) == 0)
    def _():
        blank = jnp.zeros((rank, width), F32)
        down_ref[...] = pad_rows([dq_ref[...], dv_ref[...]], width)
        upq_ref[...] = pad_rows([uq_ref[...]], width)
        upv_ref[...] = pad_rows([blank, uv_ref[...]], width)

    xhat, _ = norm_stats(x_ref[...].astype(F32))
    low = (xhat * gain_ref[...] + shift_ref[...]).astype(BF)
    n_ref[...] = low
    narrow_ref[...] = dot_nt(down_ref[...], low).astype(BF)


def norm_one(x, gain, shift, dq, dv, uq, uv):
    length, width = x.shape
    small = whole((1, width))
    adapter = whole(dq.shape)
    padded = whole((PAD, width))
    return pl.pallas_call(
        norm_one_kernel,
        grid=(length // BLOCK,),
        in_specs=[pl.BlockSpec((BLOCK, width), lambda i: (i, 0)), small, small] + [adapter] * 4,
        out_specs=[
            pl.BlockSpec((BLOCK, width), lambda i: (i, 0)),
            pl.BlockSpec((PAD, BLOCK), lambda i: (0, i)),
            padded, padded, padded,
        ],
        out_shape=[
            jax.ShapeDtypeStruct((length, width), BF),
            jax.ShapeDtypeStruct((PAD, length), BF),
        ]
        + [jax.ShapeDtypeStruct((PAD, width), BF)] * 3,
        compiler_params=params(),
        name="norm_one",
    )(x, gain, shift, dq, dv, uq, uv)


def repack_kernel(quads, half, qkv_ref, proj_ref, a_ref, b_ref):
    width = proj_ref.shape[1]
    for q in range(quads):
        ref, place = (a_ref, q) if q < half else (b_ref, q - half)
        for p in range(3):
            at = (3 * place + p) * QUAD
            ref[:, at : at + QUAD] = qkv_ref[:, p * width + q * QUAD : p * width + (q + 1) * QUAD]
    at = 3 * (quads - half) * QUAD
    b_ref[:, at : at + width] = proj_ref[...]


def repack(w_qkv, w_proj, half):
    rows, width = w_proj.shape
    quads = width // QUAD
    return pl.pallas_call(
        functools.partial(repack_kernel, quads, half),
        out_shape=[
            jax.ShapeDtypeStruct((rows, 3 * half * QUAD), BF),
            jax.ShapeDtypeStruct((rows, 3 * (quads - half) * QUAD + width), BF),
        ],
        compiler_params=params(),
        name="repack",
    )(w_qkv, w_proj)


QUAD = 2 * PAIR


def causal_below(x):
    size, wide = x.shape
    near = jnp.where(row((size, size)) <= lane((size, size)), x[:, :size], NEG)
    return near if wide == size else jnp.concatenate([near, x[:, size:]], axis=1)


def attend(length, pairs, o_ref, qx_ref, kx, vt, qt, ot):
    size = pairs[0][0].shape[0]
    ln = lane((size, PAIR))
    first = ln < HD
    bias = jnp.where(row((size, PAIR)) < length, 0.0, NEG).astype(BF)
    zero = jnp.zeros((size, PAIR), BF)
    ones = jnp.ones((16, size), BF)
    extra = jnp.where(row((HD, size)) == 0, 1.0, 0.0).astype(BF)

    def prepare(p):
        q, k, v = pairs[p]
        kx[2 * p] = jnp.where(first, k, jnp.where(ln == HD, bias, zero))
        kx[2 * p + 1] = jnp.where(first, jnp.where(ln == 0, bias, zero), k)
        v_t = v.T
        q_t = q.T
        for h in range(2):
            mine = slice(h * HD, (h + 1) * HD)
            vt[2 * p + h, :HD, :] = v_t[mine]
            vt[2 * p + h, HD:, :] = ones
            parts = [q_t[mine], extra] if h == 0 else [extra, q_t[mine]]
            qt[2 * p + h] = jnp.concatenate(parts, axis=0)

    def scores(t):
        return [
            (b, causal_below(dot(kx[t, b : b + BLOCK, :], qt[t, :, b:])))
            for b in range(0, size, BLOCK)
        ]

    def finish(t, parts):
        top = None
        for b, s in parts:
            high = jnp.max(s, axis=0, keepdims=True)
            if b == 0:
                top = high
            else:
                top = jnp.concatenate([top[:, :b], jnp.maximum(top[:, b:], high)], axis=1)
        acc = None
        for b, s in parts:
            p = jnp.exp(s - top[:, b:]).astype(BF)
            a = dot(vt[t, :, b : b + BLOCK], p)
            acc = a if b == 0 else jnp.concatenate([acc[:, :b], acc[:, b:] + a], axis=1)
        total = acc[HD : HD + 1]
        ot[t * HD : (t + 1) * HD, :] = acc[:HD] * (1.0 / total)
        a, b, c = split3(-(top + jnp.log(total)))
        r = row((HD, size))
        more = jnp.where(
            r == 0,
            1.0,
            jnp.where(
                r == 1,
                a.astype(F32),
                jnp.where(r == 2, b.astype(F32), jnp.where(r == 3, c.astype(F32), 0.0)),
            ),
        ).astype(BF)
        at = t * PAIR
        h = t % 2
        qx_ref[at + h * HD : at + (h + 1) * HD, :] = qt[t, h * HD : (h + 1) * HD, :]
        qx_ref[at + (1 - h) * HD : at + (2 - h) * HD, :] = more

    count = 2 * len(pairs)
    prepare(0)
    later = scores(0)
    for t in range(count):
        now = later
        if t + 1 < count:
            if t % 2:
                prepare((t + 1) // 2)
            later = scores(t + 1)
        finish(t, now)
    o_ref[...] = ot[...].T.astype(BF)


def qkv_copies(index_ref, shards, wbuf, sem, quad):
    rows = shards[0].shape[0]
    wide = wbuf.shape[1]
    copies = []
    for i, ref in enumerate(shards):
        at = pl.multiple_of(index_ref[i] * rows, rows)
        src = ref.at[:, quad * wide : (quad + 1) * wide]
        copies.append(pltpu.make_async_copy(src, wbuf.at[pl.ds(at, rows), :], sem))
    return copies


def forward_kernel(count, kept, quads, len_ref, index_ref, *refs):
    shards, refs = refs[:count], refs[count + kept :]
    (n_ref, narrow_ref, upq_ref, upv_ref, o_ref, qx_ref, q_ref, k_ref, v_ref,
     wbuf, kx, vt, qt, ot, sem) = refs
    step = pl.program_id(0)

    def copies(i):
        return qkv_copies(index_ref, shards, wbuf.at[i], sem.at[i], quads[i])

    @pl.when(step == 0)
    def _():
        for i in range(len(quads)):
            for c in copies(i):
                c.start()

    for i in range(len(quads)):

        @pl.when(step == i)
        def _(i=i):
            for c in copies(i):
                c.wait()

    n = n_ref[...]
    narrow = narrow_ref[...]
    w = wbuf.at[step]
    q = dot(n, w[:, :QUAD]) + SCALE * dot_tn(narrow, upq_ref[...])
    k = dot(n, w[:, QUAD : 2 * QUAD])
    v = dot(n, w[:, 2 * QUAD :]) + SCALE * dot_tn(narrow, upv_ref[...])
    q_ref[...] = (q.astype(BF).astype(F32) * (1.0 / HD**0.5)).astype(BF)
    k_ref[...] = k.astype(BF)
    v_ref[...] = v.astype(BF)
    cols = [slice(p * PAIR, (p + 1) * PAIR) for p in range(QUAD // PAIR)]
    pairs = [(q_ref[:, c], k_ref[:, c], v_ref[:, c]) for c in cols]
    attend(len_ref[0], pairs, o_ref, qx_ref, kx, vt, qt, ot)


def attention_forward(lengths, index, shards, n, narrow, upq, upv, quads, here, kept):
    length, width = n.shape
    block = pl.BlockSpec((length, QUAD), lambda s: (0, here + s))
    up = pl.BlockSpec((PAD, QUAD), lambda s: (0, here + s))
    first = 2 + len(shards)
    heads = QUAD // HD
    return pl.pallas_call(
        functools.partial(forward_kernel, len(shards), len(kept), quads),
        grid=(len(quads),),
        in_specs=[SMEM, SMEM]
        + [ANY] * (len(shards) + len(kept))
        + [whole((length, width)), whole((PAD, length)), up, up],
        out_specs=[block, pl.BlockSpec((2 * QUAD, length), lambda s: (here + s, 0))] + [block] * 3,
        out_shape=[
            jax.ShapeDtypeStruct((length, width), BF),
            jax.ShapeDtypeStruct((2 * width, length), BF),
        ]
        + [jax.ShapeDtypeStruct((length, width), BF)] * 3,
        input_output_aliases={first + i: i for i in range(len(kept))},
        scratch_shapes=[
            pltpu.VMEM((len(quads), width, 3 * QUAD), BF),
            pltpu.VMEM((heads, length, PAIR), BF),
            pltpu.VMEM((heads, HD + 16, length), BF),
            pltpu.VMEM((heads, PAIR, length), BF),
            pltpu.VMEM((QUAD, length), F32),
            pltpu.SemaphoreType.DMA((len(quads),)),
        ],
        compiler_params=params(),
        cost_estimate=CHEAP,
        name="attention_forward",
    )(lengths, index, *shards, *kept, n, narrow, upq, upv)


def rows_copies(index_ref, shards, col, wide, wbuf, sem):
    rows = shards[0].shape[0]
    copies = []
    for i, ref in enumerate(shards):
        at = pl.multiple_of(index_ref[i] * rows, rows)
        src = ref.at[:, pl.ds(col, wide)]
        copies.append(pltpu.make_async_copy(src, wbuf.at[pl.ds(at, rows), :], sem))
    return copies


def out_slice(index_ref, outs, step):
    part = outs[0][0].shape[0]
    rows = part * len(outs)
    pieces = []
    if rows >= FF_STEP:
        shard, place = divmod(step, rows // FF_STEP)
        begin = pl.multiple_of(index_ref[shard] * rows + place * FF_STEP, FF_STEP)
        wide = min(part, FF_STEP)
        for at in range(place * FF_STEP, (place + 1) * FF_STEP, wide):
            pieces.append((outs[at // part][shard], at % part, at - place * FF_STEP, wide))
        return begin, pieces
    each = FF_STEP // rows
    begin = index_ref[step * each] * rows // FF_STEP * FF_STEP
    begin = pl.multiple_of(begin, FF_STEP)
    for i in range(step * each, (step + 1) * each):
        to = index_ref[i] * rows - begin
        for h, some in enumerate(outs):
            pieces.append((some[i], 0, pl.multiple_of(to + h * part, part), part))
    return begin, pieces


def gelu_both(v):
    square = v * v
    t = jnp.tanh(v * (GELU_C + (GELU_C * GELU_A) * square))
    half = 0.5 * t + 0.5
    act = v * half
    slope = half + act * (1.0 - half) * (2.0 * GELU_C + (6.0 * GELU_C * GELU_A) * square)
    return act, slope


def split_list(refs, count, halves):
    lists = [refs[h * count : (h + 1) * count] for h in range(halves)]
    return lists, refs[count * halves :]


def blocks_of(size, rows):
    return [pl.ds(i * rows, rows) for i in range(size // rows)]


def rise_kernel(count, halves, col, index_ref, *refs):
    projs, refs = refs[:count], refs[count:]
    fcs, refs = split_list(refs, count, halves)
    (o_ref, x_ref, gain_ref, shift_ref, pre_ref, hidden_ref,
     wproj, fbuf, obuf, xbuf, hidden, n2, psem, fsem, osem, hsem) = refs
    step = pl.program_id(0)
    size, width = xbuf.shape
    steps = halves * fcs[0][0].shape[1] // FF_STEP
    slot = lax.rem(step, 2)
    places = blocks_of(size, BLOCK)

    def fc_copies(s):
        slot = s % 2
        each = steps // halves
        col = s % each * FF_STEP
        return rows_copies(index_ref, fcs[s // each], col, FF_STEP, fbuf.at[slot], fsem.at[slot])

    def row_copies(i):
        at = pl.ds(pl.multiple_of(i * BLOCK, BLOCK), BLOCK)
        return [
            pltpu.make_async_copy(o_ref.at[at, :], obuf.at[at, :], osem.at[i]),
            pltpu.make_async_copy(x_ref.at[at, :], xbuf.at[at, :], osem.at[i]),
        ]

    def hidden_copy(i):
        at = pl.ds(pl.multiple_of(i * BLOCK, BLOCK), BLOCK)
        return pltpu.make_async_copy(hidden.at[at, :], hidden_ref.at[at, :], hsem)

    @pl.when(step == 0)
    def _():
        first = rows_copies(index_ref, projs, col, width, wproj, psem)
        for c in first:
            c.start()
        for i in range(len(places)):
            for c in row_copies(i):
                c.start()
        for c in fc_copies(0):
            c.start()
        for c in first:
            c.wait()

        def begin(i, carry):
            at = pl.ds(pl.multiple_of(i * BLOCK, BLOCK), BLOCK)
            for c in row_copies(i):
                c.wait()
            total = xbuf[at, :].astype(F32) + dot(obuf[at, :], wproj[...])
            hidden[at, :] = total
            hidden_copy(i).start()
            xhat, _ = norm_stats(total)
            n2[at, :] = (xhat * gain_ref[...] + shift_ref[...]).astype(BF)
            return carry

        lax.fori_loop(0, len(places), begin, 0)

    for s in range(1, steps):

        @pl.when(step + 1 == s)
        def _(s=s):
            for c in fc_copies(s):
                c.start()

    for even in range(2):

        @pl.when(slot == even)
        def _(even=even):
            for c in fc_copies(even):
                c.wait()

    def body(i, carry):
        at = pl.ds(pl.multiple_of(i * ROWS, ROWS), ROWS)
        pre_ref[at, :] = dot(n2[at, :], fbuf[slot])
        return carry

    lax.fori_loop(0, size // ROWS, body, 0)

    @pl.when(step == steps - 1)
    def _():
        for i in range(len(places)):
            hidden_copy(i).wait()


def rise(index, projs, col, fcs, o, x, gain, shift):
    size, width = x.shape
    units = sum(half[0].shape[1] for half in fcs)
    small = whole((1, width))
    flat = [f for half in fcs for f in half]
    return pl.pallas_call(
        functools.partial(rise_kernel, len(projs), len(fcs), col),
        grid=(units // FF_STEP,),
        in_specs=[SMEM] + [ANY] * (len(projs) + len(flat) + 2) + [small, small],
        out_specs=[pl.BlockSpec((None, size, FF_STEP), lambda s: (s, 0, 0)), ANY],
        out_shape=[
            jax.ShapeDtypeStruct((units // FF_STEP, size, FF_STEP), F32),
            jax.ShapeDtypeStruct((size, width), F32),
        ],
        scratch_shapes=[
            pltpu.VMEM((width, width), BF),
            pltpu.VMEM((2, width, FF_STEP), BF),
            pltpu.VMEM((size, width), BF),
            pltpu.VMEM((size, width), BF),
            pltpu.VMEM((size, width), F32),
            pltpu.VMEM((size, width), BF),
            pltpu.SemaphoreType.DMA,
            pltpu.SemaphoreType.DMA((2,)),
            pltpu.SemaphoreType.DMA((size // BLOCK,)),
            pltpu.SemaphoreType.DMA,
        ],
        compiler_params=params(),
        cost_estimate=CHEAP,
        name="rise",
    )(index, *projs, *flat, o, x, gain, shift)


def fall_kernel(count, halves, col, steps, len_ref, index_ref, *refs):
    projs, refs = refs[:count], refs[count:]
    fcs, refs = split_list(refs, count, halves[0])
    outs, refs = split_list(refs, count, halves[1])
    (pre_ref, hidden_ref, cot_ref, gain_ref, block_ref, gh_ref, ga_ref,
     wproj, fbuf, obuf, pbuf, hidden, cbuf, low, acc, back, block, gatt, sem, fsem, lsem, wsem) = refs
    step = pl.program_id(0)
    size, width = low.shape
    slot = lax.rem(step, 2)

    def copies(s):
        begin, pieces = out_slice(index_ref, outs, s)
        slot = s % 2
        found = []
        for ref, at, to, rows in pieces:
            found.append(
                pltpu.make_async_copy(
                    ref.at[at : at + rows, :], obuf.at[slot, pl.ds(to, rows), :], sem.at[slot]
                )
            )
        src = pre_ref.at[begin // FF_STEP]
        found.append(pltpu.make_async_copy(src, pbuf.at[slot], sem.at[slot]))
        return found

    def fc_copies(s):
        begin, _ = out_slice(index_ref, outs, s)
        slot = s % 2
        wide = fcs[0][0].shape[1]
        which = begin // wide
        at = pl.multiple_of(begin - which * wide, FF_STEP)
        return which, [
            rows_copies(index_ref, some, at, FF_STEP, fbuf.at[slot], fsem.at[slot]) for some in fcs
        ]

    def start(s):
        for c in copies(s):
            c.start()
        which, found = fc_copies(s)
        for h, some in enumerate(found):

            @pl.when(which == h)
            def _(some=some):
                for c in some:
                    c.start()

    late = [pltpu.make_async_copy(hidden_ref, hidden, lsem.at[1])]
    late += rows_copies(index_ref, projs, col, width, wproj, lsem.at[1])
    first = pltpu.make_async_copy(cot_ref, cbuf, lsem.at[0])

    @pl.when(step == 0)
    def _():
        first.start()
        start(0)
        start(1)
        for c in late:
            c.start()
        first.wait()
        for i, at in enumerate(blocks_of(size, BLOCK)):
            keep = row((BLOCK, 1)) + i * BLOCK < len_ref[0]
            low[at, :] = jnp.where(keep, cbuf[at, :].astype(F32), 0.0).astype(BF)
            acc[at, :] = jnp.zeros((BLOCK, width), F32)
            back[at, :] = jnp.zeros((BLOCK, width), F32)

    for s in range(2, steps):

        @pl.when(step + 1 == s)
        def _(s=s):
            start(s)

    for even in range(2):

        @pl.when(slot == even)
        def _(even=even):
            for c in copies(even) + fc_copies(even)[1][0]:
                c.wait()

    def body(i, carry):
        at = pl.ds(pl.multiple_of(i * ROWS, ROWS), ROWS)
        act, slope = gelu_both(pbuf[slot, at, :])
        acc[at, :] += dot(act.astype(BF), obuf[slot])
        grad = (dot_nt(low[at, :], obuf[slot]) * slope).astype(BF)
        back[at, :] += dot_nt(grad, fbuf[slot])
        return carry

    lax.fori_loop(0, size // ROWS, body, 0)

    @pl.when(step == steps - 1)
    def _():
        for c in late:
            c.wait()
        def out_copies(i):
            at = pl.ds(pl.multiple_of(i * BLOCK, BLOCK), BLOCK)
            return [
                pltpu.make_async_copy(block.at[at, :], block_ref.at[at, :], wsem),
                pltpu.make_async_copy(hidden.at[at, :], gh_ref.at[at, :], wsem),
                pltpu.make_async_copy(gatt.at[at, :], ga_ref.at[at, :], wsem),
            ]

        def finish(i, carry):
            at = pl.ds(pl.multiple_of(i * BLOCK, BLOCK), BLOCK)
            h = hidden[at, :]
            keep = row((BLOCK, 1)) + i * BLOCK < len_ref[0]
            block[at, :] = jnp.where(keep, h + acc[at, :], 0.0).astype(BF)
            xhat, inv = norm_stats(h)
            gh = low[at, :].astype(F32) + norm_back(xhat, inv, gain_ref[...] * back[at, :])
            hidden[at, :] = gh
            gatt[at, :] = dot_nt(gh.astype(BF), wproj[...]).astype(BF)
            for c in out_copies(i):
                c.start()
            return carry

        lax.fori_loop(0, size // BLOCK, finish, 0)
        for i in range(size // BLOCK):
            for c in out_copies(i):
                c.wait()


def fall(lengths, index, projs, col, fcs, outs, pre, hidden, cot, gain):
    size, width = cot.shape
    steps = pre.shape[0]
    flat = [w for half in fcs + outs for w in half]
    return pl.pallas_call(
        functools.partial(fall_kernel, len(projs), (len(fcs), len(outs)), col, steps),
        grid=(steps,),
        in_specs=[SMEM, SMEM] + [ANY] * (len(projs) + len(flat) + 3) + [whole((1, width))],
        out_specs=[ANY] * 3,
        out_shape=[
            jax.ShapeDtypeStruct((size, width), BF),
            jax.ShapeDtypeStruct((size, width), F32),
            jax.ShapeDtypeStruct((size, width), BF),
        ],
        scratch_shapes=[
            pltpu.VMEM((width, width), BF),
            pltpu.VMEM((2, width, FF_STEP), BF),
            pltpu.VMEM((2, FF_STEP, width), BF),
            pltpu.VMEM((2, size, FF_STEP), F32),
            pltpu.VMEM((size, width), F32),
            pltpu.VMEM((size, width), BF),
            pltpu.VMEM((size, width), BF),
            pltpu.VMEM((size, width), F32),
            pltpu.VMEM((size, width), F32),
            pltpu.VMEM((size, width), BF),
            pltpu.VMEM((size, width), BF),
            pltpu.SemaphoreType.DMA((2,)),
            pltpu.SemaphoreType.DMA((2,)),
            pltpu.SemaphoreType.DMA((2,)),
            pltpu.SemaphoreType.DMA,
        ],
        compiler_params=params(),
        cost_estimate=CHEAP,
        name="fall",
    )(lengths, index, *projs, *flat, pre, hidden, cot, gain)


def backward_kernel(
    len_ref, qx_ref, q_ref, k_ref, v_ref, o_ref, g_ref, upq_ref, upv_ref, narrow_ref, n_ref,
    dq_ref, dk_ref, dv_ref, joint_ref, sums_ref, kx, vx, gx, kt, dqt, total,
):
    size = k_ref.shape[0]
    step = pl.program_id(0)
    ln = lane((size, PAIR))
    first = ln < HD
    bias = jnp.where(row((size, PAIR)) < len_ref[0], 0.0, NEG).astype(BF)
    kp = k_ref[...]
    vp = v_ref[...]
    g = g_ref[...]
    qp = q_ref[...]
    zero = jnp.zeros((size, PAIR), BF)
    one = jnp.ones((size, PAIR), BF)
    prod = g.astype(F32) * o_ref[...].astype(F32)
    for h in range(2):
        other = HD * (1 - h)
        mine = first if h == 0 else ~first
        extra = (ln > other) & (ln <= other + 3)
        kx[h] = jnp.where(mine, kp, jnp.where(ln == other, bias, jnp.where(extra, one, zero)))
        vx[h] = jnp.where(mine, vp, jnp.where(extra, one, zero))
        dots = jnp.sum(jnp.where(mine, prod, 0.0), axis=-1, keepdims=True)
        a, b, c = split3(jnp.broadcast_to(-dots, (size, PAIR)))
        gx[h] = jnp.where(
            mine,
            g,
            jnp.where(
                ln == other + 1,
                a,
                jnp.where(ln == other + 2, b, jnp.where(ln == other + 3, c, zero)),
            ),
        )
    kt[...] = kp.T

    def products(b, h):
        st = dot(kx[h, b : b + BLOCK, :], qx_ref[h * PAIR : (h + 1) * PAIR, b:])
        return st, dot_nt(vx[h, b : b + BLOCK, :], gx[h, b:, :])

    held = {}

    def finish(b, h, st, dp):
        p = jnp.exp(causal_below(st))
        ds = (p * dp).astype(BF)
        mine = slice(h * HD, (h + 1) * HD)
        c = dot(kt[mine, b : b + BLOCK], ds)
        if b == 0:
            dqt[mine, :] = c
        else:
            dqt[mine, b:] += c
        held[h] = (dot(p.astype(BF), g[b:]), dot(ds, qp[b:]))
        if h == 1:
            f = lane((BLOCK, PAIR)) < HD
            dv_ref[b : b + BLOCK, :] = jnp.where(f, held[0][0], held[1][0]).astype(BF)
            dk_ref[b : b + BLOCK, :] = jnp.where(f, held[0][1], held[1][1]).astype(BF)

    tasks = [(b, h) for b in range(0, size, BLOCK) for h in range(2)]
    later = products(*tasks[0])
    for j, t in enumerate(tasks):
        now = later
        if j + 1 < len(tasks):
            later = products(*tasks[j + 1])
        finish(*t, *now)
    dq = (dqt[...] * (1.0 / HD**0.5)).T.astype(BF)
    dq_ref[...] = dq
    dv = dv_ref[...]
    narrow = narrow_ref[...]
    both = jnp.concatenate([dq, dv], axis=1)
    part = dot_nt(jnp.concatenate([upq_ref[...], upv_ref[...]], axis=1), both)
    ups = SCALE * dot(narrow, both)[:8]
    gq, gv = ups[:, :PAIR], ups[:, PAIR:]
    cols = pl.ds(pl.multiple_of(step * PAIR, PAIR), PAIR)
    sums_ref[8:16, cols] = jnp.where(row((8, PAIR)) < 4, gq, gv)

    @pl.when(step == 0)
    def _():
        total[...] = part

    @pl.when(step > 0)
    def _():
        total[...] += part

    @pl.when(step == pl.num_programs(0) - 1)
    def _():
        joint = (SCALE * total[...]).astype(BF)
        joint_ref[...] = joint
        sums_ref[0:8, :] = dot(joint, n_ref[...])[:8]


def attention_backward(lengths, qx, q, k, v, o, ga, upq, upv, narrow, n):
    size, width = k.shape
    pair = pl.BlockSpec((size, PAIR), lambda p: (0, p))
    up = pl.BlockSpec((PAD, PAIR), lambda p: (0, p))
    return pl.pallas_call(
        backward_kernel,
        grid=(width // PAIR,),
        in_specs=[SMEM, pl.BlockSpec((2 * PAIR, size), lambda p: (p, 0))]
        + [pair] * 5
        + [up, up, whole((PAD, size)), whole((size, width))],
        out_specs=[pair] * 3 + [whole((PAD, size)), whole((16, width))],
        out_shape=[jax.ShapeDtypeStruct((size, width), BF)] * 3
        + [jax.ShapeDtypeStruct((PAD, size), BF), jax.ShapeDtypeStruct((16, width), F32)],
        scratch_shapes=[pltpu.VMEM((2, size, PAIR), BF)] * 3
        + [
            pltpu.VMEM((PAIR, size), BF),
            pltpu.VMEM((PAIR, size), F32),
            pltpu.VMEM((PAD, size), F32),
        ],
        compiler_params=params(),
        cost_estimate=CHEAP,
        name="attention_backward",
    )(lengths, qx, q, k, v, o, ga, upq, upv, narrow, n)


def token_kernel(counts, quads, index_ref, *refs):
    shards = []
    for count in counts:
        shards.append(refs[:count])
        refs = refs[count:]
    (dq_ref, dk_ref, dv_ref, joint_ref, down_ref, gh_ref, x_ref, gain_ref, o_ref, wbuf, sem) = refs
    step = pl.program_id(0)
    pieces = [(j, q) for j in range(len(counts)) for q in range(quads[j])]

    def copies(s):
        j, q = pieces[s]
        return qkv_copies(index_ref, shards[j], wbuf.at[s], sem.at[s], q)

    @pl.when(step == 0)
    def _():
        for s in range(len(pieces)):
            for c in copies(s):
                c.start()

    total = dot_tn(joint_ref[...], down_ref[...])
    for s in range(len(pieces)):

        @pl.when(step == 0)
        def _(s=s):
            for c in copies(s):
                c.wait()

        cols = slice(s * QUAD, (s + 1) * QUAD)
        g = jnp.concatenate([ref[:, cols] for ref in (dq_ref, dk_ref, dv_ref)], axis=1)
        total = total + dot_nt(g, wbuf[s])
    xhat, inv = norm_stats(x_ref[...].astype(F32))
    o_ref[...] = (gh_ref[...] + norm_back(xhat, inv, gain_ref[...] * total)).astype(BF)


def token_gradient(index, shards, quads, dq, dk, dv, joint, down, gh, x, gain):
    size, width = x.shape
    flat = [s for part in shards for s in part]
    block = pl.BlockSpec((BLOCK, width), lambda i: (i, 0))
    return pl.pallas_call(
        functools.partial(token_kernel, [len(p) for p in shards], quads),
        grid=(size // BLOCK,),
        in_specs=[SMEM]
        + [ANY] * len(flat)
        + [block] * 3
        + [pl.BlockSpec((PAD, BLOCK), lambda i: (0, i)), whole((PAD, width))]
        + [block, block, whole((1, width))],
        out_specs=block,
        out_shape=jax.ShapeDtypeStruct((size, width), BF),
        scratch_shapes=[
            pltpu.VMEM((sum(quads), width, 3 * QUAD), BF),
            pltpu.SemaphoreType.DMA((sum(quads),)),
        ],
        compiler_params=params(),
        cost_estimate=CHEAP,
        name="token_gradient",
    )(index, *flat, dq, dk, dv, joint, down, gh, x, gain)


BOTH = ("dp", "fsdp")


def swap(value, fn, total):
    return lax.ppermute(value, BOTH, [(i, fn(i)) for i in range(total)])


def after(value, *others):
    return lax.optimization_barrier((value,) + others)[0]


class Cube:
    def __init__(self, total, fsdp):
        self.total, self.fsdp = total, fsdp

    def even(self, i):
        return (i // self.fsdp) % 2 == 0

    def sibling(self, value):
        return swap(value, lambda i: i ^ 1, self.total)

    def first(self, value, turned=False):
        return swap(value, lambda i: i ^ (2 if self.even(i) != turned else 4), self.total)

    def second(self, value, turned=False):
        b = swap(value, lambda i: i ^ (4 if self.even(i) != turned else 2), self.total)
        c = swap(value, lambda i: i ^ self.fsdp, self.total)
        return b, c

    def all(self, own, a, b, c, turned=False):
        found = []
        for pair in (own, c, b, a) if turned else (own, a, b, c):
            found += pair
        return found

    def pair(self, value):
        return [value, self.sibling(value)]

    def index(self):
        here = lax.axis_index("fsdp").astype(jnp.int32)
        odd = lax.axis_index("dp").astype(jnp.int32) % 2
        a, c = 2 + 2 * odd, 4 - 2 * odd
        return jnp.stack([here ^ (m ^ s) for m in (0, a, 6, c) for s in (0, 1)])


def sum_rounds(total):
    bits = [1 << i for i in range(1, total.bit_length() - 1)]
    return [[1]] + [bits[i : i + 2] for i in range(0, len(bits), 2)]


def sum_round(value, bits, total):
    if len(bits) == 1:
        return value + swap(value, lambda i: i ^ bits[0], total)
    low, high = bits
    a = swap(value, lambda i: i ^ low, total)
    b = swap(value, lambda i: i ^ high, total)
    c = swap(value, lambda i: i ^ (low | high), total)
    return (value + a) + (b + c)


def local(
    sizes, tokens, lengths, cotangent, gain_one, shift_one, gain_two, shift_two,
    w_qkv, w_proj, w_fc, w_out,
    query_down_factor, query_up_factor, value_down_factor, value_up_factor,
):
    _, size, width = tokens.shape
    dp, fsdp = sizes
    total = dp * fsdp
    x = tokens.reshape(size, width)
    cot = cotangent.reshape(size, width)
    quads = width // QUAD
    half = quads // 2
    w0, w1 = repack(w_qkv, w_proj, half)
    small = (
        x, gain_one[None], shift_one[None],
        query_down_factor.T, value_down_factor.T, query_up_factor, value_up_factor,
    )
    low = tuple(range(half))
    col = 3 * (quads - half) * QUAD
    if fsdp == 8 and dp % 2 == 0:
        cube = Cube(total, fsdp)
        index = cube.index()
        a0, a1, af, ao = [cube.first(w) for w in (w0, w1, w_fc, w_out)]
        own0, own1, ownf, owno = [cube.pair(w) for w in (w0, w1, w_fc, w_out)]
        n, narrow, down, upq, upv = norm_one(*small)
        attend = functools.partial(
            attention_forward, lengths, index, narrow=narrow, upq=upq, upv=upv
        )
        a0 = after(a0, n)
        b0, c0 = cube.second(a0)
        first = cube.all(own0, *map(cube.pair, (a0, b0, c0)))
        b1, c1 = cube.second(a1)
        n1 = after(n, a1)
        kept = attend(first, n=n1, quads=low[:1], here=0, kept=[])
        kept = attend(first, n=n1, quads=low[1:], here=1, kept=kept)
        a1 = after(a1, kept[0])
        b1, c1 = after(b1, kept[0]), after(c1, kept[0])
        second = cube.all(own1, *map(cube.pair, (a1, b1, c1)))
        af = after(af, kept[0])
        bf, cf = cube.second(af)
        n2 = after(n, af)
        kept = attend(second, n=n2, quads=low, here=half, kept=kept)
        af = after(af, kept[0])
        bf, cf = after(bf, kept[0]), after(cf, kept[0])
        fcs = [cube.all(ownf, *map(cube.pair, (af, bf, cf)))]
        ao = after(ao, kept[0])
        bo, co = cube.second(ao)
        o, qx, q, k, v = kept
        o_late = after(o, ao)
        pre, hidden = rise(index, second, col, fcs, o_late, x, gain_two[None], shift_two[None])
        ao, bo, co = after(ao, hidden), after(bo, hidden), after(co, hidden)
        outs = [cube.all(owno, *map(cube.pair, (ao, bo, co)))]
    else:
        index = jnp.zeros((1,), jnp.int32)
        first, second, fcs, outs = [
            [lax.all_gather(w, "fsdp", axis=0, tiled=True)] for w in (w0, w1, w_fc, w_out)
        ]
        fcs, outs = [fcs], [outs]
        n, narrow, down, upq, upv = norm_one(*small)
        kept = attention_forward(lengths, index, first, n, narrow, upq, upv, low, 0, [])
        kept = attention_forward(lengths, index, second, n, narrow, upq, upv, low, half, kept)
        o, qx, q, k, v = kept
        pre, hidden = rise(index, second, col, fcs, o, x, gain_two[None], shift_two[None])
    block_out, gh, ga = fall(
        lengths, index, second, col, fcs, outs, pre, hidden, cot, gain_two[None]
    )
    dq, dk, dv, joint, sums = attention_backward(
        lengths, qx, q, k, v, o, ga, upq, upv, narrow, n
    )
    args = (dq, dk, dv, joint, down, gh, x, gain_one[None])
    shards, quads = [first, second], (half, quads - half)
    if total & (total - 1):
        sums = lax.psum(sums, BOTH)
        grad = token_gradient(index, shards, quads, *args)
    else:
        for bits in sum_rounds(total):
            sums = sum_round(sums, bits, total)
        grad = token_gradient(index, shards, quads, *args)
    return (
        block_out.reshape(tokens.shape),
        grad.reshape(tokens.shape),
        sums[0:4].T,
        sums[8:12],
        sums[4:8].T,
        sums[12:16],
    )


def solution(mesh):
    rows = P(BOTH, None, None)
    frozen = P("fsdp", None)
    return jax.shard_map(
        functools.partial(local, (mesh.shape["dp"], mesh.shape["fsdp"])),
        mesh=mesh,
        in_specs=(rows, P(BOTH), rows, P(), P(), P(), P()) + (frozen,) * 4 + (P(),) * 4,
        out_specs=(rows, rows, P(), P(), P(), P()),
        check_vma=False,
    )
```

```python
import functools

import jax
import jax.numpy as jnp
from jax import lax
from jax.experimental import pallas as pl
from jax.experimental.pallas import tpu as pltpu
from jax.sharding import PartitionSpec as P

BF = jnp.bfloat16
F32 = jnp.float32
HD = 64
PAIR = 2 * HD
PAD = 16
SCALE = 8.0
EPS = 1e-05
NEG = -1e30
BLOCK = 256
FF_STEP = 1024
ROWS = 512
VMEM_LIMIT = 58 * 2**20
GELU_C = 0.7978845608028654
GELU_A = 0.044715
ANY = pl.BlockSpec(memory_space=pl.ANY)
SMEM = pl.BlockSpec(memory_space=pltpu.SMEM)
CHEAP = pl.CostEstimate(flops=1000, bytes_accessed=1000, transcendentals=0)


def dot(a, b):
    return lax.dot_general(a, b, (((1,), (0,)), ((), ())), preferred_element_type=F32)


def dot_nt(a, b):
    return lax.dot_general(a, b, (((1,), (1,)), ((), ())), preferred_element_type=F32)


def dot_tn(a, b):
    return lax.dot_general(a, b, (((0,), (0,)), ((), ())), preferred_element_type=F32)


def lane(shape):
    return lax.broadcasted_iota(jnp.int32, shape, 1)


def row(shape):
    return lax.broadcasted_iota(jnp.int32, shape, 0)


def split3(x):
    a = x.astype(BF)
    r = x - a.astype(F32)
    b = r.astype(BF)
    c = (r - b.astype(F32)).astype(BF)
    return a, b, c


def whole(shape):
    return pl.BlockSpec(shape, lambda *_: (0,) * len(shape))


def params(**kw):
    return pltpu.CompilerParams(vmem_limit_bytes=VMEM_LIMIT, **kw)


def norm_stats(x):
    mean = jnp.mean(x, axis=-1, keepdims=True)
    center = x - mean
    inv = lax.rsqrt(jnp.mean(center * center, axis=-1, keepdims=True) + EPS)
    return center * inv, inv


def norm_back(xhat, inv, g):
    return inv * (
        g
        - jnp.mean(g, axis=-1, keepdims=True)
        - xhat * jnp.mean(g * xhat, axis=-1, keepdims=True)
    )


def pad_rows(parts, width):
    have = sum(p.shape[0] for p in parts)
    return jnp.concatenate(parts + [jnp.zeros((PAD - have, width), F32)], axis=0).astype(BF)


def norm_one_kernel(
    x_ref, gain_ref, shift_ref, dq_ref, dv_ref, uq_ref, uv_ref,
    n_ref, narrow_ref, down_ref, upq_ref, upv_ref,
):
    width = x_ref.shape[1]
    rank = dq_ref.shape[0]

    @pl.when(pl.program_id(0) == 0)
    def _():
        blank = jnp.zeros((rank, width), F32)
        down_ref[...] = pad_rows([dq_ref[...], dv_ref[...]], width)
        upq_ref[...] = pad_rows([uq_ref[...]], width)
        upv_ref[...] = pad_rows([blank, uv_ref[...]], width)

    xhat, _ = norm_stats(x_ref[...].astype(F32))
    low = (xhat * gain_ref[...] + shift_ref[...]).astype(BF)
    n_ref[...] = low
    narrow_ref[...] = dot_nt(down_ref[...], low).astype(BF)


def norm_one(x, gain, shift, dq, dv, uq, uv):
    length, width = x.shape
    small = whole((1, width))
    adapter = whole(dq.shape)
    padded = whole((PAD, width))
    return pl.pallas_call(
        norm_one_kernel,
        grid=(length // BLOCK,),
        in_specs=[pl.BlockSpec((BLOCK, width), lambda i: (i, 0)), small, small] + [adapter] * 4,
        out_specs=[
            pl.BlockSpec((BLOCK, width), lambda i: (i, 0)),
            pl.BlockSpec((PAD, BLOCK), lambda i: (0, i)),
            padded, padded, padded,
        ],
        out_shape=[
            jax.ShapeDtypeStruct((length, width), BF),
            jax.ShapeDtypeStruct((PAD, length), BF),
        ]
        + [jax.ShapeDtypeStruct((PAD, width), BF)] * 3,
        compiler_params=params(),
        name="norm_one",
    )(x, gain, shift, dq, dv, uq, uv)


def repack_kernel(quads, half, qkv_ref, proj_ref, a_ref, b_ref):
    width = proj_ref.shape[1]
    for q in range(quads):
        ref, place = (a_ref, q) if q < half else (b_ref, q - half)
        for p in range(3):
            at = (3 * place + p) * QUAD
            ref[:, at : at + QUAD] = qkv_ref[:, p * width + q * QUAD : p * width + (q + 1) * QUAD]
    at = 3 * (quads - half) * QUAD
    b_ref[:, at : at + width] = proj_ref[...]


def repack(w_qkv, w_proj, half):
    rows, width = w_proj.shape
    quads = width // QUAD
    return pl.pallas_call(
        functools.partial(repack_kernel, quads, half),
        out_shape=[
            jax.ShapeDtypeStruct((rows, 3 * half * QUAD), BF),
            jax.ShapeDtypeStruct((rows, 3 * (quads - half) * QUAD + width), BF),
        ],
        compiler_params=params(),
        name="repack",
    )(w_qkv, w_proj)


QUAD = 2 * PAIR


def causal_below(x):
    size, wide = x.shape
    near = jnp.where(row((size, size)) <= lane((size, size)), x[:, :size], NEG)
    return near if wide == size else jnp.concatenate([near, x[:, size:]], axis=1)


def attend(length, pairs, o_ref, qx_ref, kx, vt, qt, ot):
    size = pairs[0][0].shape[0]
    ln = lane((size, PAIR))
    first = ln < HD
    bias = jnp.where(row((size, PAIR)) < length, 0.0, NEG).astype(BF)
    zero = jnp.zeros((size, PAIR), BF)
    ones = jnp.ones((16, size), BF)
    extra = jnp.where(row((HD, size)) == 0, 1.0, 0.0).astype(BF)

    def prepare(p):
        q, k, v = pairs[p]
        kx[2 * p] = jnp.where(first, k, jnp.where(ln == HD, bias, zero))
        kx[2 * p + 1] = jnp.where(first, jnp.where(ln == 0, bias, zero), k)
        v_t = v.T
        q_t = q.T
        for h in range(2):
            mine = slice(h * HD, (h + 1) * HD)
            vt[2 * p + h, :HD, :] = v_t[mine]
            vt[2 * p + h, HD:, :] = ones
            parts = [q_t[mine], extra] if h == 0 else [extra, q_t[mine]]
            qt[2 * p + h] = jnp.concatenate(parts, axis=0)

    def scores(t):
        return [
            (b, causal_below(dot(kx[t, b : b + BLOCK, :], qt[t, :, b:])))
            for b in range(0, size, BLOCK)
        ]

    def finish(t, parts):
        top = None
        for b, s in parts:
            high = jnp.max(s, axis=0, keepdims=True)
            if b == 0:
                top = high
            else:
                top = jnp.concatenate([top[:, :b], jnp.maximum(top[:, b:], high)], axis=1)
        acc = None
        for b, s in parts:
            p = jnp.exp(s - top[:, b:]).astype(BF)
            a = dot(vt[t, :, b : b + BLOCK], p)
            acc = a if b == 0 else jnp.concatenate([acc[:, :b], acc[:, b:] + a], axis=1)
        total = acc[HD : HD + 1]
        ot[t * HD : (t + 1) * HD, :] = acc[:HD] * (1.0 / total)
        a, b, c = split3(-(top + jnp.log(total)))
        r = row((HD, size))
        more = jnp.where(
            r == 0,
            1.0,
            jnp.where(
                r == 1,
                a.astype(F32),
                jnp.where(r == 2, b.astype(F32), jnp.where(r == 3, c.astype(F32), 0.0)),
            ),
        ).astype(BF)
        at = t * PAIR
        h = t % 2
        qx_ref[at + h * HD : at + (h + 1) * HD, :] = qt[t, h * HD : (h + 1) * HD, :]
        qx_ref[at + (1 - h) * HD : at + (2 - h) * HD, :] = more

    count = 2 * len(pairs)
    prepare(0)
    later = scores(0)
    for t in range(count):
        now = later
        if t + 1 < count:
            if t % 2:
                prepare((t + 1) // 2)
            later = scores(t + 1)
        finish(t, now)
    o_ref[...] = ot[...].T.astype(BF)


def qkv_copies(index_ref, shards, wbuf, sem, quad):
    rows = shards[0].shape[0]
    wide = wbuf.shape[1]
    copies = []
    for i, ref in enumerate(shards):
        at = pl.multiple_of(index_ref[i] * rows, rows)
        src = ref.at[:, quad * wide : (quad + 1) * wide]
        copies.append(pltpu.make_async_copy(src, wbuf.at[pl.ds(at, rows), :], sem))
    return copies


def forward_kernel(count, kept, quads, len_ref, index_ref, *refs):
    shards, refs = refs[:count], refs[count + kept :]
    (n_ref, narrow_ref, upq_ref, upv_ref, o_ref, qx_ref, q_ref, k_ref, v_ref,
     wbuf, kx, vt, qt, ot, sem) = refs
    step = pl.program_id(0)

    def copies(i):
        return qkv_copies(index_ref, shards, wbuf.at[i], sem.at[i], quads[i])

    @pl.when(step == 0)
    def _():
        for i in range(len(quads)):
            for c in copies(i):
                c.start()

    for i in range(len(quads)):

        @pl.when(step == i)
        def _(i=i):
            for c in copies(i):
                c.wait()

    n = n_ref[...]
    narrow = narrow_ref[...]
    w = wbuf.at[step]
    q = dot(n, w[:, :QUAD]) + SCALE * dot_tn(narrow, upq_ref[...])
    k = dot(n, w[:, QUAD : 2 * QUAD])
    v = dot(n, w[:, 2 * QUAD :]) + SCALE * dot_tn(narrow, upv_ref[...])
    q_ref[...] = (q.astype(BF).astype(F32) * (1.0 / HD**0.5)).astype(BF)
    k_ref[...] = k.astype(BF)
    v_ref[...] = v.astype(BF)
    cols = [slice(p * PAIR, (p + 1) * PAIR) for p in range(QUAD // PAIR)]
    pairs = [(q_ref[:, c], k_ref[:, c], v_ref[:, c]) for c in cols]
    attend(len_ref[0], pairs, o_ref, qx_ref, kx, vt, qt, ot)


def attention_forward(lengths, index, shards, n, narrow, upq, upv, quads, here, kept):
    length, width = n.shape
    block = pl.BlockSpec((length, QUAD), lambda s: (0, here + s))
    up = pl.BlockSpec((PAD, QUAD), lambda s: (0, here + s))
    first = 2 + len(shards)
    heads = QUAD // HD
    return pl.pallas_call(
        functools.partial(forward_kernel, len(shards), len(kept), quads),
        grid=(len(quads),),
        in_specs=[SMEM, SMEM]
        + [ANY] * (len(shards) + len(kept))
        + [whole((length, width)), whole((PAD, length)), up, up],
        out_specs=[block, pl.BlockSpec((2 * QUAD, length), lambda s: (here + s, 0))] + [block] * 3,
        out_shape=[
            jax.ShapeDtypeStruct((length, width), BF),
            jax.ShapeDtypeStruct((2 * width, length), BF),
        ]
        + [jax.ShapeDtypeStruct((length, width), BF)] * 3,
        input_output_aliases={first + i: i for i in range(len(kept))},
        scratch_shapes=[
            pltpu.VMEM((len(quads), width, 3 * QUAD), BF),
            pltpu.VMEM((heads, length, PAIR), BF),
            pltpu.VMEM((heads, HD + 16, length), BF),
            pltpu.VMEM((heads, PAIR, length), BF),
            pltpu.VMEM((QUAD, length), F32),
            pltpu.SemaphoreType.DMA((len(quads),)),
        ],
        compiler_params=params(),
        cost_estimate=CHEAP,
        name="attention_forward",
    )(lengths, index, *shards, *kept, n, narrow, upq, upv)


def rows_copies(index_ref, shards, col, wide, wbuf, sem):
    rows = shards[0].shape[0]
    copies = []
    for i, ref in enumerate(shards):
        at = pl.multiple_of(index_ref[i] * rows, rows)
        src = ref.at[:, pl.ds(col, wide)]
        copies.append(pltpu.make_async_copy(src, wbuf.at[pl.ds(at, rows), :], sem))
    return copies


def out_slice(index_ref, outs, step):
    part = outs[0][0].shape[0]
    rows = part * len(outs)
    pieces = []
    if rows >= FF_STEP:
        shard, place = divmod(step, rows // FF_STEP)
        begin = pl.multiple_of(index_ref[shard] * rows + place * FF_STEP, FF_STEP)
        wide = min(part, FF_STEP)
        for at in range(place * FF_STEP, (place + 1) * FF_STEP, wide):
            pieces.append((outs[at // part][shard], at % part, at - place * FF_STEP, wide))
        return begin, pieces
    each = FF_STEP // rows
    begin = index_ref[step * each] * rows // FF_STEP * FF_STEP
    begin = pl.multiple_of(begin, FF_STEP)
    for i in range(step * each, (step + 1) * each):
        to = index_ref[i] * rows - begin
        for h, some in enumerate(outs):
            pieces.append((some[i], 0, pl.multiple_of(to + h * part, part), part))
    return begin, pieces


def gelu_both(v):
    square = v * v
    t = jnp.tanh(v * (GELU_C + (GELU_C * GELU_A) * square))
    half = 0.5 * t + 0.5
    act = v * half
    slope = half + act * (1.0 - half) * (2.0 * GELU_C + (6.0 * GELU_C * GELU_A) * square)
    return act, slope


def split_list(refs, count, halves):
    lists = [refs[h * count : (h + 1) * count] for h in range(halves)]
    return lists, refs[count * halves :]


def blocks_of(size, rows):
    return [pl.ds(i * rows, rows) for i in range(size // rows)]


def rise_kernel(count, halves, col, index_ref, *refs):
    projs, refs = refs[:count], refs[count:]
    fcs, refs = split_list(refs, count, halves)
    (o_ref, x_ref, gain_ref, shift_ref, pre_ref, hidden_ref,
     wproj, fbuf, obuf, xbuf, hidden, n2, psem, fsem, osem, hsem) = refs
    step = pl.program_id(0)
    size, width = xbuf.shape
    steps = halves * fcs[0][0].shape[1] // FF_STEP
    slot = lax.rem(step, 2)
    places = blocks_of(size, BLOCK)

    def fc_copies(s):
        slot = s % 2
        each = steps // halves
        col = s % each * FF_STEP
        return rows_copies(index_ref, fcs[s // each], col, FF_STEP, fbuf.at[slot], fsem.at[slot])

    def row_copies(i):
        at = pl.ds(pl.multiple_of(i * BLOCK, BLOCK), BLOCK)
        return [
            pltpu.make_async_copy(o_ref.at[at, :], obuf.at[at, :], osem.at[i]),
            pltpu.make_async_copy(x_ref.at[at, :], xbuf.at[at, :], osem.at[i]),
        ]

    def hidden_copy(i):
        at = pl.ds(pl.multiple_of(i * BLOCK, BLOCK), BLOCK)
        return pltpu.make_async_copy(hidden.at[at, :], hidden_ref.at[at, :], hsem)

    @pl.when(step == 0)
    def _():
        first = rows_copies(index_ref, projs, col, width, wproj, psem)
        for c in first:
            c.start()
        for i in range(len(places)):
            for c in row_copies(i):
                c.start()
        for c in fc_copies(0):
            c.start()
        for c in first:
            c.wait()

        def begin(i, carry):
            at = pl.ds(pl.multiple_of(i * BLOCK, BLOCK), BLOCK)
            for c in row_copies(i):
                c.wait()
            total = xbuf[at, :].astype(F32) + dot(obuf[at, :], wproj[...])
            hidden[at, :] = total
            hidden_copy(i).start()
            xhat, _ = norm_stats(total)
            n2[at, :] = (xhat * gain_ref[...] + shift_ref[...]).astype(BF)
            return carry

        lax.fori_loop(0, len(places), begin, 0)

    for s in range(1, steps):

        @pl.when(step + 1 == s)
        def _(s=s):
            for c in fc_copies(s):
                c.start()

    for even in range(2):

        @pl.when(slot == even)
        def _(even=even):
            for c in fc_copies(even):
                c.wait()

    def body(i, carry):
        at = pl.ds(pl.multiple_of(i * ROWS, ROWS), ROWS)
        pre_ref[at, :] = dot(n2[at, :], fbuf[slot])
        return carry

    lax.fori_loop(0, size // ROWS, body, 0)

    @pl.when(step == steps - 1)
    def _():
        for i in range(len(places)):
            hidden_copy(i).wait()


def rise(index, projs, col, fcs, o, x, gain, shift):
    size, width = x.shape
    units = sum(half[0].shape[1] for half in fcs)
    small = whole((1, width))
    flat = [f for half in fcs for f in half]
    return pl.pallas_call(
        functools.partial(rise_kernel, len(projs), len(fcs), col),
        grid=(units // FF_STEP,),
        in_specs=[SMEM] + [ANY] * (len(projs) + len(flat) + 2) + [small, small],
        out_specs=[pl.BlockSpec((None, size, FF_STEP), lambda s: (s, 0, 0)), ANY],
        out_shape=[
            jax.ShapeDtypeStruct((units // FF_STEP, size, FF_STEP), F32),
            jax.ShapeDtypeStruct((size, width), F32),
        ],
        scratch_shapes=[
            pltpu.VMEM((width, width), BF),
            pltpu.VMEM((2, width, FF_STEP), BF),
            pltpu.VMEM((size, width), BF),
            pltpu.VMEM((size, width), BF),
            pltpu.VMEM((size, width), F32),
            pltpu.VMEM((size, width), BF),
            pltpu.SemaphoreType.DMA,
            pltpu.SemaphoreType.DMA((2,)),
            pltpu.SemaphoreType.DMA((size // BLOCK,)),
            pltpu.SemaphoreType.DMA,
        ],
        compiler_params=params(),
        cost_estimate=CHEAP,
        name="rise",
    )(index, *projs, *flat, o, x, gain, shift)


def fall_kernel(count, halves, col, steps, len_ref, index_ref, *refs):
    projs, refs = refs[:count], refs[count:]
    fcs, refs = split_list(refs, count, halves[0])
    outs, refs = split_list(refs, count, halves[1])
    (pre_ref, hidden_ref, cot_ref, gain_ref, block_ref, gh_ref, ga_ref,
     wproj, fbuf, obuf, pbuf, hidden, cbuf, low, acc, back, block, gatt, grads, sem, fsem, lsem, wsem) = refs
    step = pl.program_id(0)
    size, width = low.shape
    slot = lax.rem(step, 2)

    def copies(s):
        begin, pieces = out_slice(index_ref, outs, s)
        slot = s % 2
        found = []
        for ref, at, to, rows in pieces:
            found.append(
                pltpu.make_async_copy(
                    ref.at[at : at + rows, :], obuf.at[slot, pl.ds(to, rows), :], sem.at[slot]
                )
            )
        src = pre_ref.at[begin // FF_STEP]
        found.append(pltpu.make_async_copy(src, pbuf.at[slot], sem.at[slot]))
        return found

    def fc_copies(s):
        begin, _ = out_slice(index_ref, outs, s)
        slot = s % 2
        wide = fcs[0][0].shape[1]
        which = begin // wide
        at = pl.multiple_of(begin - which * wide, FF_STEP)
        return which, [
            rows_copies(index_ref, some, at, FF_STEP, fbuf.at[slot], fsem.at[slot]) for some in fcs
        ]

    def start(s):
        for c in copies(s):
            c.start()
        which, found = fc_copies(s)
        for h, some in enumerate(found):

            @pl.when(which == h)
            def _(some=some):
                for c in some:
                    c.start()

    late = [pltpu.make_async_copy(hidden_ref, hidden, lsem.at[1])]
    late += rows_copies(index_ref, projs, col, width, wproj, lsem.at[1])
    first = pltpu.make_async_copy(cot_ref, cbuf, lsem.at[0])

    @pl.when(step == 0)
    def _():
        first.start()
        start(0)
        start(1)
        for c in late:
            c.start()
        first.wait()
        for i, at in enumerate(blocks_of(size, BLOCK)):
            keep = row((BLOCK, 1)) + i * BLOCK < len_ref[0]
            low[at, :] = jnp.where(keep, cbuf[at, :].astype(F32), 0.0).astype(BF)
            acc[at, :] = jnp.zeros((BLOCK, width), F32)
            back[at, :] = jnp.zeros((BLOCK, width), F32)

    for s in range(2, steps):

        @pl.when(step + 1 == s)
        def _(s=s):
            start(s)

    for even in range(2):

        @pl.when(slot == even)
        def _(even=even):
            for c in copies(even) + fc_copies(even)[1][0]:
                c.wait()

    def body(i, carry):
        at = pl.ds(pl.multiple_of(i * ROWS, ROWS), ROWS)
        down = dot_nt(low[at, :], obuf[slot])
        act, slope = gelu_both(pbuf[slot, at, :])
        acc[at, :] += dot(act.astype(BF), obuf[slot])
        back[at, :] += dot_nt((down * slope).astype(BF), fbuf[slot])
        return carry

    lax.fori_loop(0, size // ROWS, body, 0)

    @pl.when(step == steps - 1)
    def _():
        for c in late:
            c.wait()
        def out_copies(i):
            at = pl.ds(pl.multiple_of(i * BLOCK, BLOCK), BLOCK)
            return [
                pltpu.make_async_copy(block.at[at, :], block_ref.at[at, :], wsem),
                pltpu.make_async_copy(hidden.at[at, :], gh_ref.at[at, :], wsem),
                pltpu.make_async_copy(gatt.at[at, :], ga_ref.at[at, :], wsem),
            ]

        def grad(i):
            at = pl.ds(pl.multiple_of(i * BLOCK, BLOCK), BLOCK)
            h = hidden[at, :]
            keep = row((BLOCK, 1)) + i * BLOCK < len_ref[0]
            block[at, :] = jnp.where(keep, h + acc[at, :], 0.0).astype(BF)
            xhat, inv = norm_stats(h)
            gh = low[at, :].astype(F32) + norm_back(xhat, inv, gain_ref[...] * back[at, :])
            hidden[at, :] = gh
            return gh.astype(BF)

        def product(i, gh):
            at = pl.ds(pl.multiple_of(i * BLOCK, BLOCK), BLOCK)
            gatt[at, :] = dot_nt(gh, wproj[...]).astype(BF)
            for c in out_copies(i):
                c.start()

        def finish(i, carry):
            last = grads[...]
            at = pl.ds(pl.multiple_of((i - 1) * BLOCK, BLOCK), BLOCK)
            made = dot_nt(last, wproj[...]).astype(BF)
            grads[...] = grad(i)
            gatt[at, :] = made
            for c in out_copies(i - 1):
                c.start()
            return carry

        blocks = size // BLOCK
        grads[...] = grad(0)
        lax.fori_loop(1, blocks, finish, 0)
        product(blocks - 1, grads[...])
        for i in range(blocks):
            for c in out_copies(i):
                c.wait()


def fall(lengths, index, projs, col, fcs, outs, pre, hidden, cot, gain):
    size, width = cot.shape
    steps = pre.shape[0]
    flat = [w for half in fcs + outs for w in half]
    return pl.pallas_call(
        functools.partial(fall_kernel, len(projs), (len(fcs), len(outs)), col, steps),
        grid=(steps,),
        in_specs=[SMEM, SMEM] + [ANY] * (len(projs) + len(flat) + 3) + [whole((1, width))],
        out_specs=[ANY] * 3,
        out_shape=[
            jax.ShapeDtypeStruct((size, width), BF),
            jax.ShapeDtypeStruct((size, width), F32),
            jax.ShapeDtypeStruct((size, width), BF),
        ],
        scratch_shapes=[
            pltpu.VMEM((width, width), BF),
            pltpu.VMEM((2, width, FF_STEP), BF),
            pltpu.VMEM((2, FF_STEP, width), BF),
            pltpu.VMEM((2, size, FF_STEP), F32),
            pltpu.VMEM((size, width), F32),
            pltpu.VMEM((size, width), BF),
            pltpu.VMEM((size, width), BF),
            pltpu.VMEM((size, width), F32),
            pltpu.VMEM((size, width), F32),
            pltpu.VMEM((size, width), BF),
            pltpu.VMEM((size, width), BF),
            pltpu.VMEM((BLOCK, width), BF),
            pltpu.SemaphoreType.DMA((2,)),
            pltpu.SemaphoreType.DMA((2,)),
            pltpu.SemaphoreType.DMA((2,)),
            pltpu.SemaphoreType.DMA,
        ],
        compiler_params=params(),
        cost_estimate=CHEAP,
        name="fall",
    )(lengths, index, *projs, *flat, pre, hidden, cot, gain)


def backward_kernel(
    len_ref, qx_ref, q_ref, k_ref, v_ref, o_ref, g_ref, upq_ref, upv_ref, narrow_ref, n_ref,
    dq_ref, dk_ref, dv_ref, joint_ref, sums_ref, kx, vx, gx, kt, dqt, total,
):
    size = k_ref.shape[0]
    step = pl.program_id(0)
    ln = lane((size, PAIR))
    first = ln < HD
    bias = jnp.where(row((size, PAIR)) < len_ref[0], 0.0, NEG).astype(BF)
    kp = k_ref[...]
    vp = v_ref[...]
    g = g_ref[...]
    qp = q_ref[...]
    zero = jnp.zeros((size, PAIR), BF)
    one = jnp.ones((size, PAIR), BF)
    prod = g.astype(F32) * o_ref[...].astype(F32)
    for h in range(2):
        other = HD * (1 - h)
        mine = first if h == 0 else ~first
        extra = (ln > other) & (ln <= other + 3)
        kx[h] = jnp.where(mine, kp, jnp.where(ln == other, bias, jnp.where(extra, one, zero)))
        vx[h] = jnp.where(mine, vp, jnp.where(extra, one, zero))
        dots = jnp.sum(jnp.where(mine, prod, 0.0), axis=-1, keepdims=True)
        a, b, c = split3(jnp.broadcast_to(-dots, (size, PAIR)))
        gx[h] = jnp.where(
            mine,
            g,
            jnp.where(
                ln == other + 1,
                a,
                jnp.where(ln == other + 2, b, jnp.where(ln == other + 3, c, zero)),
            ),
        )
    kt[...] = kp.T

    def products(b, h):
        st = dot(kx[h, b : b + BLOCK, :], qx_ref[h * PAIR : (h + 1) * PAIR, b:])
        return st, dot_nt(vx[h, b : b + BLOCK, :], gx[h, b:, :])

    held = {}

    def finish(b, h, st, dp):
        p = jnp.exp(causal_below(st))
        ds = (p * dp).astype(BF)
        mine = slice(h * HD, (h + 1) * HD)
        c = dot(kt[mine, b : b + BLOCK], ds)
        if b == 0:
            dqt[mine, :] = c
        else:
            dqt[mine, b:] += c
        held[h] = (dot(p.astype(BF), g[b:]), dot(ds, qp[b:]))
        if h == 1:
            f = lane((BLOCK, PAIR)) < HD
            dv_ref[b : b + BLOCK, :] = jnp.where(f, held[0][0], held[1][0]).astype(BF)
            dk_ref[b : b + BLOCK, :] = jnp.where(f, held[0][1], held[1][1]).astype(BF)

    tasks = [(b, h) for b in range(0, size, BLOCK) for h in range(2)]
    later = products(*tasks[0])
    for j, t in enumerate(tasks):
        now = later
        if j + 1 < len(tasks):
            later = products(*tasks[j + 1])
        finish(*t, *now)
    dq = (dqt[...] * (1.0 / HD**0.5)).T.astype(BF)
    dq_ref[...] = dq
    dv = dv_ref[...]
    narrow = narrow_ref[...]
    both = jnp.concatenate([dq, dv], axis=1)
    part = dot_nt(jnp.concatenate([upq_ref[...], upv_ref[...]], axis=1), both)
    ups = SCALE * dot(narrow, both)[:8]
    gq, gv = ups[:, :PAIR], ups[:, PAIR:]
    cols = pl.ds(pl.multiple_of(step * PAIR, PAIR), PAIR)
    sums_ref[8:16, cols] = jnp.where(row((8, PAIR)) < 4, gq, gv)

    @pl.when(step == 0)
    def _():
        total[...] = part

    @pl.when(step > 0)
    def _():
        total[...] += part

    @pl.when(step == pl.num_programs(0) - 1)
    def _():
        joint = (SCALE * total[...]).astype(BF)
        joint_ref[...] = joint
        sums_ref[0:8, :] = dot(joint, n_ref[...])[:8]


def attention_backward(lengths, qx, q, k, v, o, ga, upq, upv, narrow, n):
    size, width = k.shape
    pair = pl.BlockSpec((size, PAIR), lambda p: (0, p))
    up = pl.BlockSpec((PAD, PAIR), lambda p: (0, p))
    return pl.pallas_call(
        backward_kernel,
        grid=(width // PAIR,),
        in_specs=[SMEM, pl.BlockSpec((2 * PAIR, size), lambda p: (p, 0))]
        + [pair] * 5
        + [up, up, whole((PAD, size)), whole((size, width))],
        out_specs=[pair] * 3 + [whole((PAD, size)), whole((16, width))],
        out_shape=[jax.ShapeDtypeStruct((size, width), BF)] * 3
        + [jax.ShapeDtypeStruct((PAD, size), BF), jax.ShapeDtypeStruct((16, width), F32)],
        scratch_shapes=[pltpu.VMEM((2, size, PAIR), BF)] * 3
        + [
            pltpu.VMEM((PAIR, size), BF),
            pltpu.VMEM((PAIR, size), F32),
            pltpu.VMEM((PAD, size), F32),
        ],
        compiler_params=params(),
        cost_estimate=CHEAP,
        name="attention_backward",
    )(lengths, qx, q, k, v, o, ga, upq, upv, narrow, n)


def token_kernel(counts, quads, index_ref, *refs):
    shards = []
    for count in counts:
        shards.append(refs[:count])
        refs = refs[count:]
    (dq_ref, dk_ref, dv_ref, joint_ref, down_ref, gh_ref, x_ref, gain_ref, o_ref,
     wbuf, made, sem) = refs
    step = pl.program_id(0)
    last = pl.num_programs(0) - 1
    pieces = [(j, q) for j in range(len(counts)) for q in range(quads[j])]

    def copies(s):
        j, q = pieces[s]
        return qkv_copies(index_ref, shards[j], wbuf.at[s], sem.at[s], q)

    def product(first):
        total = dot_tn(joint_ref[...], down_ref[...])
        for s in range(len(pieces)):
            if first:
                for c in copies(s):
                    c.wait()
            cols = slice(s * QUAD, (s + 1) * QUAD)
            g = jnp.concatenate([ref[:, cols] for ref in (dq_ref, dk_ref, dv_ref)], axis=1)
            total = total + dot_nt(g, wbuf[s])
        return total

    def finish(total):
        xhat, inv = norm_stats(x_ref[...].astype(F32))
        o_ref[...] = (gh_ref[...] + norm_back(xhat, inv, gain_ref[...] * total)).astype(BF)

    @pl.when(step == 0)
    def _():
        for s in range(len(pieces)):
            for c in copies(s):
                c.start()
        made[...] = product(True)

    @pl.when((step > 0) & (step < last))
    def _():
        held = made[...]
        total = product(False)
        finish(held)
        made[...] = total

    @pl.when(step == last)
    def _():
        finish(made[...])


def token_gradient(index, shards, quads, dq, dk, dv, joint, down, gh, x, gain):
    size, width = x.shape
    flat = [s for part in shards for s in part]
    blocks = size // BLOCK
    ahead = pl.BlockSpec((BLOCK, width), lambda i: (jnp.minimum(i, blocks - 1), 0))
    behind = pl.BlockSpec((BLOCK, width), lambda i: (jnp.maximum(i - 1, 0), 0))
    narrow = pl.BlockSpec((PAD, BLOCK), lambda i: (0, jnp.minimum(i, blocks - 1)))
    return pl.pallas_call(
        functools.partial(token_kernel, [len(p) for p in shards], quads),
        grid=(blocks + 1,),
        in_specs=[SMEM]
        + [ANY] * len(flat)
        + [ahead] * 3
        + [narrow, whole((PAD, width)), behind, behind, whole((1, width))],
        out_specs=behind,
        out_shape=jax.ShapeDtypeStruct((size, width), BF),
        scratch_shapes=[
            pltpu.VMEM((sum(quads), width, 3 * QUAD), BF),
            pltpu.VMEM((BLOCK, width), F32),
            pltpu.SemaphoreType.DMA((sum(quads),)),
        ],
        compiler_params=params(),
        cost_estimate=CHEAP,
        name="token_gradient",
    )(index, *flat, dq, dk, dv, joint, down, gh, x, gain)


BOTH = ("dp", "fsdp")


def swap(value, fn, total):
    return lax.ppermute(value, BOTH, [(i, fn(i)) for i in range(total)])


def after(value, *others):
    return lax.optimization_barrier((value,) + others)[0]


class Cube:
    def __init__(self, total, fsdp):
        self.total, self.fsdp = total, fsdp

    def even(self, i):
        return (i // self.fsdp) % 2 == 0

    def sibling(self, value):
        return swap(value, lambda i: i ^ 1, self.total)

    def first(self, value, turned=False):
        return swap(value, lambda i: i ^ (2 if self.even(i) != turned else 4), self.total)

    def second(self, value, turned=False):
        b = swap(value, lambda i: i ^ (4 if self.even(i) != turned else 2), self.total)
        c = swap(value, lambda i: i ^ self.fsdp, self.total)
        return b, c

    def all(self, own, a, b, c, turned=False):
        found = []
        for pair in (own, c, b, a) if turned else (own, a, b, c):
            found += pair
        return found

    def pair(self, value):
        return [value, self.sibling(value)]

    def index(self):
        here = lax.axis_index("fsdp").astype(jnp.int32)
        odd = lax.axis_index("dp").astype(jnp.int32) % 2
        a, c = 2 + 2 * odd, 4 - 2 * odd
        return jnp.stack([here ^ (m ^ s) for m in (0, a, 6, c) for s in (0, 1)])


def sum_rounds(total):
    bits = [1 << i for i in range(1, total.bit_length() - 1)]
    return [[1]] + [bits[i : i + 2] for i in range(0, len(bits), 2)]


def sum_round(value, bits, total):
    if len(bits) == 1:
        return value + swap(value, lambda i: i ^ bits[0], total)
    low, high = bits
    a = swap(value, lambda i: i ^ low, total)
    b = swap(value, lambda i: i ^ high, total)
    c = swap(value, lambda i: i ^ (low | high), total)
    return (value + a) + (b + c)


def local(
    sizes, tokens, lengths, cotangent, gain_one, shift_one, gain_two, shift_two,
    w_qkv, w_proj, w_fc, w_out,
    query_down_factor, query_up_factor, value_down_factor, value_up_factor,
):
    _, size, width = tokens.shape
    dp, fsdp = sizes
    total = dp * fsdp
    x = tokens.reshape(size, width)
    cot = cotangent.reshape(size, width)
    quads = width // QUAD
    half = quads // 2
    w0, w1 = repack(w_qkv, w_proj, half)
    small = (
        x, gain_one[None], shift_one[None],
        query_down_factor.T, value_down_factor.T, query_up_factor, value_up_factor,
    )
    low = tuple(range(half))
    col = 3 * (quads - half) * QUAD
    if fsdp == 8 and dp % 2 == 0:
        cube = Cube(total, fsdp)
        index = cube.index()
        a0, a1, af, ao = [cube.first(w) for w in (w0, w1, w_fc, w_out)]
        own0, own1, ownf, owno = [cube.pair(w) for w in (w0, w1, w_fc, w_out)]
        n, narrow, down, upq, upv = norm_one(*small)
        attend = functools.partial(
            attention_forward, lengths, index, narrow=narrow, upq=upq, upv=upv
        )
        a0 = after(a0, n)
        b0, c0 = cube.second(a0)
        first = cube.all(own0, *map(cube.pair, (a0, b0, c0)))
        b1, c1 = cube.second(a1)
        n1 = after(n, a1)
        kept = attend(first, n=n1, quads=low[:1], here=0, kept=[])
        kept = attend(first, n=n1, quads=low[1:], here=1, kept=kept)
        a1 = after(a1, kept[0])
        b1, c1 = after(b1, kept[0]), after(c1, kept[0])
        second = cube.all(own1, *map(cube.pair, (a1, b1, c1)))
        af = after(af, kept[0])
        bf, cf = cube.second(af)
        n2 = after(n, af)
        pair_af = cube.pair(af)
        kept = attend(second, n=n2, quads=low, here=half, kept=kept)
        bf, cf = after(bf, kept[0]), after(cf, kept[0])
        fcs = [cube.all(ownf, pair_af, *map(cube.pair, (bf, cf)))]
        ao = after(ao, kept[0])
        bo, co = cube.second(ao)
        o, qx, q, k, v = kept
        o_late = after(o, ao)
        pair_ao = cube.pair(ao)
        pre, hidden = rise(index, second, col, fcs, o_late, x, gain_two[None], shift_two[None])
        bo, co = after(bo, hidden), after(co, hidden)
        outs = [cube.all(owno, pair_ao, *map(cube.pair, (bo, co)))]
    else:
        index = jnp.zeros((1,), jnp.int32)
        first, second, fcs, outs = [
            [lax.all_gather(w, "fsdp", axis=0, tiled=True)] for w in (w0, w1, w_fc, w_out)
        ]
        fcs, outs = [fcs], [outs]
        n, narrow, down, upq, upv = norm_one(*small)
        kept = attention_forward(lengths, index, first, n, narrow, upq, upv, low, 0, [])
        kept = attention_forward(lengths, index, second, n, narrow, upq, upv, low, half, kept)
        o, qx, q, k, v = kept
        pre, hidden = rise(index, second, col, fcs, o, x, gain_two[None], shift_two[None])
    block_out, gh, ga = fall(
        lengths, index, second, col, fcs, outs, pre, hidden, cot, gain_two[None]
    )
    dq, dk, dv, joint, sums = attention_backward(
        lengths, qx, q, k, v, o, ga, upq, upv, narrow, n
    )
    args = (dq, dk, dv, joint, down, gh, x, gain_one[None])
    shards, quads = [first, second], (half, quads - half)
    if total & (total - 1):
        sums = lax.psum(sums, BOTH)
        grad = token_gradient(index, shards, quads, *args)
    else:
        for bits in sum_rounds(total):
            sums = sum_round(sums, bits, total)
        grad = token_gradient(index, shards, quads, *args)
    return (
        block_out.reshape(tokens.shape),
        grad.reshape(tokens.shape),
        sums[0:4].T,
        sums[8:12],
        sums[4:8].T,
        sums[12:16],
    )


def solution(mesh):
    rows = P(BOTH, None, None)
    frozen = P("fsdp", None)
    return jax.shard_map(
        functools.partial(local, (mesh.shape["dp"], mesh.shape["fsdp"])),
        mesh=mesh,
        in_specs=(rows, P(BOTH), rows, P(), P(), P(), P()) + (frozen,) * 4 + (P(),) * 4,
        out_specs=(rows, rows, P(), P(), P(), P()),
        check_vma=False,
    )
```

```python
import functools

import jax
import jax.numpy as jnp
from jax import lax
from jax.experimental import pallas as pl
from jax.experimental.pallas import tpu as pltpu
from jax.sharding import PartitionSpec as P

BF = jnp.bfloat16
F32 = jnp.float32
HD = 64
PAIR = 2 * HD
PAD = 16
SCALE = 8.0
EPS = 1e-05
NEG = -1e30
BLOCK = 256
FF_STEP = 1024
ROWS = 1024
VMEM_LIMIT = 58 * 2**20
GELU_C = 0.7978845608028654
GELU_A = 0.044715
ANY = pl.BlockSpec(memory_space=pl.ANY)
SMEM = pl.BlockSpec(memory_space=pltpu.SMEM)
CHEAP = pl.CostEstimate(flops=1000, bytes_accessed=1000, transcendentals=0)


def dot(a, b):
    return lax.dot_general(a, b, (((1,), (0,)), ((), ())), preferred_element_type=F32)


def dot_nt(a, b):
    return lax.dot_general(a, b, (((1,), (1,)), ((), ())), preferred_element_type=F32)


def dot_tn(a, b):
    return lax.dot_general(a, b, (((0,), (0,)), ((), ())), preferred_element_type=F32)


def lane(shape):
    return lax.broadcasted_iota(jnp.int32, shape, 1)


def row(shape):
    return lax.broadcasted_iota(jnp.int32, shape, 0)


def split3(x):
    a = x.astype(BF)
    r = x - a.astype(F32)
    b = r.astype(BF)
    c = (r - b.astype(F32)).astype(BF)
    return a, b, c


def whole(shape):
    return pl.BlockSpec(shape, lambda *_: (0,) * len(shape))


def params(**kw):
    return pltpu.CompilerParams(vmem_limit_bytes=VMEM_LIMIT, **kw)


def norm_stats(x):
    mean = jnp.mean(x, axis=-1, keepdims=True)
    center = x - mean
    inv = lax.rsqrt(jnp.mean(center * center, axis=-1, keepdims=True) + EPS)
    return center * inv, inv


def norm_back(xhat, inv, g):
    return inv * (
        g
        - jnp.mean(g, axis=-1, keepdims=True)
        - xhat * jnp.mean(g * xhat, axis=-1, keepdims=True)
    )


def pad_rows(parts, width):
    have = sum(p.shape[0] for p in parts)
    return jnp.concatenate(parts + [jnp.zeros((PAD - have, width), F32)], axis=0).astype(BF)


def norm_one_kernel(
    x_ref, gain_ref, shift_ref, dq_ref, dv_ref, uq_ref, uv_ref,
    n_ref, narrow_ref, down_ref, upq_ref, upv_ref,
):
    width = x_ref.shape[1]
    rank = dq_ref.shape[0]

    @pl.when(pl.program_id(0) == 0)
    def _():
        blank = jnp.zeros((rank, width), F32)
        down_ref[...] = pad_rows([dq_ref[...], dv_ref[...]], width)
        upq_ref[...] = pad_rows([uq_ref[...]], width)
        upv_ref[...] = pad_rows([blank, uv_ref[...]], width)

    xhat, _ = norm_stats(x_ref[...].astype(F32))
    low = (xhat * gain_ref[...] + shift_ref[...]).astype(BF)
    n_ref[...] = low
    narrow_ref[...] = dot_nt(down_ref[...], low).astype(BF)


def norm_one(x, gain, shift, dq, dv, uq, uv):
    length, width = x.shape
    small = whole((1, width))
    adapter = whole(dq.shape)
    padded = whole((PAD, width))
    return pl.pallas_call(
        norm_one_kernel,
        grid=(length // BLOCK,),
        in_specs=[pl.BlockSpec((BLOCK, width), lambda i: (i, 0)), small, small] + [adapter] * 4,
        out_specs=[
            pl.BlockSpec((BLOCK, width), lambda i: (i, 0)),
            pl.BlockSpec((PAD, BLOCK), lambda i: (0, i)),
            padded, padded, padded,
        ],
        out_shape=[
            jax.ShapeDtypeStruct((length, width), BF),
            jax.ShapeDtypeStruct((PAD, length), BF),
        ]
        + [jax.ShapeDtypeStruct((PAD, width), BF)] * 3,
        compiler_params=params(),
        name="norm_one",
    )(x, gain, shift, dq, dv, uq, uv)


def repack_kernel(begin, end, qkv_ref, proj_ref, o_ref):
    width = qkv_ref.shape[1] // 3
    for q in range(begin, end):
        for p in range(3):
            at = (3 * (q - begin) + p) * QUAD
            o_ref[:, at : at + QUAD] = qkv_ref[:, p * width + q * QUAD : p * width + (q + 1) * QUAD]
    if proj_ref is not None:
        o_ref[:, 3 * (end - begin) * QUAD :] = proj_ref[...]


def repack_alone(begin, end, qkv_ref, o_ref):
    repack_kernel(begin, end, qkv_ref, None, o_ref)


def repack(w_qkv, begin, end, *proj):
    rows = w_qkv.shape[0]
    wide = 3 * (end - begin) * QUAD + sum(w.shape[1] for w in proj)
    return pl.pallas_call(
        functools.partial(repack_kernel if proj else repack_alone, begin, end),
        out_shape=jax.ShapeDtypeStruct((rows, wide), BF),
        compiler_params=params(),
        name="repack",
    )(w_qkv, *proj)


QUAD = 2 * PAIR


def causal_below(x):
    size, wide = x.shape
    near = jnp.where(row((size, size)) <= lane((size, size)), x[:, :size], NEG)
    return near if wide == size else jnp.concatenate([near, x[:, size:]], axis=1)


def attend(length, pairs, o_ref, qx_ref, kx, vt, qt, ot):
    size = pairs[0][0].shape[0]
    ln = lane((size, PAIR))
    first = ln < HD
    bias = jnp.where(row((size, PAIR)) < length, 0.0, NEG).astype(BF)
    zero = jnp.zeros((size, PAIR), BF)
    ones = jnp.ones((16, size), BF)
    extra = jnp.where(row((HD, size)) == 0, 1.0, 0.0).astype(BF)

    def prepare(p):
        q, k, v = pairs[p]
        kx[2 * p] = jnp.where(first, k, jnp.where(ln == HD, bias, zero))
        kx[2 * p + 1] = jnp.where(first, jnp.where(ln == 0, bias, zero), k)
        v_t = v.T
        q_t = q.T
        for h in range(2):
            mine = slice(h * HD, (h + 1) * HD)
            vt[2 * p + h, :HD, :] = v_t[mine]
            vt[2 * p + h, HD:, :] = ones
            parts = [q_t[mine], extra] if h == 0 else [extra, q_t[mine]]
            qt[2 * p + h] = jnp.concatenate(parts, axis=0)

    def scores(t):
        return [
            (b, causal_below(dot(kx[t, b : b + BLOCK, :], qt[t, :, b:])))
            for b in range(0, size, BLOCK)
        ]

    def finish(t, parts):
        top = None
        for b, s in parts:
            high = jnp.max(s, axis=0, keepdims=True)
            if b == 0:
                top = high
            else:
                top = jnp.concatenate([top[:, :b], jnp.maximum(top[:, b:], high)], axis=1)
        acc = None
        for b, s in parts:
            p = jnp.exp(s - top[:, b:]).astype(BF)
            a = dot(vt[t, :, b : b + BLOCK], p)
            acc = a if b == 0 else jnp.concatenate([acc[:, :b], acc[:, b:] + a], axis=1)
        total = acc[HD : HD + 1]
        ot[t * HD : (t + 1) * HD, :] = acc[:HD] * (1.0 / total)
        a, b, c = split3(-(top + jnp.log(total)))
        r = row((HD, size))
        more = jnp.where(
            r == 0,
            1.0,
            jnp.where(
                r == 1,
                a.astype(F32),
                jnp.where(r == 2, b.astype(F32), jnp.where(r == 3, c.astype(F32), 0.0)),
            ),
        ).astype(BF)
        at = t * PAIR
        h = t % 2
        qx_ref[at + h * HD : at + (h + 1) * HD, :] = qt[t, h * HD : (h + 1) * HD, :]
        qx_ref[at + (1 - h) * HD : at + (2 - h) * HD, :] = more

    count = 2 * len(pairs)
    prepare(0)
    later = scores(0)
    for t in range(count):
        now = later
        if t + 1 < count:
            if t % 2:
                prepare((t + 1) // 2)
            later = scores(t + 1)
        finish(t, now)
    o_ref[...] = ot[...].T.astype(BF)


def qkv_copies(index_ref, shards, wbuf, sem, quad):
    rows = shards[0].shape[0]
    wide = wbuf.shape[1]
    copies = []
    for i, ref in enumerate(shards):
        at = pl.multiple_of(index_ref[i] * rows, rows)
        src = ref.at[:, quad * wide : (quad + 1) * wide]
        copies.append(pltpu.make_async_copy(src, wbuf.at[pl.ds(at, rows), :], sem))
    return copies


def forward_kernel(count, kept, quads, len_ref, index_ref, *refs):
    shards, refs = refs[:count], refs[count + kept :]
    (n_ref, narrow_ref, upq_ref, upv_ref, o_ref, qx_ref, q_ref, k_ref, v_ref,
     wbuf, kx, vt, qt, ot, sem) = refs
    step = pl.program_id(0)

    def copies(i):
        return qkv_copies(index_ref, shards, wbuf.at[i], sem.at[i], quads[i])

    @pl.when(step == 0)
    def _():
        for i in range(len(quads)):
            for c in copies(i):
                c.start()

    for i in range(len(quads)):

        @pl.when(step == i)
        def _(i=i):
            for c in copies(i):
                c.wait()

    n = n_ref[...]
    narrow = narrow_ref[...]
    w = wbuf.at[step]
    q = dot(n, w[:, :QUAD]) + SCALE * dot_tn(narrow, upq_ref[...])
    k = dot(n, w[:, QUAD : 2 * QUAD])
    v = dot(n, w[:, 2 * QUAD :]) + SCALE * dot_tn(narrow, upv_ref[...])
    q_ref[...] = (q.astype(BF).astype(F32) * (1.0 / HD**0.5)).astype(BF)
    k_ref[...] = k.astype(BF)
    v_ref[...] = v.astype(BF)
    cols = [slice(p * PAIR, (p + 1) * PAIR) for p in range(QUAD // PAIR)]
    pairs = [(q_ref[:, c], k_ref[:, c], v_ref[:, c]) for c in cols]
    attend(len_ref[0], pairs, o_ref, qx_ref, kx, vt, qt, ot)


def attention_forward(lengths, index, shards, n, narrow, upq, upv, quads, here, kept):
    length, width = n.shape
    block = pl.BlockSpec((length, QUAD), lambda s: (0, here + s))
    up = pl.BlockSpec((PAD, QUAD), lambda s: (0, here + s))
    first = 2 + len(shards)
    heads = QUAD // HD
    return pl.pallas_call(
        functools.partial(forward_kernel, len(shards), len(kept), quads),
        grid=(len(quads),),
        in_specs=[SMEM, SMEM]
        + [ANY] * (len(shards) + len(kept))
        + [whole((length, width)), whole((PAD, length)), up, up],
        out_specs=[block, pl.BlockSpec((2 * QUAD, length), lambda s: (here + s, 0))] + [block] * 3,
        out_shape=[
            jax.ShapeDtypeStruct((length, width), BF),
            jax.ShapeDtypeStruct((2 * width, length), BF),
        ]
        + [jax.ShapeDtypeStruct((length, width), BF)] * 3,
        input_output_aliases={first + i: i for i in range(len(kept))},
        scratch_shapes=[
            pltpu.VMEM((len(quads), width, 3 * QUAD), BF),
            pltpu.VMEM((heads, length, PAIR), BF),
            pltpu.VMEM((heads, HD + 16, length), BF),
            pltpu.VMEM((heads, PAIR, length), BF),
            pltpu.VMEM((QUAD, length), F32),
            pltpu.SemaphoreType.DMA((len(quads),)),
        ],
        compiler_params=params(),
        cost_estimate=CHEAP,
        name="attention_forward",
    )(lengths, index, *shards, *kept, n, narrow, upq, upv)


def rows_copies(index_ref, shards, col, wide, wbuf, sem):
    rows = shards[0].shape[0]
    copies = []
    for i, ref in enumerate(shards):
        at = pl.multiple_of(index_ref[i] * rows, rows)
        src = ref.at[:, pl.ds(col, wide)]
        copies.append(pltpu.make_async_copy(src, wbuf.at[pl.ds(at, rows), :], sem))
    return copies


def out_slice(index_ref, outs, step):
    part = outs[0][0].shape[0]
    rows = part * len(outs)
    pieces = []
    if rows >= FF_STEP:
        shard, place = divmod(step, rows // FF_STEP)
        begin = pl.multiple_of(index_ref[shard] * rows + place * FF_STEP, FF_STEP)
        wide = min(part, FF_STEP)
        for at in range(place * FF_STEP, (place + 1) * FF_STEP, wide):
            pieces.append((outs[at // part][shard], at % part, at - place * FF_STEP, wide))
        return begin, pieces
    each = FF_STEP // rows
    begin = index_ref[step * each] * rows // FF_STEP * FF_STEP
    begin = pl.multiple_of(begin, FF_STEP)
    for i in range(step * each, (step + 1) * each):
        to = index_ref[i] * rows - begin
        for h, some in enumerate(outs):
            pieces.append((some[i], 0, pl.multiple_of(to + h * part, part), part))
    return begin, pieces


def gelu_both(v):
    square = v * v
    t = jnp.tanh(v * (GELU_C + (GELU_C * GELU_A) * square))
    half = 0.5 * t + 0.5
    act = v * half
    slope = half + act * (1.0 - half) * (2.0 * GELU_C + (6.0 * GELU_C * GELU_A) * square)
    return act, slope


def split_list(refs, count, halves):
    lists = [refs[h * count : (h + 1) * count] for h in range(halves)]
    return lists, refs[count * halves :]


def blocks_of(size, rows):
    return [pl.ds(i * rows, rows) for i in range(size // rows)]


def rise_kernel(count, halves, col, index_ref, *refs):
    projs, refs = refs[:count], refs[count:]
    fcs, refs = split_list(refs, count, halves)
    (o_ref, x_ref, gain_ref, shift_ref, pre_ref, hidden_ref,
     wproj, fbuf, obuf, xbuf, hidden, n2, psem, fsem, osem, hsem) = refs
    step = pl.program_id(0)
    size, width = xbuf.shape
    steps = halves * fcs[0][0].shape[1] // FF_STEP
    slot = lax.rem(step, 2)
    places = blocks_of(size, BLOCK)

    def fc_copies(s):
        slot = s % 2
        each = steps // halves
        col = s % each * FF_STEP
        return rows_copies(index_ref, fcs[s // each], col, FF_STEP, fbuf.at[slot], fsem.at[slot])

    def row_copies(i):
        at = pl.ds(pl.multiple_of(i * BLOCK, BLOCK), BLOCK)
        return [
            pltpu.make_async_copy(o_ref.at[at, :], obuf.at[at, :], osem.at[i]),
            pltpu.make_async_copy(x_ref.at[at, :], xbuf.at[at, :], osem.at[i]),
        ]

    def hidden_copy(i):
        at = pl.ds(pl.multiple_of(i * BLOCK, BLOCK), BLOCK)
        return pltpu.make_async_copy(hidden.at[at, :], hidden_ref.at[at, :], hsem)

    @pl.when(step == 0)
    def _():
        first = rows_copies(index_ref, projs, col, width, wproj, psem)
        for c in first:
            c.start()
        for i in range(len(places)):
            for c in row_copies(i):
                c.start()
        for c in fc_copies(0):
            c.start()
        for c in first:
            c.wait()

        def begin(i, carry):
            at = pl.ds(pl.multiple_of(i * BLOCK, BLOCK), BLOCK)
            for c in row_copies(i):
                c.wait()
            total = xbuf[at, :].astype(F32) + dot(obuf[at, :], wproj[...])
            hidden[at, :] = total
            hidden_copy(i).start()
            xhat, _ = norm_stats(total)
            n2[at, :] = (xhat * gain_ref[...] + shift_ref[...]).astype(BF)
            return carry

        lax.fori_loop(0, len(places), begin, 0)

    for s in range(1, steps):

        @pl.when(step + 1 == s)
        def _(s=s):
            for c in fc_copies(s):
                c.start()

    for even in range(2):

        @pl.when(slot == even)
        def _(even=even):
            for c in fc_copies(even):
                c.wait()

    def body(i, carry):
        at = pl.ds(pl.multiple_of(i * ROWS, ROWS), ROWS)
        pre_ref[at, :] = dot(n2[at, :], fbuf[slot])
        return carry

    lax.fori_loop(0, size // ROWS, body, 0)

    @pl.when(step == steps - 1)
    def _():
        for i in range(len(places)):
            hidden_copy(i).wait()


def rise(index, projs, col, fcs, o, x, gain, shift):
    size, width = x.shape
    units = sum(half[0].shape[1] for half in fcs)
    small = whole((1, width))
    flat = [f for half in fcs for f in half]
    return pl.pallas_call(
        functools.partial(rise_kernel, len(projs), len(fcs), col),
        grid=(units // FF_STEP,),
        in_specs=[SMEM] + [ANY] * (len(projs) + len(flat) + 2) + [small, small],
        out_specs=[pl.BlockSpec((None, size, FF_STEP), lambda s: (s, 0, 0)), ANY],
        out_shape=[
            jax.ShapeDtypeStruct((units // FF_STEP, size, FF_STEP), F32),
            jax.ShapeDtypeStruct((size, width), F32),
        ],
        scratch_shapes=[
            pltpu.VMEM((width, width), BF),
            pltpu.VMEM((2, width, FF_STEP), BF),
            pltpu.VMEM((size, width), BF),
            pltpu.VMEM((size, width), BF),
            pltpu.VMEM((size, width), F32),
            pltpu.VMEM((size, width), BF),
            pltpu.SemaphoreType.DMA,
            pltpu.SemaphoreType.DMA((2,)),
            pltpu.SemaphoreType.DMA((size // BLOCK,)),
            pltpu.SemaphoreType.DMA,
        ],
        compiler_params=params(),
        cost_estimate=CHEAP,
        name="rise",
    )(index, *projs, *flat, o, x, gain, shift)


def fall_kernel(count, halves, col, steps, len_ref, index_ref, *refs):
    projs, refs = refs[:count], refs[count:]
    fcs, refs = split_list(refs, count, halves[0])
    outs, refs = split_list(refs, count, halves[1])
    (pre_ref, hidden_ref, cot_ref, gain_ref, block_ref, gh_ref, ga_ref,
     wproj, fbuf, obuf, pbuf, hidden, cbuf, low, acc, back, block, gatt, grads, sem, fsem, lsem, wsem) = refs
    step = pl.program_id(0)
    size, width = low.shape
    slot = lax.rem(step, 2)

    def copies(s):
        begin, pieces = out_slice(index_ref, outs, s)
        slot = s % 2
        found = []
        for ref, at, to, rows in pieces:
            found.append(
                pltpu.make_async_copy(
                    ref.at[at : at + rows, :], obuf.at[slot, pl.ds(to, rows), :], sem.at[slot]
                )
            )
        src = pre_ref.at[begin // FF_STEP]
        found.append(pltpu.make_async_copy(src, pbuf.at[slot], sem.at[slot]))
        return found

    def fc_copies(s):
        begin, _ = out_slice(index_ref, outs, s)
        slot = s % 2
        wide = fcs[0][0].shape[1]
        which = begin // wide
        at = pl.multiple_of(begin - which * wide, FF_STEP)
        return which, [
            rows_copies(index_ref, some, at, FF_STEP, fbuf.at[slot], fsem.at[slot]) for some in fcs
        ]

    def start(s):
        for c in copies(s):
            c.start()
        which, found = fc_copies(s)
        for h, some in enumerate(found):

            @pl.when(which == h)
            def _(some=some):
                for c in some:
                    c.start()

    late = [pltpu.make_async_copy(hidden_ref, hidden, lsem.at[1])]
    late += rows_copies(index_ref, projs, col, width, wproj, lsem.at[1])
    first = pltpu.make_async_copy(cot_ref, cbuf, lsem.at[0])

    @pl.when(step == 0)
    def _():
        first.start()
        start(0)
        start(1)
        for c in late:
            c.start()
        first.wait()
        for i, at in enumerate(blocks_of(size, BLOCK)):
            keep = row((BLOCK, 1)) + i * BLOCK < len_ref[0]
            low[at, :] = jnp.where(keep, cbuf[at, :].astype(F32), 0.0).astype(BF)
            acc[at, :] = jnp.zeros((BLOCK, width), F32)
            back[at, :] = jnp.zeros((BLOCK, width), F32)

    for s in range(2, steps):

        @pl.when(step + 1 == s)
        def _(s=s):
            start(s)

    for even in range(2):

        @pl.when(slot == even)
        def _(even=even):
            for c in copies(even) + fc_copies(even)[1][0]:
                c.wait()

    def body(i, carry):
        at = pl.ds(pl.multiple_of(i * ROWS, ROWS), ROWS)
        down = dot_nt(low[at, :], obuf[slot])
        act, slope = gelu_both(pbuf[slot, at, :])
        acc[at, :] += dot(act.astype(BF), obuf[slot])
        back[at, :] += dot_nt((down * slope).astype(BF), fbuf[slot])
        return carry

    lax.fori_loop(0, size // ROWS, body, 0)

    @pl.when(step == steps - 1)
    def _():
        for c in late:
            c.wait()
        def out_copies(i):
            at = pl.ds(pl.multiple_of(i * BLOCK, BLOCK), BLOCK)
            return [
                pltpu.make_async_copy(block.at[at, :], block_ref.at[at, :], wsem),
                pltpu.make_async_copy(hidden.at[at, :], gh_ref.at[at, :], wsem),
                pltpu.make_async_copy(gatt.at[at, :], ga_ref.at[at, :], wsem),
            ]

        def grad(i):
            at = pl.ds(pl.multiple_of(i * BLOCK, BLOCK), BLOCK)
            h = hidden[at, :]
            keep = row((BLOCK, 1)) + i * BLOCK < len_ref[0]
            block[at, :] = jnp.where(keep, h + acc[at, :], 0.0).astype(BF)
            xhat, inv = norm_stats(h)
            gh = low[at, :].astype(F32) + norm_back(xhat, inv, gain_ref[...] * back[at, :])
            hidden[at, :] = gh
            return gh.astype(BF)

        def product(i, gh):
            at = pl.ds(pl.multiple_of(i * BLOCK, BLOCK), BLOCK)
            gatt[at, :] = dot_nt(gh, wproj[...]).astype(BF)
            for c in out_copies(i):
                c.start()

        def finish(i, carry):
            last = grads[...]
            at = pl.ds(pl.multiple_of((i - 1) * BLOCK, BLOCK), BLOCK)
            made = dot_nt(last, wproj[...]).astype(BF)
            grads[...] = grad(i)
            gatt[at, :] = made
            for c in out_copies(i - 1):
                c.start()
            return carry

        blocks = size // BLOCK
        grads[...] = grad(0)
        lax.fori_loop(1, blocks, finish, 0)
        product(blocks - 1, grads[...])
        for i in range(blocks):
            for c in out_copies(i):
                c.wait()


def fall(lengths, index, projs, col, fcs, outs, pre, hidden, cot, gain):
    size, width = cot.shape
    steps = pre.shape[0]
    flat = [w for half in fcs + outs for w in half]
    return pl.pallas_call(
        functools.partial(fall_kernel, len(projs), (len(fcs), len(outs)), col, steps),
        grid=(steps,),
        in_specs=[SMEM, SMEM] + [ANY] * (len(projs) + len(flat) + 3) + [whole((1, width))],
        out_specs=[ANY] * 3,
        out_shape=[
            jax.ShapeDtypeStruct((size, width), BF),
            jax.ShapeDtypeStruct((size, width), F32),
            jax.ShapeDtypeStruct((size, width), BF),
        ],
        scratch_shapes=[
            pltpu.VMEM((width, width), BF),
            pltpu.VMEM((2, width, FF_STEP), BF),
            pltpu.VMEM((2, FF_STEP, width), BF),
            pltpu.VMEM((2, size, FF_STEP), F32),
            pltpu.VMEM((size, width), F32),
            pltpu.VMEM((size, width), BF),
            pltpu.VMEM((size, width), BF),
            pltpu.VMEM((size, width), F32),
            pltpu.VMEM((size, width), F32),
            pltpu.VMEM((size, width), BF),
            pltpu.VMEM((size, width), BF),
            pltpu.VMEM((BLOCK, width), BF),
            pltpu.SemaphoreType.DMA((2,)),
            pltpu.SemaphoreType.DMA((2,)),
            pltpu.SemaphoreType.DMA((2,)),
            pltpu.SemaphoreType.DMA,
        ],
        compiler_params=params(),
        cost_estimate=CHEAP,
        name="fall",
    )(lengths, index, *projs, *flat, pre, hidden, cot, gain)


def backward_kernel(
    len_ref, qx_ref, q_ref, k_ref, v_ref, o_ref, g_ref, upq_ref, upv_ref, narrow_ref, n_ref,
    dq_ref, dk_ref, dv_ref, joint_ref, sums_ref, kx, vx, gx, kt, dqt, total,
):
    size = k_ref.shape[0]
    step = pl.program_id(0)
    ln = lane((size, PAIR))
    first = ln < HD
    bias = jnp.where(row((size, PAIR)) < len_ref[0], 0.0, NEG).astype(BF)
    kp = k_ref[...]
    vp = v_ref[...]
    g = g_ref[...]
    qp = q_ref[...]
    zero = jnp.zeros((size, PAIR), BF)
    one = jnp.ones((size, PAIR), BF)
    prod = g.astype(F32) * o_ref[...].astype(F32)
    for h in range(2):
        other = HD * (1 - h)
        mine = first if h == 0 else ~first
        extra = (ln > other) & (ln <= other + 3)
        kx[h] = jnp.where(mine, kp, jnp.where(ln == other, bias, jnp.where(extra, one, zero)))
        vx[h] = jnp.where(mine, vp, jnp.where(extra, one, zero))
        dots = jnp.sum(jnp.where(mine, prod, 0.0), axis=-1, keepdims=True)
        a, b, c = split3(jnp.broadcast_to(-dots, (size, PAIR)))
        gx[h] = jnp.where(
            mine,
            g,
            jnp.where(
                ln == other + 1,
                a,
                jnp.where(ln == other + 2, b, jnp.where(ln == other + 3, c, zero)),
            ),
        )
    kt[...] = kp.T

    def products(b, h):
        st = dot(kx[h, b : b + BLOCK, :], qx_ref[h * PAIR : (h + 1) * PAIR, b:])
        return st, dot_nt(vx[h, b : b + BLOCK, :], gx[h, b:, :])

    held = {}

    def finish(b, h, st, dp):
        p = jnp.exp(causal_below(st))
        ds = (p * dp).astype(BF)
        mine = slice(h * HD, (h + 1) * HD)
        c = dot(kt[mine, b : b + BLOCK], ds)
        if b == 0:
            dqt[mine, :] = c
        else:
            dqt[mine, b:] += c
        held[h] = (dot(p.astype(BF), g[b:]), dot(ds, qp[b:]))
        if h == 1:
            f = lane((BLOCK, PAIR)) < HD
            dv_ref[b : b + BLOCK, :] = jnp.where(f, held[0][0], held[1][0]).astype(BF)
            dk_ref[b : b + BLOCK, :] = jnp.where(f, held[0][1], held[1][1]).astype(BF)

    tasks = [(b, h) for b in range(0, size, BLOCK) for h in range(2)]
    later = products(*tasks[0])
    for j, t in enumerate(tasks):
        now = later
        if j + 1 < len(tasks):
            later = products(*tasks[j + 1])
        finish(*t, *now)
    dq = (dqt[...] * (1.0 / HD**0.5)).T.astype(BF)
    dq_ref[...] = dq
    dv = dv_ref[...]
    narrow = narrow_ref[...]
    both = jnp.concatenate([dq, dv], axis=1)
    part = dot_nt(jnp.concatenate([upq_ref[...], upv_ref[...]], axis=1), both)
    ups = SCALE * dot(narrow, both)[:8]
    gq, gv = ups[:, :PAIR], ups[:, PAIR:]
    cols = pl.ds(pl.multiple_of(step * PAIR, PAIR), PAIR)
    sums_ref[8:16, cols] = jnp.where(row((8, PAIR)) < 4, gq, gv)

    @pl.when(step == 0)
    def _():
        total[...] = part

    @pl.when(step > 0)
    def _():
        total[...] += part

    @pl.when(step == pl.num_programs(0) - 1)
    def _():
        joint = (SCALE * total[...]).astype(BF)
        joint_ref[...] = joint
        sums_ref[0:8, :] = dot(joint, n_ref[...])[:8]


def attention_backward(lengths, qx, q, k, v, o, ga, upq, upv, narrow, n):
    size, width = k.shape
    pair = pl.BlockSpec((size, PAIR), lambda p: (0, p))
    up = pl.BlockSpec((PAD, PAIR), lambda p: (0, p))
    return pl.pallas_call(
        backward_kernel,
        grid=(width // PAIR,),
        in_specs=[SMEM, pl.BlockSpec((2 * PAIR, size), lambda p: (p, 0))]
        + [pair] * 5
        + [up, up, whole((PAD, size)), whole((size, width))],
        out_specs=[pair] * 3 + [whole((PAD, size)), whole((16, width))],
        out_shape=[jax.ShapeDtypeStruct((size, width), BF)] * 3
        + [jax.ShapeDtypeStruct((PAD, size), BF), jax.ShapeDtypeStruct((16, width), F32)],
        scratch_shapes=[pltpu.VMEM((2, size, PAIR), BF)] * 3
        + [
            pltpu.VMEM((PAIR, size), BF),
            pltpu.VMEM((PAIR, size), F32),
            pltpu.VMEM((PAD, size), F32),
        ],
        compiler_params=params(),
        cost_estimate=CHEAP,
        name="attention_backward",
    )(lengths, qx, q, k, v, o, ga, upq, upv, narrow, n)


def token_kernel(counts, quads, index_ref, *refs):
    shards = []
    for count in counts:
        shards.append(refs[:count])
        refs = refs[count:]
    (dq_ref, dk_ref, dv_ref, joint_ref, down_ref, gh_ref, x_ref, gain_ref, o_ref,
     wbuf, made, sem) = refs
    step = pl.program_id(0)
    last = pl.num_programs(0) - 1
    pieces = [(j, q) for j in range(len(counts)) for q in range(quads[j])]

    def copies(s):
        j, q = pieces[s]
        return qkv_copies(index_ref, shards[j], wbuf.at[s], sem.at[s], q)

    def product(first):
        total = dot_tn(joint_ref[...], down_ref[...])
        for s in range(len(pieces)):
            if first:
                for c in copies(s):
                    c.wait()
            cols = slice(s * QUAD, (s + 1) * QUAD)
            g = jnp.concatenate([ref[:, cols] for ref in (dq_ref, dk_ref, dv_ref)], axis=1)
            total = total + dot_nt(g, wbuf[s])
        return total

    def finish(total):
        xhat, inv = norm_stats(x_ref[...].astype(F32))
        o_ref[...] = (gh_ref[...] + norm_back(xhat, inv, gain_ref[...] * total)).astype(BF)

    @pl.when(step == 0)
    def _():
        for s in range(len(pieces)):
            for c in copies(s):
                c.start()
        made[...] = product(True)

    @pl.when((step > 0) & (step < last))
    def _():
        held = made[...]
        total = product(False)
        finish(held)
        made[...] = total

    @pl.when(step == last)
    def _():
        finish(made[...])


def token_gradient(index, shards, quads, dq, dk, dv, joint, down, gh, x, gain):
    size, width = x.shape
    flat = [s for part in shards for s in part]
    blocks = size // BLOCK
    ahead = pl.BlockSpec((BLOCK, width), lambda i: (jnp.minimum(i, blocks - 1), 0))
    behind = pl.BlockSpec((BLOCK, width), lambda i: (jnp.maximum(i - 1, 0), 0))
    narrow = pl.BlockSpec((PAD, BLOCK), lambda i: (0, jnp.minimum(i, blocks - 1)))
    return pl.pallas_call(
        functools.partial(token_kernel, [len(p) for p in shards], quads),
        grid=(blocks + 1,),
        in_specs=[SMEM]
        + [ANY] * len(flat)
        + [ahead] * 3
        + [narrow, whole((PAD, width)), behind, behind, whole((1, width))],
        out_specs=behind,
        out_shape=jax.ShapeDtypeStruct((size, width), BF),
        scratch_shapes=[
            pltpu.VMEM((sum(quads), width, 3 * QUAD), BF),
            pltpu.VMEM((BLOCK, width), F32),
            pltpu.SemaphoreType.DMA((sum(quads),)),
        ],
        compiler_params=params(),
        cost_estimate=CHEAP,
        name="token_gradient",
    )(index, *flat, dq, dk, dv, joint, down, gh, x, gain)


BOTH = ("dp", "fsdp")


def swap(value, fn, total):
    return lax.ppermute(value, BOTH, [(i, fn(i)) for i in range(total)])


def after(value, *others):
    return lax.optimization_barrier((value,) + others)[0]


class Cube:
    def __init__(self, total, fsdp):
        self.total, self.fsdp = total, fsdp

    def even(self, i):
        return (i // self.fsdp) % 2 == 0

    def sibling(self, value):
        return swap(value, lambda i: i ^ 1, self.total)

    def first(self, value, turned=False):
        return swap(value, lambda i: i ^ (2 if self.even(i) != turned else 4), self.total)

    def second(self, value, turned=False):
        b = swap(value, lambda i: i ^ (4 if self.even(i) != turned else 2), self.total)
        c = swap(value, lambda i: i ^ self.fsdp, self.total)
        return b, c

    def all(self, own, a, b, c, turned=False):
        found = []
        for pair in (own, c, b, a) if turned else (own, a, b, c):
            found += pair
        return found

    def pair(self, value):
        return [value, self.sibling(value)]

    def index(self):
        here = lax.axis_index("fsdp").astype(jnp.int32)
        odd = lax.axis_index("dp").astype(jnp.int32) % 2
        a, c = 2 + 2 * odd, 4 - 2 * odd
        return jnp.stack([here ^ (m ^ s) for m in (0, a, 6, c) for s in (0, 1)])


def sum_rounds(total):
    bits = [1 << i for i in range(1, total.bit_length() - 1)]
    return [[1]] + [bits[i : i + 2] for i in range(0, len(bits), 2)]


def sum_round(value, bits, total):
    if len(bits) == 1:
        return value + swap(value, lambda i: i ^ bits[0], total)
    low, high = bits
    a = swap(value, lambda i: i ^ low, total)
    b = swap(value, lambda i: i ^ high, total)
    c = swap(value, lambda i: i ^ (low | high), total)
    return (value + a) + (b + c)


def local(
    sizes, tokens, lengths, cotangent, gain_one, shift_one, gain_two, shift_two,
    w_qkv, w_proj, w_fc, w_out,
    query_down_factor, query_up_factor, value_down_factor, value_up_factor,
):
    _, size, width = tokens.shape
    dp, fsdp = sizes
    total = dp * fsdp
    x = tokens.reshape(size, width)
    cot = cotangent.reshape(size, width)
    quads = width // QUAD
    half = quads // 2
    w0, w1 = repack(w_qkv, 0, half), repack(w_qkv, half, quads, w_proj)
    small = (
        x, gain_one[None], shift_one[None],
        query_down_factor.T, value_down_factor.T, query_up_factor, value_up_factor,
    )
    low = tuple(range(half))
    col = 3 * (quads - half) * QUAD
    if fsdp == 8 and dp % 2 == 0:
        cube = Cube(total, fsdp)
        index = cube.index()
        a0, a1, af, ao = [cube.first(w) for w in (w0, w1, w_fc, w_out)]
        own0, own1, ownf, owno = [cube.pair(w) for w in (w0, w1, w_fc, w_out)]
        n, narrow, down, upq, upv = norm_one(*small)
        attend = functools.partial(
            attention_forward, lengths, index, narrow=narrow, upq=upq, upv=upv
        )
        a0 = after(a0, n)
        b0, c0 = cube.second(a0)
        first = cube.all(own0, *map(cube.pair, (a0, b0, c0)))
        b1, c1 = cube.second(a1)
        n1 = after(n, a1)
        kept = attend(first, n=n1, quads=low[:1], here=0, kept=[])
        kept = attend(first, n=n1, quads=low[1:], here=1, kept=kept)
        a1 = after(a1, kept[0])
        b1, c1 = after(b1, kept[0]), after(c1, kept[0])
        second = cube.all(own1, *map(cube.pair, (a1, b1, c1)))
        af = after(af, kept[0])
        bf, cf = cube.second(af)
        n2 = after(n, af)
        pair_af = cube.pair(af)
        kept = attend(second, n=n2, quads=low, here=half, kept=kept)
        bf, cf = after(bf, kept[0]), after(cf, kept[0])
        fcs = [cube.all(ownf, pair_af, *map(cube.pair, (bf, cf)))]
        ao = after(ao, kept[0])
        bo, co = cube.second(ao)
        o, qx, q, k, v = kept
        o_late = after(o, ao)
        pair_ao = cube.pair(ao)
        pre, hidden = rise(index, second, col, fcs, o_late, x, gain_two[None], shift_two[None])
        bo, co = after(bo, hidden), after(co, hidden)
        outs = [cube.all(owno, pair_ao, *map(cube.pair, (bo, co)))]
    else:
        index = jnp.zeros((1,), jnp.int32)
        first, second, fcs, outs = [
            [lax.all_gather(w, "fsdp", axis=0, tiled=True)] for w in (w0, w1, w_fc, w_out)
        ]
        fcs, outs = [fcs], [outs]
        n, narrow, down, upq, upv = norm_one(*small)
        kept = attention_forward(lengths, index, first, n, narrow, upq, upv, low, 0, [])
        kept = attention_forward(lengths, index, second, n, narrow, upq, upv, low, half, kept)
        o, qx, q, k, v = kept
        pre, hidden = rise(index, second, col, fcs, o, x, gain_two[None], shift_two[None])
    block_out, gh, ga = fall(
        lengths, index, second, col, fcs, outs, pre, hidden, cot, gain_two[None]
    )
    dq, dk, dv, joint, sums = attention_backward(
        lengths, qx, q, k, v, o, ga, upq, upv, narrow, n
    )
    args = (dq, dk, dv, joint, down, gh, x, gain_one[None])
    shards, quads = [first, second], (half, quads - half)
    if total & (total - 1):
        sums = lax.psum(sums, BOTH)
        grad = token_gradient(index, shards, quads, *args)
    else:
        for bits in sum_rounds(total):
            sums = sum_round(sums, bits, total)
        grad = token_gradient(index, shards, quads, *args)
    return (
        block_out.reshape(tokens.shape),
        grad.reshape(tokens.shape),
        sums[0:4].T,
        sums[8:12],
        sums[4:8].T,
        sums[12:16],
    )


def solution(mesh):
    rows = P(BOTH, None, None)
    frozen = P("fsdp", None)
    return jax.shard_map(
        functools.partial(local, (mesh.shape["dp"], mesh.shape["fsdp"])),
        mesh=mesh,
        in_specs=(rows, P(BOTH), rows, P(), P(), P(), P()) + (frozen,) * 4 + (P(),) * 4,
        out_specs=(rows, rows, P(), P(), P(), P()),
        check_vma=False,
    )
```
